32 devices in a mesh: fsdp: 2 (over x), ctx: 4 (over y, core), tp: 4 (over z).
Axes of the slice: x: 2, y: 2, z: 4, core: 2. Of those that a mesh axis runs over, the one named last changes fastest.
Arguments:
- q_in: bfloat16 [2, 1024, 4096], P('fsdp', 'ctx', 'tp'), may hold values from -6 to 6
- k_in: bfloat16 [2, 1024, 4096], P('fsdp', 'ctx', 'tp'), may hold values from -6 to 6
- v_in: bfloat16 [2, 1024, 4096], P('fsdp', 'ctx', 'tp'), may hold values from -6 to 6
- grad_out: bfloat16 [2, 1024, 4096], P('fsdp', 'ctx', 'tp'), may hold values from -6 to 6
- genome_ids: int32 [2, 1024], P('fsdp', 'ctx'), may hold values from 0 to 7, never falling along the last dimension, each value on 1 to 256 neighbouring positions
- long_filter: bfloat16 [256, 128], P('tp', 'fsdp'), may hold values from -0.5 to 0.5
- short_filter: float32 [3, 7, 4096], P(None, None, 'tp'), may hold values from -2 to 2
Outputs:
- grad_q: bfloat16 [2, 1024, 4096], P('fsdp', 'ctx', 'tp')
- grad_k: bfloat16 [2, 1024, 4096], P('fsdp', 'ctx', 'tp')
- grad_v: bfloat16 [2, 1024, 4096], P('fsdp', 'ctx', 'tp')
- grad_long: float32 [256, 128], P('tp', 'fsdp')
- grad_short: float32 [3, 7, 4096], P(None, None, 'tp')
The draws below stay inside these ranges and needn't reach their ends.
Inputs may be any that keep to these rules, and one draw needn't show every extreme that they name: `genome_ids`: along each sequence the genome ids never fall; each genome covers 1 to 256 positions, and one covers exactly that many.
All inputs are finite; a program needn't handle non-finite values.
Results may differ from the reference program's by a relative error of at most 0.005.
Values may be sent and summed in bfloat16 or wider, within the bound.
No kernel may reach another device: no remote copies, remote signals or barrier semaphores. Data moves between devices by JAX's collectives and lax.ppermute only.
A program may use at most 128 MiB of HBM per device.

```python
import math
import jax
import jax.numpy as jnp
import numpy as np
from jax import lax

CH = 4096
GROUP = 16
TAPS = 128
SHORT = 7
LEN = 1024
SEQS = 2
GROUPS = 256
GENOMES = 8


def levels(stream_key, extent, shards, least, top_value):
    gain = 1.0
    for dim, parts in shards:
        draws = jax.random.uniform(jax.random.fold_in(jax.random.fold_in(stream_key, 6), dim), (parts,), jnp.float32, least / len(shards), top_value / len(shards))
        gain = gain * jnp.repeat(jnp.exp(draws), extent[dim] // parts).reshape((-1,) + (1,) * (len(extent) - 1 - dim))
    return gain


def length_profile(count, total, most, slope):
    portions = [(1 << 20) // math.isqrt(grade ** slope) + 1 for grade in range(2, count + 1)]
    rest, holding = total - most - (count - 1), [1] * (count - 1)
    while rest > 0:
        candidates = [i for i in range(count - 1) if holding[i] < most]
        mass, budget = sum([portions[i] for i in candidates]), rest
        for i in candidates:
            extra = min(most - holding[i], max(1, budget * portions[i] // mass), rest)
            holding[i] = holding[i] + extra
            rest = rest - extra
    return np.array([most] + holding)


def uneven_parts(rng, number_of, total, most, skew):
    if number_of == 2:
        one = jax.random.randint(rng, (), max(1, total - most), min(most, total - 1) + 1)
        return jnp.stack([one, total - one])
    lengths = jnp.asarray(length_profile(number_of, total, most, skew), jnp.int32)
    pairs = (number_of - 1) // 2
    giver, receiver = lengths[1:1 + 2 * pairs:2], lengths[2:2 + 2 * pairs:2]
    margin = jnp.minimum(giver - 1, most - receiver)
    shifted = jax.random.randint(jax.random.fold_in(rng, 1), (pairs,), 0, 1 << 20) % (margin + 1)
    lengths = lengths.at[1:1 + 2 * pairs:2].set(giver - shifted).at[2:2 + 2 * pairs:2].set(receiver + shifted)
    return lengths[jax.random.permutation(jax.random.fold_in(rng, 2), number_of)]


def bell_draw(rng, shape, deviation, bound, pieces=(), held_as=jnp.bfloat16):
    loudness = levels(rng, shape, pieces, -0.22, 0.18) if pieces else 1.0
    array = jax.random.normal(rng, shape, jnp.float32) * deviation * loudness
    return jnp.minimum(jnp.maximum(array, -bound), bound).astype(held_as)


def setup_inputs(seed: int = 0) -> dict:
    seeds = jax.random.split(jax.random.key(seed), 8)
    q_in = bell_draw(seeds[0], (SEQS, LEN, CH), 1.0, 6.0, ((0, 2), (1, 4), (2, 4)))
    k_in = bell_draw(seeds[1], (SEQS, LEN, CH), 1.0, 6.0, ((0, 2), (1, 4), (2, 4)))
    v_in = bell_draw(seeds[2], (SEQS, LEN, CH), 1.0, 6.0, ((0, 2), (1, 4), (2, 4)))
    grad_out = bell_draw(seeds[3], (SEQS, LEN, CH), 1.0, 6.0, ((0, 2), (1, 4), (2, 4)))
    genome_ids = jax.vmap(lambda own: jnp.searchsorted(jnp.cumsum(uneven_parts(own, GENOMES, LEN, LEN // 4, 1)), jnp.arange(LEN), side="right"))(jax.random.split(seeds[4], SEQS)).reshape((SEQS, LEN)).astype(jnp.int32)
    long_filter = bell_draw(seeds[5], (GROUPS, TAPS), TAPS ** -0.5, 0.5, ((0, 4), (1, 2)))
    short_filter = bell_draw(seeds[6], (3, SHORT, CH), SHORT ** -0.5, 2.0, ((2, 4),), jnp.float32)
    return {"q_in": q_in, "k_in": k_in, "v_in": v_in, "grad_out": grad_out, "genome_ids": genome_ids, "long_filter": long_filter, "short_filter": short_filter}


def toeplitz_band(filters, causal):
    group_count, tap_count = filters.shape
    if causal:
        pattern = jnp.concatenate([jnp.zeros((group_count, 1), filters.dtype), filters[:, ::-1], jnp.zeros((group_count, tap_count), filters.dtype)], axis=1)
    else:
        pattern = jnp.concatenate([filters, jnp.zeros((group_count, tap_count + 1), filters.dtype)], axis=1)
    tiled = jnp.tile(pattern, (1, tap_count))[:, :2 * tap_count * tap_count]
    return tiled.reshape(group_count, tap_count, 2 * tap_count)

def causal_long(signal, row_ids, band, block_count):
    group_count, tap_count = (band.shape[0], band.shape[1])
    channels = signal.shape[1]

    def one_block(index):
        offset = index * tap_count
        window = lax.dynamic_slice_in_dim(signal, offset, 2 * tap_count, 0)
        window_ids = lax.dynamic_slice_in_dim(row_ids, offset, 2 * tap_count, 0)
        same = (window_ids[tap_count:][:, None] == window_ids[None, :]).astype(jnp.float32)
        weights = band.astype(jnp.float32) * same[None]
        grouped = window.reshape(2 * tap_count, group_count, channels // group_count).astype(jnp.float32)
        result = jnp.einsum('gij,jgc->igc', weights, grouped)
        return result.reshape(tap_count, channels)
    blocks = lax.map(one_block, jnp.arange(block_count, dtype=jnp.int32))
    return blocks.reshape(block_count * tap_count, channels)

def anti_long(signal, row_ids, band, block_count):
    group_count, tap_count = (band.shape[0], band.shape[1])
    channels = signal.shape[1]

    def one_block(index):
        offset = index * tap_count
        window = lax.dynamic_slice_in_dim(signal, offset, 2 * tap_count, 0)
        window_ids = lax.dynamic_slice_in_dim(row_ids, offset, 2 * tap_count, 0)
        same = (window_ids[:tap_count][:, None] == window_ids[None, :]).astype(jnp.float32)
        weights = band.astype(jnp.float32) * same[None]
        grouped = window.reshape(2 * tap_count, group_count, channels // group_count).astype(jnp.float32)
        result = jnp.einsum('gij,jgc->igc', weights, grouped)
        return result.reshape(tap_count, channels)
    blocks = lax.map(one_block, jnp.arange(block_count, dtype=jnp.int32))
    return blocks.reshape(block_count * tap_count, channels)

def tap_sums(grads, signal, row_ids, block_count, group_count, tap_count):
    channels = grads.shape[1]

    def one_block(carry, index):
        offset = index * tap_count
        rows_here = lax.dynamic_slice_in_dim(grads, offset, tap_count, 0).reshape(tap_count, group_count, channels // group_count).astype(jnp.float32)
        window = lax.dynamic_slice_in_dim(signal, offset, 2 * tap_count, 0).reshape(2 * tap_count, group_count, channels // group_count).astype(jnp.float32)
        window_ids = lax.dynamic_slice_in_dim(row_ids, offset, 2 * tap_count, 0)
        same = (window_ids[tap_count:][:, None] == window_ids[None, :]).astype(jnp.float32)
        products = jnp.einsum('igc,jgc->gij', rows_here, window) * same[None]
        flipped = products[:, :, ::-1].reshape(group_count, 2 * tap_count * tap_count)
        skewed = flipped[:, tap_count - 1:tap_count - 1 + tap_count * (2 * tap_count - 1)]
        skewed = skewed.reshape(group_count, tap_count, 2 * tap_count - 1)[:, :, :tap_count]
        return (carry + lax.optimization_barrier(jnp.sum(skewed, axis=1)), None)
    start = jnp.zeros((group_count, tap_count), jnp.float32)
    total, unused = lax.scan(one_block, start, jnp.arange(block_count, dtype=jnp.int32))
    return total

def short_causal(source, row_ids, weights, out_rows):
    width = weights.shape[0]
    lead = width - 1
    out_ids = row_ids[lead:lead + out_rows]
    total = jnp.zeros((out_rows, source.shape[1]), jnp.float32)
    for offset in range(width):
        begin = lead - offset
        piece = source[begin:begin + out_rows].astype(jnp.float32)
        same = (out_ids == row_ids[begin:begin + out_rows]).astype(jnp.float32)
        total = total + weights[offset][None, :] * piece * same[:, None]
    return total

def short_anti(grads, row_ids, weights, out_rows):
    width = weights.shape[0]
    out_ids = row_ids[:out_rows]
    total = jnp.zeros((out_rows, grads.shape[1]), jnp.float32)
    for offset in range(width):
        piece = grads[offset:offset + out_rows]
        same = (out_ids == row_ids[offset:offset + out_rows]).astype(jnp.float32)
        total = total + weights[offset][None, :] * piece * same[:, None]
    return total

def short_grad(grads, source, row_ids):
    out_rows = grads.shape[0]
    width = source.shape[0] - out_rows + 1
    lead = width - 1
    out_ids = row_ids[lead:lead + out_rows]
    sums = []
    for offset in range(width):
        begin = lead - offset
        piece = source[begin:begin + out_rows].astype(jnp.float32)
        same = (out_ids == row_ids[begin:begin + out_rows]).astype(jnp.float32)
        sums.append(lax.optimization_barrier(jnp.sum(grads * piece * same[:, None], axis=0)))
    return jnp.stack(sums)

def reference(q_in, k_in, v_in, grad_out, genome_ids, long_filter, short_filter):
    lead = SHORT - 1
    reach = TAPS + lead
    block_count = LEN // TAPS
    forward_band = toeplitz_band(long_filter, True)
    backward_band = toeplitz_band(long_filter, False)

    def one_sequence(items):
        query_rows, key_rows, value_rows, upstream, id_row = items
        ids_float = (id_row + 1).astype(jnp.float32)
        ids_back = jnp.concatenate([jnp.zeros((reach,), jnp.float32), ids_float])
        blank = jnp.zeros((reach, CH), jnp.bfloat16)
        key_ext = jnp.concatenate([blank, key_rows])
        value_ext = jnp.concatenate([blank, value_rows])
        query_ext = jnp.concatenate([blank[:lead], query_rows])
        query_ids = ids_back[reach - lead:]
        long_ids = ids_back[lead:]
        key_conv = short_causal(key_ext, ids_back, short_filter[1], LEN + TAPS)
        value_conv = short_causal(value_ext, ids_back, short_filter[2], LEN + TAPS)
        mixed = (key_conv * value_conv).astype(jnp.bfloat16)
        query_conv = short_causal(query_ext, query_ids, short_filter[0], LEN)
        filtered = causal_long(mixed, long_ids, forward_band, block_count)
        grad_filtered = (upstream.astype(jnp.float32) * query_conv).astype(jnp.bfloat16)
        grad_query = upstream.astype(jnp.float32) * filtered
        ids_front = jnp.concatenate([ids_float, jnp.zeros((TAPS,), jnp.float32)])
        grad_mixed = anti_long(jnp.concatenate([grad_filtered, jnp.zeros((TAPS, CH), jnp.bfloat16)]), ids_front, backward_band, block_count)
        grad_key = grad_mixed * value_conv[TAPS:]
        grad_value = grad_mixed * key_conv[TAPS:]
        short_ids = ids_front[:LEN + lead]
        edge = jnp.zeros((lead, CH), jnp.float32)
        out_q = short_anti(jnp.concatenate([grad_query, edge]), short_ids, short_filter[0], LEN).astype(jnp.bfloat16)
        out_k = short_anti(jnp.concatenate([grad_key, edge]), short_ids, short_filter[1], LEN).astype(jnp.bfloat16)
        out_v = short_anti(jnp.concatenate([grad_value, edge]), short_ids, short_filter[2], LEN).astype(jnp.bfloat16)
        long_part = tap_sums(grad_filtered, mixed, long_ids, block_count, GROUPS, TAPS)
        short_part = jnp.stack([short_grad(grad_query, query_ext, query_ids), short_grad(grad_key, key_ext[reach - lead:], query_ids), short_grad(grad_value, value_ext[reach - lead:], query_ids)])
        return (out_q, out_k, out_v, long_part, short_part)
    results = lax.map(one_sequence, (q_in, k_in, v_in, grad_out, genome_ids))
    grad_long = lax.optimization_barrier(jnp.sum(results[3], axis=0)) / math.sqrt(SEQS * LEN * GROUP)
    grad_short = lax.optimization_barrier(jnp.sum(results[4], axis=0)) / math.sqrt(SEQS * LEN)
    return (results[0], results[1], results[2], grad_long, grad_short)
```

```python
import functools
import math

import jax
import jax.numpy as jnp
from jax import lax
from jax.experimental import pallas as pl
from jax.experimental.pallas import tpu as pltpu
from jax.sharding import PartitionSpec as P

TAPS = 128
SHORT = 7
LANES = 128
LEAD = 16
REACH = TAPS + LEAD
F32 = jnp.float32
BF16 = jnp.bfloat16
NT = (((1,), (1,)), ((), ()))
NN = (((1,), (0,)), ((), ()))


def shifted(block, axis, distance):
    devices = range(lax.axis_size(axis))
    route = [(i - distance, i) for i in devices if i - distance in devices]
    return lax.ppermute(block, axis, route)


def dot(a, b, dims):
    return lax.dot_general(a, b, dims, preferred_element_type=F32)


def mixer_kernel(
    rows,
    long_scale,
    short_scale,
    ids_ref,
    taps_ref,
    w_ref,
    pk_ref,
    pv_ref,
    pq_ref,
    nq_ref,
    ng_ref,
    nk_ref,
    nv_ref,
    q_ref,
    k_ref,
    v_ref,
    g_ref,
    oq_ref,
    ok_ref,
    ov_ref,
    part_ref,
    idc,
    mj,
    ml,
    mn,
    mp,
    flip,
    xk,
    xv,
    xq,
    xg,
    ks,
    vs,
    uf,
    dzf,
    ut,
    utr,
    dzt,
    dzr,
    zt,
    dut,
    dq,
    dk,
    dv,
    gl,
):
    blocks = rows // TAPS
    frame = 2 * TAPS
    width = TAPS // LANES * LANES

    @pl.when(pl.program_id(0) == 0)
    def prepare():
        row = lax.broadcasted_iota(jnp.int32, (TAPS, TAPS), 0)
        col = lax.broadcasted_iota(jnp.int32, (TAPS, TAPS), 1)
        for b in range(blocks + 4):
            line = jnp.broadcast_to(ids_ref[:, TAPS * b : TAPS * (b + 1)], (TAPS, TAPS))
            idc[TAPS * b : TAPS * (b + 1), :] = line.T
        step = 8

        def short_masks(i, carry):
            base = pl.multiple_of(TAPS + step * i, 8)
            here = idc[pl.ds(base, step), :]
            for j in range(1, SHORT):
                mj[j - 1, pl.ds(base, step), :] = (here == idc[pl.ds(base - j, step), :]).astype(F32)
            return carry

        lax.fori_loop(0, (rows + TAPS + REACH) // step, short_masks, 0)

        def same(t_block, s_block, count):
            start = TAPS * (t_block + 2)
            line = ids_ref[:, TAPS * (s_block + 2) : TAPS * (s_block + 3)]
            return (idc[start : start + count, :] == line).astype(F32)

        lower = (row >= col).astype(F32)
        upper = 1.0 - lower
        flip[...] = (row + col == TAPS - 1).astype(BF16)
        for b in range(blocks):
            ml[b] = (same(b, b, TAPS) * lower).astype(BF16)
        for b in range(blocks + 1):
            ml[blocks + b] = (same(b, b - 1, TAPS) * upper).astype(BF16)
        mn[0] = (same(blocks, blocks, 16) * lower[:16]).astype(BF16)
        mn[1] = (same(blocks, blocks, 16) * (row <= col).astype(F32)[:16]).astype(BF16)
        mn[2] = (same(blocks, blocks + 1, 16) * (row > col).astype(F32)[:16]).astype(BF16)
        for b in range(blocks):
            both = same(b, b, TAPS) * lower + same(b, b - 1, TAPS) * upper
            mp[b] = dot(both.astype(BF16), flip[...], NN)
        uf[...] = jnp.zeros_like(uf)
        dzf[...] = jnp.zeros_like(dzf)

    xk[0:REACH] = pk_ref[...].astype(F32)
    xv[0:REACH] = pv_ref[...].astype(F32)
    xk[REACH : REACH + rows] = k_ref[0].astype(F32)
    xv[REACH : REACH + rows] = v_ref[0].astype(F32)
    xk[REACH + rows : REACH + rows + LEAD] = nk_ref[...].astype(F32)
    xv[REACH + rows : REACH + rows + LEAD] = nv_ref[...].astype(F32)
    xq[0:LEAD] = pq_ref[...].astype(F32)
    xq[LEAD : LEAD + rows] = q_ref[0].astype(F32)
    xq[LEAD + rows : LEAD + rows + REACH] = nq_ref[...].astype(F32)
    xg[0:rows] = g_ref[0].astype(F32)
    xg[rows : rows + REACH] = ng_ref[...].astype(F32)

    weights = [[w_ref[i, j : j + 1, :] for j in range(SHORT)] for i in range(3)]
    chunk = 40

    def convolve(i, carry):
        low = pl.multiple_of(chunk * i, 8)
        key = weights[1][0] * xk[pl.ds(low + LEAD, chunk), :]
        value = weights[2][0] * xv[pl.ds(low + LEAD, chunk), :]
        for j in range(1, SHORT):
            mask = mj[j - 1, pl.ds(low + TAPS, chunk), :]
            key += weights[1][j] * (mask * xk[pl.ds(low + LEAD - j, chunk), :])
            value += weights[2][j] * (mask * xv[pl.ds(low + LEAD - j, chunk), :])
        ks[pl.ds(low, chunk), :] = key
        vs[pl.ds(low, chunk), :] = value
        uf[pl.ds(low, chunk), :] = key * value
        query = weights[0][0] * xq[pl.ds(low + LEAD, chunk), :]
        for j in range(1, SHORT):
            mask = mj[j - 1, pl.ds(low + frame, chunk), :]
            query += weights[0][j] * (mask * xq[pl.ds(low + LEAD - j, chunk), :])
        dzf[pl.ds(low, chunk), :] = xg[pl.ds(low, chunk), :] * query
        return carry

    lax.fori_loop(0, (rows + REACH) // chunk, convolve, 0)

    for b in range(blocks + 2):
        here = slice(TAPS * b, TAPS * (b + 1))
        turned = uf[here, :].T.astype(BF16)
        ut[:, here] = turned
        if b <= blocks:
            utr[:, here] = dot(turned, flip[...], NN).astype(BF16)
        dzt[:, here] = dzf[here, :].T.astype(BF16)
        if b < blocks:
            dzr[here, :] = dzf[here, :].astype(BF16)

    lane_group = lax.broadcasted_iota(jnp.int32, (TAPS, LANES), 1) // 16
    row = lax.broadcasted_iota(jnp.int32, (TAPS, TAPS), 0)
    col = lax.broadcasted_iota(jnp.int32, (TAPS, TAPS), 1)
    lower_flipped = row + col >= TAPS - 1

    for g in range(LANES // 16):
        c = slice(16 * g, 16 * g + 16)
        line = jnp.broadcast_to(taps_ref[g : g + 1, 0:TAPS], (TAPS, TAPS))
        band = pltpu.roll(line, 0, 1, stride=1, stride_axis=0).astype(BF16)
        line = jnp.broadcast_to(taps_ref[g : g + 1, TAPS:], (16, TAPS))
        other = pltpu.roll(line, 0, 1, stride=1, stride_axis=0).astype(BF16)
        near = [band * ml[b] for b in range(blocks)]
        far = [band * ml[blocks + b] for b in range(blocks + 1)]
        for b in range(blocks):
            window = slice(TAPS * b, TAPS * (b + 2))
            here = slice(TAPS * b, TAPS * (b + 1))
            zt[c, here] = dot(ut[c, window], jnp.concatenate([far[b], near[b]], axis=1), NT)
            dut[c, here] = dot(dzt[c, window], jnp.concatenate([near[b], far[b + 1]], axis=0), NN)
        window = slice(TAPS * blocks, TAPS * (blocks + 2))
        here = slice(TAPS * blocks, TAPS * blocks + 16)
        edge = jnp.concatenate([far[blocks][:16], band[:16] * mn[0]], axis=1)
        zt[c, here] = dot(ut[c, window], edge, NT)
        edge = jnp.concatenate([other * mn[1], other * mn[2]], axis=1)
        dut[c, here] = dot(dzt[c, window], edge, NT)
        total = None
        for b in range(blocks):
            here = slice(TAPS * b, TAPS * (b + 1))
            mine = jnp.where(lane_group == g, dzr[here, :], jnp.zeros((), BF16))
            pairs = dot(mine, utr[:, TAPS * b : TAPS * (b + 2)], NN)
            term = jnp.where(lower_flipped, pairs[:, TAPS:], pairs[:, :TAPS]) * mp[b]
            total = term if total is None else total + term
        skewed = pltpu.roll(total, 1, 1, stride=1, stride_axis=0)
        gl[g : g + 1, :] = jnp.sum(skewed, axis=0, keepdims=True)

    for b in range(blocks + 1):
        count = TAPS if b < blocks else 16
        here = slice(TAPS * b, TAPS * b + count)
        z = zt[:, TAPS * b : TAPS * (b + 1)].T[:count]
        du = dut[:, TAPS * b : TAPS * (b + 1)].T[:count]
        there = slice(TAPS * (b + 1), TAPS * (b + 1) + count)
        dq[here, :] = xg[here, :] * z
        dk[here, :] = du * vs[there, :]
        dv[here, :] = du * ks[there, :]

    part = 32

    def finish(i, sums):
        low = pl.multiple_of(part * i, part)
        fresh = []
        for grad, source, lead, w, out in (
            (dq, xq, LEAD, weights[0], oq_ref),
            (dk, xk, REACH, weights[1], ok_ref),
            (dv, xv, REACH, weights[2], ov_ref),
        ):
            x = source[pl.ds(low + lead, part), :]
            total = None
            for j in range(SHORT):
                piece = grad[pl.ds(low + j, part), :]
                if j:
                    piece = piece * mj[j - 1, pl.ds(low + frame + j, part), :]
                total = w[j] * piece if total is None else total + w[j] * piece
                fresh.append(jnp.sum((x * piece).reshape(part // 8, 8, LANES), axis=0))
            out[0, pl.ds(low, part), :] = total.astype(BF16)
        return tuple(a + b for a, b in zip(sums, fresh))

    zero = jnp.zeros((8, LANES), F32)
    sums = lax.fori_loop(0, rows // part, finish, (zero,) * (3 * SHORT))
    lines = [jnp.sum(s, axis=0, keepdims=True) * short_scale for s in sums]
    for n, line in enumerate(lines):
        part_ref[n : n + 1, :] = line
    part_ref[3 * SHORT : 24, :] = jnp.zeros((24 - 3 * SHORT, LANES), F32)
    part_ref[24:32, :] = gl[...] * long_scale


def mixer(ids, taps, short_filter, prev, succ, q_in, k_in, v_in, grad_out, scales):
    rows, channels = q_in.shape[1:]
    blocks = rows // TAPS
    tail = pl.BlockSpec
    local = pl.BlockSpec((1, rows, LANES), lambda i: (0, 0, i))
    vm = lambda *shape: pltpu.VMEM(shape, F32)
    vb = lambda *shape: pltpu.VMEM(shape, BF16)
    out = jax.ShapeDtypeStruct((1, rows, channels), BF16)
    place = 2 * REACH // LEAD
    return pl.pallas_call(
        functools.partial(mixer_kernel, rows, *scales),
        grid=(channels // LANES,),
        in_specs=[
            pl.BlockSpec(ids.shape, lambda i: (0, 0)),
            pl.BlockSpec((LANES // 16, 2 * TAPS), lambda i: (i, 0)),
            pl.BlockSpec((3, SHORT, LANES), lambda i: (0, 0, i)),
            pl.BlockSpec((REACH, LANES), lambda i: (0, i)),
            pl.BlockSpec((REACH, LANES), lambda i: (1, i)),
            pl.BlockSpec((LEAD, LANES), lambda i: (place, i)),
            pl.BlockSpec((REACH, LANES), lambda i: (0, i)),
            pl.BlockSpec((REACH, LANES), lambda i: (1, i)),
            pl.BlockSpec((LEAD, LANES), lambda i: (place, i)),
            pl.BlockSpec((LEAD, LANES), lambda i: (place + 1, i)),
            local,
            local,
            local,
            local,
        ],
        out_specs=[local, local, local, pl.BlockSpec((32, LANES), lambda i: (0, i))],
        out_shape=[out, out, out, jax.ShapeDtypeStruct((32, channels), F32)],
        scratch_shapes=[
            vm(rows + 4 * TAPS, LANES),
            vm(SHORT - 1, rows + 4 * TAPS, LANES),
            vb(2 * blocks + 1, TAPS, TAPS),
            vb(3, 16, TAPS),
            vm(blocks, TAPS, TAPS),
            vb(TAPS, TAPS),
            vm(rows + REACH + LEAD, LANES),
            vm(rows + REACH + LEAD, LANES),
            vm(rows + REACH + LEAD, LANES),
            vm(rows + REACH, LANES),
            vm(rows + REACH, LANES),
            vm(rows + REACH, LANES),
            vm(rows + 2 * TAPS, LANES),
            vm(rows + 2 * TAPS, LANES),
            vb(LANES, rows + 2 * TAPS),
            vb(LANES, rows + TAPS),
            vb(LANES, rows + 2 * TAPS),
            vb(rows, LANES),
            vm(LANES, rows + TAPS),
            vm(LANES, rows + TAPS),
            vm(rows + 16, LANES),
            vm(rows + 16, LANES),
            vm(rows + 16, LANES),
            vm(8, LANES),
        ],
        compiler_params=pltpu.CompilerParams(vmem_limit_bytes=40 << 20),
        name="mixer",
    )(
        ids,
        taps,
        short_filter,
        prev,
        prev,
        prev,
        succ,
        succ,
        succ,
        succ,
        q_in,
        k_in,
        v_in,
        grad_out,
    )


def total_over(x, axis):
    size = lax.axis_size(axis)
    if size & (size - 1):
        return lax.psum(x, axis)
    bit = 1
    while bit < size:
        x = x + lax.ppermute(x, axis, [(i, i ^ bit) for i in range(size)])
        bit *= 2
    return x


def body(q_in, k_in, v_in, grad_out, genome_ids, long_filter, short_filter):
    rows, channels = q_in.shape[1:]
    seq_count = lax.axis_size("fsdp")
    length = rows * lax.axis_size("ctx")
    ids = genome_ids + 1
    wide = jnp.zeros((1, channels - REACH), BF16)
    tail_ids = jnp.concatenate([ids[:, rows - REACH :].astype(BF16), wide], axis=1)
    head_ids = jnp.concatenate([ids[:, :REACH].astype(BF16), wide], axis=1)
    tail = jnp.concatenate(
        [k_in[0, rows - REACH :], v_in[0, rows - REACH :], q_in[0, rows - LEAD :], tail_ids]
    )
    head = jnp.concatenate(
        [q_in[0, :REACH], grad_out[0, :REACH], k_in[0, :LEAD], v_in[0, :LEAD], head_ids]
    )
    prev = shifted(tail, "ctx", 1)
    succ = shifted(head, "ctx", -1)
    filters = lax.all_gather(long_filter, "fsdp", axis=1, tiled=True).astype(F32)
    blank = jnp.zeros((1, 2 * TAPS - REACH), F32)
    ids_ext = jnp.concatenate(
        [
            blank,
            prev[2 * REACH + LEAD :, :REACH].astype(F32),
            ids.astype(F32),
            succ[2 * REACH + 2 * LEAD :, :REACH].astype(F32),
            blank,
        ],
        axis=1,
    )
    turned = jnp.concatenate([filters[:, :1], filters[:, :0:-1]], axis=1)
    taps = jnp.concatenate([turned, filters], axis=1)
    groups = filters.shape[0]
    scales = (
        1.0 / math.sqrt(seq_count * length * (channels // groups)),
        1.0 / math.sqrt(seq_count * length),
    )
    out_q, out_k, out_v, sums = mixer(
        ids_ext, taps, short_filter, prev, succ, q_in, k_in, v_in, grad_out, scales
    )
    sums = total_over(total_over(sums, "ctx"), "fsdp")
    grad_short = sums[: 3 * SHORT].reshape(3, SHORT, channels)
    grad_long = sums[24:].reshape(8, channels // LANES, LANES).transpose(1, 0, 2)
    grad_long = grad_long.reshape(groups, TAPS)
    own = TAPS // seq_count
    grad_long = lax.dynamic_slice_in_dim(grad_long, lax.axis_index("fsdp") * own, own, 1)
    return out_q, out_k, out_v, grad_long, grad_short


def solution(mesh):
    return jax.shard_map(
        body,
        mesh=mesh,
        in_specs=(
            P("fsdp", "ctx", "tp"),
            P("fsdp", "ctx", "tp"),
            P("fsdp", "ctx", "tp"),
            P("fsdp", "ctx", "tp"),
            P("fsdp", "ctx"),
            P("tp", "fsdp"),
            P(None, None, "tp"),
        ),
        out_specs=(
            P("fsdp", "ctx", "tp"),
            P("fsdp", "ctx", "tp"),
            P("fsdp", "ctx", "tp"),
            P("tp", "fsdp"),
            P(None, None, "tp"),
        ),
        check_vma=False,
    )
```

```python
import functools
import math

import jax
import jax.numpy as jnp
from jax import lax
from jax.experimental import pallas as pl
from jax.experimental.pallas import tpu as pltpu
from jax.sharding import PartitionSpec as P

TAPS = 128
SHORT = 7
LANES = 128
GROUP = 16
EDGE = 8
HEAD_ROWS = LANES + 48
F32 = jnp.float32
BF16 = jnp.bfloat16
NT = (((1,), (1,)), ((), ()))
NN = (((1,), (0,)), ((), ()))
VMEM = pl.BlockSpec(memory_space=pltpu.VMEM)
HBM = pl.BlockSpec(memory_space=pltpu.HBM)


def swapped(near, far, axis):
    size = lax.axis_size(axis)
    near_route = [(i, i ^ 1) for i in range(size) if i ^ 1 < size]
    far_route = [(i + 1, i) for i in range(1, size - 1, 2)]
    far_route = far_route + [(i, j) for j, i in far_route]
    return lax.ppermute(near, axis, near_route), lax.ppermute(far, axis, far_route)


def dot(a, b, dims):
    return lax.dot_general(a, b, dims, preferred_element_type=F32)


def lanes_of(i):
    return pl.ds(pl.multiple_of(i * LANES, LANES), LANES)


def spread(line):
    return jnp.broadcast_to(line, (TAPS, TAPS)).T


def copy_all(pairs, sems, i, wait=False):
    for n, (source, target) in enumerate(pairs):
        copy = pltpu.make_async_copy(source, target, sems.at[i, n])
        if wait:
            copy.wait()
        else:
            copy.start()


def local_kernel(
    rows,
    ids_hbm,
    w_hbm,
    q_hbm,
    k_hbm,
    v_hbm,
    g_hbm,
    conv_hbm,
    turn_hbm,
    dzr_hbm,
    near_hbm,
    far_hbm,
    ids_ref,
    w_ref,
    bq,
    bk,
    bv,
    bg,
    conv_ref,
    turn_ref,
    dzr_ref,
    tail_ref,
    head_ref,
    idc,
    mj,
    xq,
    xk,
    xv,
    uf,
    dzf,
    small_sems,
    in_sems,
    out_sems,
):
    blocks = rows // TAPS
    count = q_hbm.shape[2] // LANES
    odd = lax.rem(lax.axis_index("ctx"), 2)

    def small():
        return ((ids_hbm, ids_ref), (w_hbm, w_ref))

    def inputs(i):
        lane = lanes_of(i)
        pairs = ((q_hbm, bq), (k_hbm, bk), (v_hbm, bv), (g_hbm, bg))
        return [(a.at[0, :, lane], b.at[i]) for a, b in pairs]

    def outputs(i):
        pairs = ((conv_ref, conv_hbm), (turn_ref, turn_hbm), (dzr_ref, dzr_hbm))
        return [(a.at[i], b.at[i]) for a, b in pairs]

    def packets(to_near, to_far):
        return ((to_near, near_hbm), (to_far, far_hbm))

    copy_all(small(), small_sems, 0)

    def fetch(i, carry):
        copy_all(inputs(i), in_sems, i)
        return carry

    lax.fori_loop(0, count, fetch, 0)
    copy_all(small(), small_sems, 0, wait=True)
    ids = (ids_ref[...] + 1).astype(F32)
    idc[0:EDGE] = jnp.zeros((EDGE, LANES), F32)
    for b in range(blocks):
        idc[EDGE + TAPS * b : EDGE + TAPS * (b + 1)] = spread(ids[:, TAPS * b : TAPS * (b + 1)])
    for x in (xq, xk, xv):
        x[0:EDGE] = jnp.zeros((EDGE, LANES), F32)

    def masks(i, carry):
        base = pl.multiple_of(16 * i, 16)
        here = idc[pl.ds(base + EDGE, 16), :]
        for j in range(1, SHORT):
            mj[j - 1, pl.ds(base, 16), :] = (here == idc[pl.ds(base + EDGE - j, 16), :]).astype(F32)
        return carry

    lax.fori_loop(0, rows // 16, masks, 0)
    pad = jnp.zeros((EDGE - blocks, LANES), F32)
    id_rows = [ids[:, TAPS * b : TAPS * (b + 1)] for b in range(blocks)]
    id_tile = jnp.concatenate(id_rows + [pad], axis=0)
    part = 32

    def one_block(i, carry):
        lane = lanes_of(i)
        copy_all(inputs(i), in_sems, i, wait=True)
        w = [[w_ref[n, j : j + 1, lane] for j in range(SHORT)] for n in range(3)]
        for x, source in ((xq, bq), (xk, bk), (xv, bv)):
            x[EDGE : EDGE + rows] = source[i].astype(F32)

        def convolve(n, inner):
            low = pl.multiple_of(part * n, part)
            out = []
            for x, taps in ((xq, w[0]), (xk, w[1]), (xv, w[2])):
                total = taps[0] * x[pl.ds(low + EDGE, part), :]
                for j in range(1, SHORT):
                    mask = mj[j - 1, pl.ds(low, part), :]
                    total += taps[j] * (mask * x[pl.ds(low + EDGE - j, part), :])
                out.append(total)
            conv_ref[i, 0, pl.ds(low, part), :] = out[1]
            conv_ref[i, 1, pl.ds(low, part), :] = out[2]
            uf[pl.ds(low, part), :] = out[1] * out[2]
            dz = bg[i, pl.ds(low, part), :].astype(F32) * out[0]
            dzf[pl.ds(low, part), :] = dz
            dzr_ref[i, pl.ds(low, part), :] = dz.astype(BF16)
            return inner

        lax.fori_loop(0, rows // part, convolve, 0)
        for b in range(blocks):
            here = slice(TAPS * b, TAPS * (b + 1))
            turned = uf[here, :].T.astype(BF16)
            turn_ref[i, 0:LANES, here] = turned
            if b == blocks - 1:
                tail_ref[i, 0:LANES, :] = turned
            turned = dzf[here, :].T.astype(BF16)
            turn_ref[i, LANES : 2 * LANES, here] = turned
            if b == 0:
                head_ref[i, 0:LANES, :] = turned

        def pair(a, b):
            return jnp.concatenate([a, b], axis=0).astype(BF16)

        last = slice(rows, rows + EDGE)
        first = slice(EDGE, 2 * EDGE)
        g_first = bg[i, 0 : 2 * EDGE, :].astype(F32)[:EDGE]
        beyond = slice(TAPS, TAPS + EDGE)
        tail_ref[i, LANES : LANES + 16, :] = pair(xk[last, :], xv[last, :])
        tail_ref[i, LANES + 16 : LANES + 32, :] = pair(xq[last, :], id_tile)
        tail_ref[i, LANES + 32 : LANES + 48, :] = jnp.zeros((16, LANES), BF16)
        head_ref[i, LANES : LANES + 16, :] = pair(xq[first, :], g_first)
        head_ref[i, LANES + 16 : LANES + 32, :] = pair(xk[first, :], xv[first, :])
        head_ref[i, LANES + 32 : LANES + 48, :] = pair(dzf[beyond, :], id_tile)
        copy_all(outputs(i), out_sems, i)
        return carry

    lax.fori_loop(0, count, one_block, 0)

    @pl.when(odd == 0)
    def even_packets():
        copy_all(packets(tail_ref, head_ref), small_sems, 0)
        copy_all(packets(tail_ref, head_ref), small_sems, 0, wait=True)

    @pl.when(odd == 1)
    def odd_packets():
        copy_all(packets(head_ref, tail_ref), small_sems, 0)
        copy_all(packets(head_ref, tail_ref), small_sems, 0, wait=True)

    def drain(i, carry):
        copy_all(outputs(i), out_sems, i, wait=True)
        return carry

    lax.fori_loop(0, count, drain, 0)


def local_part(ids, short_filter, q_in, k_in, v_in, grad_out):
    rows, channels = q_in.shape[1:]
    count = channels // LANES
    vm = lambda *shape: pltpu.VMEM(shape, F32)
    vb = lambda *shape: pltpu.VMEM(shape, BF16)
    shape = jax.ShapeDtypeStruct
    results = (
        ((count, 2, rows, LANES), F32),
        ((count, 2 * LANES, rows), BF16),
        ((count, rows, LANES), BF16),
    )
    packet = (count, HEAD_ROWS, LANES)
    return pl.pallas_call(
        functools.partial(local_kernel, rows),
        in_specs=[HBM] * 6,
        out_specs=[HBM] * 5,
        out_shape=[shape(*r) for r in results] + [shape(packet, BF16)] * 2,
        scratch_shapes=[
            pltpu.VMEM(ids.shape, jnp.int32),
            vm(*short_filter.shape),
            vb(count, rows, LANES),
            vb(count, rows, LANES),
            vb(count, rows, LANES),
            vb(count, rows, LANES),
            *[pltpu.VMEM(*r) for r in results],
            vb(*packet),
            vb(*packet),
            vm(rows + EDGE, LANES),
            vm(SHORT - 1, rows, LANES),
            vm(rows + EDGE, LANES),
            vm(rows + EDGE, LANES),
            vm(rows + EDGE, LANES),
            vm(rows, LANES),
            vm(rows, LANES),
            pltpu.SemaphoreType.DMA((1, 2)),
            pltpu.SemaphoreType.DMA((count, 4)),
            pltpu.SemaphoreType.DMA((count, 3)),
        ],
        compiler_params=pltpu.CompilerParams(vmem_limit_bytes=63 << 20),
        name="local_part",
    )(ids, short_filter, q_in, k_in, v_in, grad_out)


def mixer_kernel(
    rows,
    long_scale,
    short_scale,
    ids_hbm,
    filters_hbm,
    w_hbm,
    near_hbm,
    far_hbm,
    q_hbm,
    k_hbm,
    v_hbm,
    g_hbm,
    conv_hbm,
    turn_hbm,
    dzr_hbm,
    oq_hbm,
    ok_hbm,
    ov_hbm,
    part_ref,
    ids_ref,
    filters_ref,
    w_ref,
    prev_ref,
    next_ref,
    bq,
    bk,
    bv,
    bg,
    conv_ref,
    turn_ref,
    dzr_ref,
    oq_ref,
    ok_ref,
    ov_ref,
    taps_ref,
    idr,
    idc,
    mj,
    ml,
    mn,
    mp,
    flip,
    edges,
    ut,
    utr,
    dzt,
    dzr,
    zt,
    dut,
    dq,
    dk,
    dv,
    gl,
    small_sems,
    in_sems,
    out_sems,
):
    blocks = rows // TAPS
    frame = rows
    count = q_hbm.shape[2] // LANES
    per = LANES // GROUP
    odd = lax.rem(lax.axis_index("ctx"), 2)

    def small():
        return ((ids_hbm, ids_ref), (filters_hbm, filters_ref), (w_hbm, w_ref))

    def halos(i):
        return (
            ((far_hbm.at[i], prev_ref.at[i]), (near_hbm.at[i], next_ref.at[i])),
            ((near_hbm.at[i], prev_ref.at[i]), (far_hbm.at[i], next_ref.at[i])),
        )

    def inputs(i):
        lane = lanes_of(i)
        pairs = ((q_hbm, bq), (k_hbm, bk), (v_hbm, bv), (g_hbm, bg))
        pairs = [(a.at[0, :, lane], b.at[i]) for a, b in pairs]
        more = ((conv_hbm, conv_ref), (turn_hbm, turn_ref), (dzr_hbm, dzr_ref))
        return pairs + [(a.at[i], b.at[i]) for a, b in more]

    def outputs(i):
        lane = lanes_of(i)
        pairs = ((oq_ref, oq_hbm), (ok_ref, ok_hbm), (ov_ref, ov_hbm))
        return [(a.at[i], b.at[0, :, lane]) for a, b in pairs]

    copy_all(small(), small_sems, 0)

    def fetch(i, carry):
        @pl.when(odd == 0)
        def even_halos():
            copy_all(halos(i)[0], in_sems, i)

        @pl.when(odd == 1)
        def odd_halos():
            copy_all(halos(i)[1], in_sems, i)

        for n, (source, target) in enumerate(inputs(i)):
            pltpu.make_async_copy(source, target, in_sems.at[i, n + 2]).start()
        return carry

    lax.fori_loop(0, count, fetch, 0)

    def arrive(i):
        copy_all(halos(i)[0], in_sems, i, wait=True)
        for n, (source, target) in enumerate(inputs(i)):
            pltpu.make_async_copy(source, target, in_sems.at[i, n + 2]).wait()

    copy_all(small(), small_sems, 0, wait=True)
    arrive(0)

    row = lax.broadcasted_iota(jnp.int32, (TAPS, TAPS), 0)
    col = lax.broadcasted_iota(jnp.int32, (TAPS, TAPS), 1)
    own_ids = (ids_ref[...] + 1).astype(F32)
    prev_ids = prev_ref[0, LANES + 16 : LANES + 32, :].astype(F32)
    next_ids = next_ref[0, LANES + 32 : LANES + 48, :].astype(F32)
    for b in range(blocks):
        idr[b : b + 1, :] = prev_ids[EDGE + b : EDGE + b + 1]
        idr[blocks + b : blocks + b + 1, :] = own_ids[:, TAPS * b : TAPS * (b + 1)]
        idr[2 * blocks + b : 2 * blocks + b + 1, :] = next_ids[EDGE + b : EDGE + b + 1]
    for b in range(3 * blocks):
        idc[TAPS * b : TAPS * (b + 1), :] = spread(idr[b : b + 1, :])

    def short_masks(i, carry):
        base = pl.multiple_of(frame + EDGE * i, EDGE)
        here = idc[pl.ds(base, EDGE), :]
        for j in range(1, SHORT):
            mj[j - 1, pl.ds(base, EDGE), :] = (here == idc[pl.ds(base - j, EDGE), :]).astype(F32)
        return carry

    lax.fori_loop(0, (rows + 2 * EDGE) // EDGE, short_masks, 0)

    def same(t_block, s_block, length):
        start = frame + TAPS * t_block
        line = idr[blocks + s_block : blocks + s_block + 1, :]
        return (idc[start : start + length, :] == line).astype(F32)

    lower = (row >= col).astype(F32)
    upper = 1.0 - lower
    flip[...] = (row + col == TAPS - 1).astype(BF16)
    for b in range(blocks):
        ml[b] = (same(b, b, TAPS) * lower).astype(BF16)
    for b in range(blocks + 1):
        ml[blocks + b] = (same(b, b - 1, TAPS) * upper).astype(BF16)
    mn[0] = (same(blocks, blocks, 16) * lower[:16]).astype(BF16)
    mn[1] = (same(blocks, blocks, 16) * (row <= col).astype(F32)[:16]).astype(BF16)
    mn[2] = (same(blocks, blocks + 1, 16) * (row > col).astype(F32)[:16]).astype(BF16)
    for b in range(blocks):
        both = same(b, b, TAPS) * lower + same(b, b - 1, TAPS) * upper
        mp[b] = dot(both.astype(BF16), flip[...], NN)
    negated = jnp.logical_or(row + col == TAPS, row + col == 0).astype(BF16)
    reversed_taps = dot(filters_ref[...], negated, NN)
    forward_taps = filters_ref[...].astype(F32)
    for i in range(count):
        taps_ref[i, :, 0:TAPS] = reversed_taps[per * i : per * (i + 1)]
        taps_ref[i, :, TAPS:] = forward_taps[per * i : per * (i + 1)]

    lane_group = col // GROUP
    lower_flipped = row + col >= TAPS - 1
    first_lanes = col < EDGE
    blank = jnp.zeros((TAPS - EDGE, LANES), F32)

    def turned(x):
        return jnp.concatenate([x, blank], axis=0).T.astype(BF16)

    def filters_of(i):
        return [[w_ref[n, j : j + 1, lanes_of(i)] for j in range(SHORT)] for n in range(3)]

    def long_steps(i):
        w = filters_of(i)
        prev_kv = prev_ref[i, LANES : LANES + 16, :].astype(F32)
        prev_q = prev_ref[i, LANES + 16 : LANES + 32, :].astype(F32)
        next_qg = next_ref[i, LANES : LANES + 16, :].astype(F32)
        next_kv = next_ref[i, LANES + 16 : LANES + 32, :].astype(F32)
        next_dz = next_ref[i, LANES + 32 : LANES + 48, :].astype(F32)
        for n, (source, before, after) in enumerate(
            (
                (bq, prev_q[:EDGE], next_qg[:EDGE]),
                (bk, prev_kv[:EDGE], next_kv[:EDGE]),
                (bv, prev_kv[EDGE:], next_kv[EDGE:]),
            )
        ):
            edges[n, 0, 0:EDGE] = before
            edges[n, 0, EDGE : 2 * EDGE] = source[i, 0:16, :].astype(F32)[:EDGE]
            edges[n, 1, 0:EDGE] = source[i, rows - 16 : rows, :].astype(F32)[EDGE:]
            edges[n, 1, EDGE : 2 * EDGE] = after

        def convolve(n, m):
            low = frame + rows * m
            total = w[n][0] * edges[n, m, EDGE : 2 * EDGE]
            for j in range(1, SHORT):
                mask = mj[j - 1, low : low + EDGE, :]
                total += w[n][j] * (mask * edges[n, m, EDGE - j : 2 * EDGE - j])
            return total

        upstream = (bg[i, 0:16, :].astype(F32)[:EDGE], next_qg[EDGE:])
        fixed = []
        for m in range(2):
            query, key, value = [convolve(n, m) for n in range(3)]
            fixed.append((key, value, key * value, upstream[m] * query))

        ut[:, 0:TAPS] = prev_ref[i, 0:LANES, :]
        ut[:, TAPS : TAPS + rows] = turn_ref[i, 0:LANES, :]
        ut[:, TAPS : 2 * TAPS] = jnp.where(
            first_lanes, turned(fixed[0][2]), turn_ref[i, 0:LANES, 0:TAPS]
        )
        ut[:, TAPS + rows : 2 * TAPS + rows] = turned(fixed[1][2])
        dzt[:, TAPS:rows] = turn_ref[i, LANES:, TAPS:rows]
        dzt[:, 0:TAPS] = jnp.where(first_lanes, turned(fixed[0][3]), turn_ref[i, LANES:, 0:TAPS])
        dzt[:, rows : rows + TAPS] = jnp.where(
            first_lanes, turned(fixed[1][3]), next_ref[i, 0:LANES, :]
        )
        dzt[:, rows + TAPS :] = turned(next_dz[:EDGE])
        dzr[...] = dzr_ref[i]
        rest = dzr_ref[i, 0:16, :].astype(F32)[EDGE:]
        dzr[0:16] = jnp.concatenate([fixed[0][3], rest], axis=0).astype(BF16)
        for b in range(blocks + 1):
            here = slice(TAPS * b, TAPS * (b + 1))
            utr[:, here] = dot(ut[:, here], flip[...], NN).astype(BF16)

        def one_group(n):
            c = slice(GROUP * n, GROUP * (n + 1))
            line = jnp.broadcast_to(taps_ref[i, n : n + 1, 0:TAPS], (TAPS, TAPS))
            band = pltpu.roll(line, 0, 1, stride=1, stride_axis=0).astype(BF16)
            line = jnp.broadcast_to(taps_ref[i, n : n + 1, TAPS:], (16, TAPS))
            other = pltpu.roll(line, 0, 1, stride=1, stride_axis=0).astype(BF16)
            near = [band * ml[b] for b in range(blocks)]
            far = [band * ml[blocks + b] for b in range(blocks + 1)]
            for b in range(blocks):
                window = slice(TAPS * b, TAPS * (b + 2))
                here = slice(TAPS * b, TAPS * (b + 1))
                zt[c, here] = dot(ut[c, window], jnp.concatenate([far[b], near[b]], axis=1), NT)
                dut[c, here] = dot(dzt[c, window], jnp.concatenate([near[b], far[b + 1]], axis=0), NN)
            window = slice(TAPS * blocks, TAPS * (blocks + 2))
            here = slice(TAPS * blocks, TAPS * blocks + 16)
            edge = jnp.concatenate([far[blocks][:16], band[:16] * mn[0]], axis=1)
            zt[c, here] = dot(ut[c, window], edge, NT)
            edge = jnp.concatenate([other * mn[1], other * mn[2]], axis=1)
            dut[c, here] = dot(dzt[c, window], edge, NT)
            total = None
            for b in range(blocks):
                here = slice(TAPS * b, TAPS * (b + 1))
                mine = jnp.where(lane_group == n, dzr[here, :], jnp.zeros((), BF16))
                pairs = dot(mine, utr[:, TAPS * b : TAPS * (b + 2)], NN)
                term = jnp.where(lower_flipped, pairs[:, TAPS:], pairs[:, :TAPS]) * mp[b]
                total = term if total is None else total + term
            skewed = pltpu.roll(total, 1, 1, stride=1, stride_axis=0)
            gl[n : n + 1, :] = jnp.sum(skewed, axis=0, keepdims=True)

        def close():
            for b in range(blocks + 1):
                length = TAPS if b < blocks else EDGE
                here = slice(TAPS * b, TAPS * b + length)
                z = zt[:, TAPS * b : TAPS * (b + 1)].T[:length]
                du = dut[:, TAPS * b : TAPS * (b + 1)].T[:length]
                if b < blocks:
                    dq[here, :] = bg[i, here, :].astype(F32) * z
                    dk[here, :] = du * conv_ref[i, 1, here, :]
                    dv[here, :] = du * conv_ref[i, 0, here, :]
                else:
                    dq[here, :] = upstream[1] * z
                if b in (0, blocks):
                    key, value = fixed[0 if b == 0 else 1][:2]
                    there = slice(TAPS * b, TAPS * b + EDGE)
                    dk[there, :] = du[:EDGE] * value
                    dv[there, :] = du[:EDGE] * key
            part_ref[24:32, lanes_of(i)] = gl[...] * long_scale

        return one_group, close

    part = rows // per

    def finish_steps(i):
        w = filters_of(i)
        sums = [None] * (3 * SHORT)

        def one_part(m):
            low = part * m
            for n, (grad, source, out) in enumerate(
                ((dq, bq, oq_ref), (dk, bk, ok_ref), (dv, bv, ov_ref))
            ):
                x = source[i, low : low + part, :].astype(F32)
                total = None
                for j in range(SHORT):
                    piece = grad[low + j : low + j + part, :]
                    if j:
                        start = low + frame + j
                        piece = piece * mj[j - 1, start : start + part, :]
                    total = w[n][j] * piece if total is None else total + w[n][j] * piece
                    fresh = jnp.sum((x * piece).reshape(part // 8, 8, LANES), axis=0)
                    at = SHORT * n + j
                    sums[at] = fresh if m == 0 else sums[at] + fresh
                out[i, low : low + part, :] = total.astype(BF16)

        def close():
            lines = [jnp.sum(s, axis=0, keepdims=True) * short_scale for s in sums]
            lines.append(jnp.zeros((24 - 3 * SHORT, LANES), F32))
            part_ref[0:24, lanes_of(i)] = jnp.concatenate(lines, axis=0)
            copy_all(outputs(i), out_sems, i)

        return one_part, close

    one_group, close = long_steps(0)
    for n in range(per):
        one_group(n)
    close()

    def both(i, carry):
        arrive(i)
        one_group, close_long = long_steps(i)
        one_part, close_finish = finish_steps(i - 1)
        for n in range(per):
            one_group(n)
            one_part(n)
        close_finish()
        close_long()
        return carry

    lax.fori_loop(1, count, both, 0)
    one_part, close = finish_steps(count - 1)
    for n in range(per):
        one_part(n)
    close()

    def drain(i, carry):
        copy_all(outputs(i), out_sems, i, wait=True)
        return carry

    lax.fori_loop(0, count, drain, 0)


def mixer(operands, rows, channels, scales):
    blocks = rows // TAPS
    count = channels // LANES
    ids, filters, short_filter = operands[:3]
    vm = lambda *shape: pltpu.VMEM(shape, F32)
    vb = lambda *shape: pltpu.VMEM(shape, BF16)
    out = jax.ShapeDtypeStruct((1, rows, channels), BF16)
    buffered = [vb(count, rows, LANES)] * 4
    return pl.pallas_call(
        functools.partial(mixer_kernel, rows, *scales),
        in_specs=[HBM] * len(operands),
        out_specs=[HBM, HBM, HBM, VMEM],
        out_shape=[out, out, out, jax.ShapeDtypeStruct((32, channels), F32)],
        scratch_shapes=[
            pltpu.VMEM(ids.shape, jnp.int32),
            vb(*filters.shape),
            vm(*short_filter.shape),
            vb(count, HEAD_ROWS, LANES),
            vb(count, HEAD_ROWS, LANES),
            *buffered,
            vm(count, 2, rows, LANES),
            vb(count, 2 * LANES, rows),
            vb(count, rows, LANES),
            *buffered[:3],
            vm(count, LANES // GROUP, 2 * TAPS),
            vm(8, LANES),
            vm(3 * rows, LANES),
            vm(SHORT - 1, 3 * rows, LANES),
            vb(2 * blocks + 1, TAPS, TAPS),
            vb(3, 16, TAPS),
            vm(blocks, TAPS, TAPS),
            vb(TAPS, TAPS),
            vm(3, 2, 2 * EDGE, LANES),
            vb(LANES, rows + 2 * TAPS),
            vb(LANES, rows + TAPS),
            vb(LANES, rows + 2 * TAPS),
            vb(rows, LANES),
            vm(LANES, rows + TAPS),
            vm(LANES, rows + TAPS),
            vm(rows + 16, LANES),
            vm(rows + 16, LANES),
            vm(rows + 16, LANES),
            vm(8, LANES),
            pltpu.SemaphoreType.DMA((1, 3)),
            pltpu.SemaphoreType.DMA((count, 9)),
            pltpu.SemaphoreType.DMA((count, 3)),
        ],
        compiler_params=pltpu.CompilerParams(vmem_limit_bytes=63 << 20),
        name="mixer",
    )(*operands)


def total_over(x, axis):
    size = lax.axis_size(axis)
    if size & (size - 1):
        return lax.psum(x, axis)
    bit = 1
    while bit < size:
        x = x + lax.ppermute(x, axis, [(i, i ^ bit) for i in range(size)])
        bit *= 2
    return x


def all_taps(long_filter):
    if lax.axis_size("fsdp") != 2:
        return lax.all_gather(long_filter, "fsdp", axis=1, tiled=True)
    other = lax.ppermute(long_filter, "fsdp", [(0, 1), (1, 0)])
    first = lax.axis_index("fsdp") == 0
    return jnp.where(
        first,
        jnp.concatenate([long_filter, other], axis=1),
        jnp.concatenate([other, long_filter], axis=1),
    )


def body(q_in, k_in, v_in, grad_out, genome_ids, long_filter, short_filter):
    rows, channels = q_in.shape[1:]
    seq_count = lax.axis_size("fsdp")
    length = rows * lax.axis_size("ctx")
    filters = all_taps(long_filter)
    groups = filters.shape[0]
    conv, turn, dzr, near, far = local_part(
        genome_ids, short_filter, q_in, k_in, v_in, grad_out
    )
    near, far = swapped(near, far, "ctx")
    scales = (
        1.0 / math.sqrt(seq_count * length * (channels // groups)),
        1.0 / math.sqrt(seq_count * length),
    )
    operands = (
        genome_ids, filters, short_filter, near, far, q_in, k_in, v_in, grad_out, conv, turn, dzr,
    )
    out_q, out_k, out_v, sums = mixer(operands, rows, channels, scales)
    sums = total_over(total_over(sums, "ctx"), "fsdp")
    grad_short = sums[: 3 * SHORT].reshape(3, SHORT, channels)
    grad_long = sums[24:].reshape(8, channels // LANES, LANES).transpose(1, 0, 2)
    grad_long = grad_long.reshape(groups, TAPS)
    own = TAPS // seq_count
    grad_long = lax.dynamic_slice_in_dim(grad_long, lax.axis_index("fsdp") * own, own, 1)
    return out_q, out_k, out_v, grad_long, grad_short


def solution(mesh):
    return jax.shard_map(
        body,
        mesh=mesh,
        in_specs=(
            P("fsdp", "ctx", "tp"),
            P("fsdp", "ctx", "tp"),
            P("fsdp", "ctx", "tp"),
            P("fsdp", "ctx", "tp"),
            P("fsdp", "ctx"),
            P("tp", "fsdp"),
            P(None, None, "tp"),
        ),
        out_specs=(
            P("fsdp", "ctx", "tp"),
            P("fsdp", "ctx", "tp"),
            P("fsdp", "ctx", "tp"),
            P("tp", "fsdp"),
            P(None, None, "tp"),
        ),
        check_vma=False,
    )
```

```python
import functools
import math

import jax
import jax.numpy as jnp
from jax import lax
from jax.experimental import pallas as pl
from jax.experimental.pallas import tpu as pltpu
from jax.sharding import PartitionSpec as P

TAPS = 128
SHORT = 7
LANES = 128
GROUP = 16
EDGE = 8
VMEM_LIMIT = 63 << 20
HEAD_ROWS = LANES + 48
F32 = jnp.float32
BF16 = jnp.bfloat16
NT = (((1,), (1,)), ((), ()))
NN = (((1,), (0,)), ((), ()))
VMEM = pl.BlockSpec(memory_space=pltpu.VMEM)
HBM = pl.BlockSpec(memory_space=pltpu.HBM)


def swapped(near, far, axis):
    size = lax.axis_size(axis)
    near_route = [(i, i ^ 1) for i in range(size) if i ^ 1 < size]
    far_route = [(i + 1, i) for i in range(1, size - 1, 2)]
    far_route = far_route + [(i, j) for j, i in far_route]
    return lax.ppermute(near, axis, near_route), lax.ppermute(far, axis, far_route)


def dot(a, b, dims):
    return lax.dot_general(a, b, dims, preferred_element_type=F32)


def lanes_of(i):
    return pl.ds(pl.multiple_of(i * LANES, LANES), LANES)


def spread(line):
    return jnp.broadcast_to(line, (TAPS, TAPS)).T


def copy_all(pairs, sems, i, wait=False):
    for n, (source, target) in enumerate(pairs):
        copy = pltpu.make_async_copy(source, target, sems.at[i, n])
        if wait:
            copy.wait()
        else:
            copy.start()


def half_kernel(
    rows,
    edge,
    ids_hbm,
    w_hbm,
    q_hbm,
    k_hbm,
    v_hbm,
    g_hbm,
    conv_hbm,
    dzr_hbm,
    one_hbm,
    two_hbm,
    ids_ref,
    w_ref,
    bq,
    bk,
    bv,
    bg,
    conv_ref,
    dzr_ref,
    one_ref,
    two_ref,
    idc,
    mj,
    xq,
    xk,
    xv,
    uf,
    dzf,
    small_sems,
    in_sems,
    out_sems,
    packet_sems,
):
    count = q_hbm.shape[2] // LANES
    odd = lax.rem(lax.axis_index("ctx"), 2)
    kv_low, q_low = (TAPS, 0) if edge else (0, TAPS)
    lead = 16

    def small():
        return ((ids_hbm, ids_ref), (w_hbm, w_ref))

    def inputs(i):
        lane = lanes_of(i)
        pairs = ((q_hbm, bq), (k_hbm, bk), (v_hbm, bv), (g_hbm, bg))
        return [(a.at[0, :, lane], b.at[:, lane]) for a, b in pairs]

    def outputs(i):
        pairs = [(conv_ref, conv_hbm), (dzr_ref, dzr_hbm)]
        return [(a.at[i], b.at[i]) for a, b in pairs]

    def packets(i):
        one, two = one_ref.at[i], two_ref.at[i]
        near, far = one_hbm.at[i], two_hbm.at[i]
        return ((one, near), (two, far)), ((two, near), (one, far))

    def send_packets(i):
        if not edge:
            copy_all(packets(i)[0], packet_sems, i)
            return

        @pl.when(odd == 0)
        def even_packets():
            copy_all(packets(i)[0], packet_sems, i)

        @pl.when(odd == 1)
        def odd_packets():
            copy_all(packets(i)[1], packet_sems, i)

    copy_all(small(), small_sems, 0)

    def fetch(i, carry):
        copy_all(inputs(i), in_sems, i)
        return carry

    lax.fori_loop(0, count, fetch, 0)
    copy_all(small(), small_sems, 0, wait=True)
    ids = (ids_ref[...] + 1).astype(F32)
    idc[0:EDGE] = jnp.zeros((EDGE, LANES), F32)
    for b in range(2):
        idc[EDGE + TAPS * b : EDGE + TAPS * (b + 1)] = spread(ids[:, TAPS * b : TAPS * (b + 1)])
    for x in (xq, xk, xv):
        x[0:lead] = jnp.zeros((lead, LANES), F32)

    def masks(i, carry):
        base = pl.multiple_of(16 * i, 16)
        here = idc[pl.ds(base + EDGE, 16), :]
        for j in range(1, SHORT):
            mj[j - 1, pl.ds(base, 16), :] = (here == idc[pl.ds(base + EDGE - j, 16), :]).astype(F32)
        return carry

    lax.fori_loop(0, rows // 16, masks, 0)
    pad = jnp.zeros((EDGE - 2, LANES), F32)
    id_rows = [ids[:, TAPS * b : TAPS * (b + 1)] for b in range(2)]
    id_tile = jnp.concatenate(id_rows + [pad], axis=0)
    part = 32

    def pair(a, b):
        return jnp.concatenate([a, b], axis=0).astype(BF16)

    def one_block(i, carry):
        lane = lanes_of(i)
        copy_all(inputs(i), in_sems, i, wait=True)
        w = [[w_ref[n, j : j + 1, lane] for j in range(SHORT)] for n in range(3)]
        for x, source, low in ((xq, bq, q_low), (xk, bk, kv_low), (xv, bv, kv_low)):
            if low:
                x[0:lead] = source[low - lead : low, lane].astype(F32)
            size = TAPS if low else TAPS + lead
            x[lead : lead + size] = source[low : low + size, lane].astype(F32)

        def filtered(x, taps, low, at, size):
            total = taps[0] * x[pl.ds(at + lead, size), :]
            for j in range(1, SHORT):
                mask = mj[j - 1, pl.ds(at + low, size), :]
                total += taps[j] * (mask * x[pl.ds(at + lead - j, size), :])
            return total

        def convolve(n, inner):
            at = pl.multiple_of(part * n, part)
            key = filtered(xk, w[1], kv_low, at, part)
            value = filtered(xv, w[2], kv_low, at, part)
            query = filtered(xq, w[0], q_low, at, part)
            conv_ref[i, 0, pl.ds(at, part), :] = key
            conv_ref[i, 1, pl.ds(at, part), :] = value
            uf[pl.ds(at, part), :] = key * value
            dz = bg[pl.ds(at + q_low, part), lane].astype(F32) * query
            dzf[pl.ds(at, part), :] = dz
            dzr_ref[i, pl.ds(at, part), :] = dz.astype(BF16)
            return inner

        lax.fori_loop(0, TAPS // part, convolve, 0)
        one_ref[i, 0:LANES, :] = uf[...].T.astype(BF16)
        two_ref[i, 0:LANES, :] = dzf[...].T.astype(BF16)
        if edge:
            beyond = bg[TAPS : TAPS + 16, lane].astype(F32)[:EDGE]
            beyond = beyond * filtered(xq, w[0], q_low, TAPS, EDGE)
            last = slice(lead + TAPS - EDGE, lead + TAPS)
            q_last = bq[rows - 16 : rows, lane].astype(F32)[EDGE:]
            k_first = bk[0:16, lane].astype(F32)[:EDGE]
            v_first = bv[0:16, lane].astype(F32)[:EDGE]
            g_first = bg[0:16, lane].astype(F32)[:EDGE]
            one_ref[i, LANES : LANES + 16, :] = pair(xk[last, :], xv[last, :])
            one_ref[i, LANES + 16 : LANES + 32, :] = pair(q_last, id_tile)
            one_ref[i, LANES + 32 : LANES + 48, :] = jnp.zeros((16, LANES), BF16)
            two_ref[i, LANES : LANES + 16, :] = pair(xq[lead : lead + EDGE, :], g_first)
            two_ref[i, LANES + 16 : LANES + 32, :] = pair(k_first, v_first)
            two_ref[i, LANES + 32 : LANES + 48, :] = pair(beyond, id_tile)
        send_packets(i)
        copy_all(outputs(i), out_sems, i)
        return carry

    lax.fori_loop(0, count, one_block, 0)

    def drain(i, carry):
        copy_all(packets(i)[0], packet_sems, i, wait=True)
        copy_all(outputs(i), out_sems, i, wait=True)
        return carry

    lax.fori_loop(0, count, drain, 0)


def half_part(edge, ids, short_filter, q_in, k_in, v_in, grad_out):
    rows, channels = q_in.shape[1:]
    count = channels // LANES
    vm = lambda *shape: pltpu.VMEM(shape, F32)
    vb = lambda *shape: pltpu.VMEM(shape, BF16)
    packet = (count, HEAD_ROWS if edge else LANES, LANES)
    results = (
        ((count, 2, TAPS, LANES), F32),
        ((count, TAPS, LANES), BF16),
        (packet, BF16),
        (packet, BF16),
    )
    return pl.pallas_call(
        functools.partial(half_kernel, rows, edge),
        in_specs=[HBM] * 6,
        out_specs=[HBM] * 4,
        out_shape=[jax.ShapeDtypeStruct(*r) for r in results],
        scratch_shapes=[
            pltpu.VMEM(ids.shape, jnp.int32),
            vm(*short_filter.shape),
            *[vb(rows, channels)] * 4,
            *[pltpu.VMEM(*r) for r in results],
            vm(rows + EDGE, LANES),
            vm(SHORT - 1, rows, LANES),
            *[vm(TAPS + 32, LANES)] * 3,
            vm(TAPS, LANES),
            vm(TAPS, LANES),
            pltpu.SemaphoreType.DMA((1, 2)),
            pltpu.SemaphoreType.DMA((count, 4)),
            pltpu.SemaphoreType.DMA((count, 2)),
            pltpu.SemaphoreType.DMA((count, 2)),
        ],
        compiler_params=pltpu.CompilerParams(vmem_limit_bytes=VMEM_LIMIT),
        cost_estimate=pl.CostEstimate(
            flops=8_000_000_000, bytes_accessed=16_000_000, transcendentals=0
        ),
        name="edge_half" if edge else "other_half",
    )(ids, short_filter, q_in, k_in, v_in, grad_out)


def mixer_kernel(
    rows,
    long_scale,
    short_scale,
    ids_hbm,
    filters_hbm,
    w_hbm,
    near_hbm,
    far_hbm,
    q_hbm,
    k_hbm,
    v_hbm,
    g_hbm,
    sent_near_hbm,
    sent_far_hbm,
    conv_late_hbm,
    dzr_early_hbm,
    conv_early_hbm,
    dzr_late_hbm,
    u_early_hbm,
    dz_late_hbm,
    oq_hbm,
    ok_hbm,
    ov_hbm,
    part_ref,
    ids_ref,
    filters_ref,
    w_ref,
    prev_ref,
    next_ref,
    bq,
    bk,
    bv,
    bg,
    tail_ref,
    head_ref,
    conv_late,
    dzr_early,
    conv_early,
    dzr_late,
    u_early,
    dz_late,
    oq_ref,
    ok_ref,
    ov_ref,
    tiles,
    idr,
    idc,
    mj,
    ml,
    mn,
    mp,
    flip,
    edges,
    ut,
    utr,
    dzt,
    dzr,
    zt,
    dut,
    dq,
    dk,
    dv,
    gl,
    fixes,
    bands,
    others,
    tops,
    products,
    small_sems,
    halo_sems,
    in_sems,
    out_sems,
):
    blocks = rows // TAPS
    frame = rows
    count = q_hbm.shape[2] // LANES
    per = LANES // GROUP
    odd = lax.rem(lax.axis_index("ctx"), 2)

    def small():
        return ((ids_hbm, ids_ref), (filters_hbm, filters_ref), (w_hbm, w_ref))

    waves = ((0, 1), (1, count - 1))

    def halos(wave):
        span = pl.ds(*waves[wave])
        far, near = far_hbm.at[span], near_hbm.at[span]
        prev, succ = prev_ref.at[span], next_ref.at[span]
        sent_far, sent_near = sent_far_hbm.at[span], sent_near_hbm.at[span]
        tail, head = tail_ref.at[span], head_ref.at[span]
        return (
            ((far, prev), (near, succ), (sent_near, tail), (sent_far, head)),
            ((near, prev), (far, succ), (sent_far, tail), (sent_near, head)),
        )

    def inputs(wave):
        start, size = waves[wave]
        span = pl.ds(start, size)
        lane = pl.ds(start * LANES, size * LANES)
        pairs = ((q_hbm, bq), (k_hbm, bk), (v_hbm, bv), (g_hbm, bg))
        pairs = [(a.at[0, :, lane], b.at[:, lane]) for a, b in pairs]
        more = (
            (conv_late_hbm, conv_late),
            (dzr_early_hbm, dzr_early),
            (conv_early_hbm, conv_early),
            (dzr_late_hbm, dzr_late),
            (u_early_hbm, u_early),
            (dz_late_hbm, dz_late),
        )
        return [(a.at[span], b.at[span]) for a, b in more] + pairs

    def outputs(i):
        lane = lanes_of(i)
        pairs = ((oq_ref, oq_hbm), (ok_ref, ok_hbm), (ov_ref, ov_hbm))
        return [(a.at[:, lane], b.at[0, :, lane]) for a, b in pairs]

    copy_all(small(), small_sems, 0)

    for wave in range(2):

        @pl.when(odd == 0)
        def even_halos():
            copy_all(halos(wave)[0], halo_sems, wave)

        @pl.when(odd == 1)
        def odd_halos():
            copy_all(halos(wave)[1], halo_sems, wave)

        copy_all(inputs(wave), in_sems, wave)

    def arrive(wave):
        copy_all(halos(wave)[0], halo_sems, wave, wait=True)
        copy_all(inputs(wave), in_sems, wave, wait=True)

    copy_all(small(), small_sems, 0, wait=True)
    arrive(0)

    row = lax.broadcasted_iota(jnp.int32, (TAPS, TAPS), 0)
    col = lax.broadcasted_iota(jnp.int32, (TAPS, TAPS), 1)
    own_ids = (ids_ref[...] + 1).astype(F32)
    prev_ids = prev_ref[0, LANES + 16 : LANES + 32, :].astype(F32)
    next_ids = next_ref[0, LANES + 32 : LANES + 48, :].astype(F32)
    for b in range(blocks):
        idr[b : b + 1, :] = prev_ids[EDGE + b : EDGE + b + 1]
        idr[blocks + b : blocks + b + 1, :] = own_ids[:, TAPS * b : TAPS * (b + 1)]
        idr[2 * blocks + b : 2 * blocks + b + 1, :] = next_ids[EDGE + b : EDGE + b + 1]
    for b in range(3 * blocks):
        idc[TAPS * b : TAPS * (b + 1), :] = spread(idr[b : b + 1, :])

    def short_masks(i, carry):
        base = pl.multiple_of(frame + EDGE * i, EDGE)
        here = idc[pl.ds(base, EDGE), :]
        for j in range(1, SHORT):
            mj[j - 1, pl.ds(base, EDGE), :] = (here == idc[pl.ds(base - j, EDGE), :]).astype(F32)
        return carry

    lax.fori_loop(0, (rows + 2 * EDGE) // EDGE, short_masks, 0)

    def same(t_block, s_block, length):
        start = frame + TAPS * t_block
        line = idr[blocks + s_block : blocks + s_block + 1, :]
        return (idc[start : start + length, :] == line).astype(F32)

    lower = (row >= col).astype(F32)
    upper = 1.0 - lower
    flip[...] = (row + col == TAPS - 1).astype(BF16)
    for b in range(blocks):
        ml[b] = (same(b, b, TAPS) * lower).astype(BF16)
    for b in range(blocks + 1):
        ml[blocks + b] = (same(b, b - 1, TAPS) * upper).astype(BF16)
    mn[0] = (same(blocks, blocks, 16) * lower[:16]).astype(BF16)
    mn[1] = (same(blocks, blocks, 16) * (row <= col).astype(F32)[:16]).astype(BF16)
    mn[2] = (same(blocks, blocks + 1, 16) * (row > col).astype(F32)[:16]).astype(BF16)
    for b in range(blocks):
        both = same(b, b, TAPS) * lower + same(b, b - 1, TAPS) * upper
        mp[b] = dot(both.astype(BF16), flip[...], NN)
    negated = jnp.logical_or(row + col == TAPS, row + col == 0).astype(BF16)
    reversed_taps = dot(filters_ref[...], negated, NN)
    forward_taps = filters_ref[...].astype(F32)
    for i in range(count * per):
        tiles[i, 0:1, :] = reversed_taps[i : i + 1]
        tiles[i, 1:2, :] = forward_taps[i : i + 1]

    lane_group = col // GROUP
    lower_flipped = row + col >= TAPS - 1
    first_lanes = col < EDGE
    blank = jnp.zeros((TAPS - EDGE, LANES), F32)

    def turned(x):
        return jnp.concatenate([x, blank], axis=0).T.astype(BF16)

    def filters_of(i):
        return [[w_ref[n, j : j + 1, lanes_of(i)] for j in range(SHORT)] for n in range(3)]

    def prepare(i):
        w = filters_of(i)
        prev_kv = prev_ref[i, LANES : LANES + 16, :].astype(F32)
        prev_q = prev_ref[i, LANES + 16 : LANES + 32, :].astype(F32)
        next_qg = next_ref[i, LANES : LANES + 16, :].astype(F32)
        next_kv = next_ref[i, LANES + 16 : LANES + 32, :].astype(F32)
        next_dz = next_ref[i, LANES + 32 : LANES + 48, :].astype(F32)
        for n, (source, before, after) in enumerate(
            (
                (bq, prev_q[:EDGE], next_qg[:EDGE]),
                (bk, prev_kv[:EDGE], next_kv[:EDGE]),
                (bv, prev_kv[EDGE:], next_kv[EDGE:]),
            )
        ):
            edges[n, 0, 0:EDGE] = before
            edges[n, 0, EDGE : 2 * EDGE] = source[0:16, lanes_of(i)].astype(F32)[:EDGE]
            edges[n, 1, 0:EDGE] = source[rows - 16 : rows, lanes_of(i)].astype(F32)[EDGE:]
            edges[n, 1, EDGE : 2 * EDGE] = after

        def convolve(n, m):
            low = frame + rows * m
            total = w[n][0] * edges[n, m, EDGE : 2 * EDGE]
            for j in range(1, SHORT):
                mask = mj[j - 1, low : low + EDGE, :]
                total += w[n][j] * (mask * edges[n, m, EDGE - j : 2 * EDGE - j])
            return total

        upstream = (bg[0:16, lanes_of(i)].astype(F32)[:EDGE], next_qg[EDGE:])
        fixed = []
        for m in range(2):
            query, key, value = [convolve(n, m) for n in range(3)]
            fixed.append((key, value, key * value, upstream[m] * query))

        ut[:, 0:TAPS] = prev_ref[i, 0:LANES, :]
        ut[:, TAPS : 2 * TAPS] = jnp.where(first_lanes, turned(fixed[0][2]), u_early[i])
        ut[:, 2 * TAPS : 3 * TAPS] = tail_ref[i, 0:LANES, :]
        ut[:, 3 * TAPS :] = turned(fixed[1][2])
        dzt[:, 0:TAPS] = jnp.where(first_lanes, turned(fixed[0][3]), head_ref[i, 0:LANES, :])
        dzt[:, TAPS : 2 * TAPS] = dz_late[i]
        dzt[:, 2 * TAPS : 3 * TAPS] = jnp.where(
            first_lanes, turned(fixed[1][3]), next_ref[i, 0:LANES, :]
        )
        dzt[:, 3 * TAPS :] = turned(next_dz[:EDGE])
        dzr[0:TAPS] = dzr_early[i]
        dzr[TAPS:] = dzr_late[i]
        rest = dzr_early[i, 0:16, :].astype(F32)[EDGE:]
        dzr[0:16] = jnp.concatenate([fixed[0][3], rest], axis=0).astype(BF16)
        for b in range(blocks + 1):
            here = slice(TAPS * b, TAPS * (b + 1))
            utr[:, here] = dot(ut[:, here], flip[...], NN).astype(BF16)

        for m in range(2):
            for n in range(2):
                fixes[m, n] = fixed[m][n]

    def make_bands(i, m, slot):
        if True:
            g = per * i + m
            base = pltpu.roll(jnp.broadcast_to(tiles[g, 0:1, :], (16, TAPS)), 0, 1, stride=1, stride_axis=0)
            base = base.astype(BF16)
            bands[slot, 0:16] = base
            for r in range(16, TAPS, 16):
                bands[slot, r : r + 16] = pltpu.roll(base, r, 1)
            tops[16 * m : 16 * m + 16] = base
            line = jnp.broadcast_to(tiles[g, 1:2, :], (16, TAPS))
            line = pltpu.roll(line, 0, 1, stride=1, stride_axis=0).astype(BF16)
            others[16 * m : 16 * m + 16] = line

    def sum_taps(i, m):
        skewed = pltpu.roll(products[m], 1, 1, stride=1, stride_axis=0)
        gl[per * i + m] = jnp.sum(skewed.reshape(TAPS // 8, 8, TAPS), axis=0)

    def multiply_taps():
        for b in range(blocks):
            here = slice(TAPS * b, TAPS * (b + 1))
            mine = [jnp.where(lane_group == m, dzr[here, :], jnp.zeros((), BF16)) for m in range(per)]
            pairs = dot(jnp.concatenate(mine, axis=0), utr[:, TAPS * b : TAPS * (b + 2)], NN)
            for m in range(per):
                own = pairs[TAPS * m : TAPS * (m + 1)]
                term = jnp.where(lower_flipped, own[:, TAPS:], own[:, :TAPS]) * mp[b]
                products[m] = term if b == 0 else products[m] + term

    def multiply(m, slot):
        c = slice(GROUP * m, GROUP * (m + 1))
        band = bands[slot]
        near = [band * ml[b] for b in range(blocks)]
        far = [band * ml[blocks + b] for b in range(blocks + 1)]
        weights = jnp.concatenate(
            [jnp.concatenate([far[b], near[b]], axis=1) for b in range(blocks)], axis=0
        )
        both = jnp.concatenate([ut[c, TAPS * b : TAPS * (b + 2)] for b in range(blocks)], axis=0)
        result = dot(both, weights, NT)
        for b in range(blocks):
            here = slice(TAPS * b, TAPS * (b + 1))
            zt[c, here] = result[GROUP * b : GROUP * (b + 1), here]
        weights = jnp.concatenate(
            [jnp.concatenate([near[b], far[b + 1]], axis=0) for b in range(blocks)], axis=1
        )
        both = jnp.concatenate([dzt[c, TAPS * b : TAPS * (b + 2)] for b in range(blocks)], axis=0)
        result = dot(both, weights, NN)
        for b in range(blocks):
            here = slice(TAPS * b, TAPS * (b + 1))
            dut[c, here] = result[GROUP * b : GROUP * (b + 1), here]

    def edge_rows(rows_of, first, second, signal):
        left = [rows_of[16 * m : 16 * m + 16] * first for m in range(per)]
        right = [rows_of[16 * m : 16 * m + 16] * second for m in range(per)]
        left, right = jnp.concatenate(left, axis=0), jnp.concatenate(right, axis=0)
        result = dot(jnp.concatenate([left, right], axis=1), signal, NT)
        total = None
        for m in range(per):
            own = jnp.where(lane_group[:16] == m, result[16 * m : 16 * m + 16], 0.0)
            total = own if total is None else total + own
        return total

    def close(i):
        below = next_ref[i, LANES : LANES + 16, :].astype(F32)[EDGE:]
        window = slice(TAPS * blocks, TAPS * (blocks + 2))
        z2 = edge_rows(tops, ml[2 * blocks, 0:16], mn[0], ut[:, window])
        du2 = edge_rows(others, mn[1], mn[2], dzt[:, window])
        for b in range(blocks + 1):
            length = TAPS if b < blocks else EDGE
            here = slice(TAPS * b, TAPS * b + length)
            z = zt[:, here].T if b < blocks else z2[:EDGE]
            du = dut[:, here].T if b < blocks else du2[:EDGE]
            if b < blocks:
                dq[here, :] = bg[here, lanes_of(i)].astype(F32) * z
                conv = conv_late if b else conv_early
                dk[here, :] = du * conv[i, 1]
                dv[here, :] = du * conv[i, 0]
            else:
                dq[here, :] = below * z
            if b in (0, blocks):
                m = 0 if b == 0 else 1
                key, value = fixes[m, 0], fixes[m, 1]
                there = slice(TAPS * b, TAPS * b + EDGE)
                dk[there, :] = du[:EDGE] * value
                dv[there, :] = du[:EDGE] * key

    steps = per
    groups = count * per
    part = 32

    def finish_steps(i):
        arrays = ((dq, bq, oq_ref), (dk, bk, ok_ref), (dv, bv, ov_ref))
        lane = lanes_of(i)
        for n in range(3 * SHORT):
            tiles[groups + n] = jnp.zeros((8, LANES), F32)

        def one_part(m):
            for n, (grad, source, out) in enumerate(arrays):
                sums = [None] * SHORT
                for at in range(rows // steps // part):
                    low = rows // steps * m + part * at
                    x = source[pl.ds(low, part), lane].astype(F32)
                    total = None
                    for j in range(SHORT):
                        piece = grad[pl.ds(low + j, part), :]
                        if j:
                            piece = piece * mj[j - 1, pl.ds(low + frame + j, part), :]
                        scaled = w_ref[n, j : j + 1, lane] * piece
                        total = scaled if total is None else total + scaled
                        fresh = jnp.sum((x * piece).reshape(part // 8, 8, LANES), axis=0)
                        sums[j] = fresh if at == 0 else sums[j] + fresh
                    out[pl.ds(low, part), lane] = total.astype(BF16)
                for j in range(SHORT):
                    tiles[groups + SHORT * n + j] += sums[j]

        def close():
            for n in range(3 * SHORT):
                line = jnp.sum(tiles[groups + n], axis=0, keepdims=True) * short_scale
                part_ref[n : n + 1, lane] = line
            copy_all(outputs(i), out_sems, i)

        return one_part, close

    part_ref[3 * SHORT : 24, :] = jnp.zeros((24 - 3 * SHORT, part_ref.shape[1]), F32)

    def long_block(i, between):
        make_bands(i, 0, 0)
        multiply_taps()
        for m in range(per):
            if m + 1 < per:
                make_bands(i, m + 1, (m + 1) % 2)
            multiply(m, m % 2)
            sum_taps(i, m)
            between(m)

    prepare(0)
    long_block(0, lambda m: None)
    close(0)
    arrive(1)
    prepare(1)

    def both(i, carry):
        one_part, close_finish = finish_steps(i - 1)
        long_block(i, one_part)
        close_finish()
        close(i)
        prepare(jnp.minimum(i + 1, count - 1))
        return carry

    lax.fori_loop(1, count, both, 0)
    one_part, close_finish = finish_steps(count - 1)
    for m in range(per):
        one_part(m)
    close_finish()
    for i in range(count):
        lines = [jnp.sum(gl[per * i + n], axis=0, keepdims=True) for n in range(per)]
        here = slice(LANES * i, LANES * (i + 1))
        part_ref[24:32, here] = jnp.concatenate(lines, axis=0) * long_scale

    def drain(i, carry):
        copy_all(outputs(i), out_sems, i, wait=True)
        return carry

    lax.fori_loop(0, count, drain, 0)


def mixer(operands, rows, channels, scales):
    blocks = rows // TAPS
    count = channels // LANES
    ids, filters, short_filter = operands[:3]
    vm = lambda *shape: pltpu.VMEM(shape, F32)
    vb = lambda *shape: pltpu.VMEM(shape, BF16)
    out = jax.ShapeDtypeStruct((1, rows, channels), BF16)
    buffered = [vb(rows, channels)] * 4
    return pl.pallas_call(
        functools.partial(mixer_kernel, rows, *scales),
        in_specs=[HBM] * len(operands),
        out_specs=[HBM, HBM, HBM, VMEM],
        out_shape=[out, out, out, jax.ShapeDtypeStruct((32, channels), F32)],
        scratch_shapes=[
            pltpu.VMEM(ids.shape, jnp.int32),
            vb(*filters.shape),
            vm(*short_filter.shape),
            vb(count, HEAD_ROWS, LANES),
            vb(count, HEAD_ROWS, LANES),
            *buffered,
            vb(count, HEAD_ROWS, LANES),
            vb(count, HEAD_ROWS, LANES),
            vm(count, 2, TAPS, LANES),
            vb(count, TAPS, LANES),
            vm(count, 2, TAPS, LANES),
            vb(count, TAPS, LANES),
            vb(count, LANES, TAPS),
            vb(count, LANES, TAPS),
            *buffered[:3],
            vm(channels // GROUP + 3 * SHORT, 8, TAPS),
            vm(8, LANES),
            vm(3 * rows, LANES),
            vm(SHORT - 1, 3 * rows, LANES),
            vb(2 * blocks + 1, TAPS, TAPS),
            vb(3, 16, TAPS),
            vm(blocks, TAPS, TAPS),
            vb(TAPS, TAPS),
            vm(3, 2, 2 * EDGE, LANES),
            vb(LANES, rows + 2 * TAPS),
            vb(LANES, rows + TAPS),
            vb(LANES, rows + 2 * TAPS),
            vb(rows, LANES),
            vm(LANES, rows + TAPS),
            vm(LANES, rows + TAPS),
            vm(rows + 16, LANES),
            vm(rows + 16, LANES),
            vm(rows + 16, LANES),
            vm(channels // GROUP, 8, TAPS),
            vm(2, 2, EDGE, LANES),
            vb(2, TAPS, TAPS),
            vb(LANES, TAPS),
            vb(LANES, TAPS),
            vm(LANES // GROUP, TAPS, TAPS),
            pltpu.SemaphoreType.DMA((1, 3)),
            pltpu.SemaphoreType.DMA((2, 4)),
            pltpu.SemaphoreType.DMA((2, 10)),
            pltpu.SemaphoreType.DMA((count, 3)),
        ],
        compiler_params=pltpu.CompilerParams(vmem_limit_bytes=63 << 20),
        name="mixer",
    )(*operands)


AXES = ("fsdp", "ctx")


def exchanged(x, bits):
    size = lax.axis_size(AXES)
    return lax.ppermute(x, AXES, [(i, i ^ bits) for i in range(size)]).astype(F32)


def sum_pair(x):
    return x + exchanged(x, 1)


def sum_rest(x):
    size = lax.axis_size(AXES)
    bit = 2
    while bit < size:
        sent = x.astype(BF16)
        x = sent.astype(F32) + exchanged(sent, bit)
        if 2 * bit < size:
            x = x + (exchanged(sent, 2 * bit) + exchanged(sent, 3 * bit))
        bit *= 4
    return x


def all_taps(long_filter):
    if lax.axis_size("fsdp") != 2:
        return lax.all_gather(long_filter, "fsdp", axis=1, tiled=True)
    other = lax.ppermute(long_filter, "fsdp", [(0, 1), (1, 0)])
    first = lax.axis_index("fsdp") == 0
    return jnp.where(
        first,
        jnp.concatenate([long_filter, other], axis=1),
        jnp.concatenate([other, long_filter], axis=1),
    )


def body(q_in, k_in, v_in, grad_out, genome_ids, long_filter, short_filter):
    rows, channels = q_in.shape[1:]
    seq_count = lax.axis_size("fsdp")
    length = rows * lax.axis_size("ctx")
    filters = all_taps(long_filter)
    groups = filters.shape[0]
    arrays = (genome_ids, short_filter, q_in, k_in, v_in, grad_out)
    conv_late, dzr_early, sent_near, sent_far = half_part(True, *arrays)
    near, far = swapped(sent_near, sent_far, "ctx")
    sent_near, sent_far, genome_ids = lax.optimization_barrier((sent_near, sent_far, genome_ids))
    conv_early, dzr_late, u_early, dz_late = half_part(False, genome_ids, *arrays[1:])
    scales = (
        1.0 / math.sqrt(seq_count * length * (channels // groups)),
        1.0 / math.sqrt(seq_count * length),
    )
    operands = (
        genome_ids, filters, short_filter, near, far, q_in, k_in, v_in, grad_out,
        sent_near, sent_far, conv_late, dzr_early, conv_early, dzr_late, u_early, dz_late,
    )
    out_q, out_k, out_v, sums = mixer(operands, rows, channels, scales)
    power = lax.axis_size(AXES)
    if power & (power - 1):
        sums = lax.psum(sums, AXES)
    else:
        sums = sum_rest(sum_pair(sums))
    grad_short = sums[: 3 * SHORT].reshape(3, SHORT, channels)
    grad_long = sums[24:].reshape(8, channels // LANES, LANES).transpose(1, 0, 2)
    grad_long = grad_long.reshape(groups, TAPS)
    own = TAPS // seq_count
    grad_long = lax.dynamic_slice_in_dim(grad_long, lax.axis_index("fsdp") * own, own, 1)
    return out_q, out_k, out_v, grad_long, grad_short


def solution(mesh):
    return jax.shard_map(
        body,
        mesh=mesh,
        in_specs=(
            P("fsdp", "ctx", "tp"),
            P("fsdp", "ctx", "tp"),
            P("fsdp", "ctx", "tp"),
            P("fsdp", "ctx", "tp"),
            P("fsdp", "ctx"),
            P("tp", "fsdp"),
            P(None, None, "tp"),
        ),
        out_specs=(
            P("fsdp", "ctx", "tp"),
            P("fsdp", "ctx", "tp"),
            P("fsdp", "ctx", "tp"),
            P("tp", "fsdp"),
            P(None, None, "tp"),
        ),
        check_vma=False,
    )
```

```python
import functools
import math

import jax
import jax.numpy as jnp
from jax import lax
from jax.experimental import pallas as pl
from jax.experimental.pallas import tpu as pltpu
from jax.sharding import PartitionSpec as P

TAPS = 128
SHORT = 7
LANES = 128
GROUP = 16
EDGE = 8
VMEM_LIMIT = 65300 << 10
HEAD_ROWS = LANES + 48
F32 = jnp.float32
BF16 = jnp.bfloat16
NT = (((1,), (1,)), ((), ()))
NN = (((1,), (0,)), ((), ()))
VMEM = pl.BlockSpec(memory_space=pltpu.VMEM)
HBM = pl.BlockSpec(memory_space=pltpu.HBM)


def swapped(near, far, axis):
    size = lax.axis_size(axis)
    near_route = [(i, i ^ 1) for i in range(size) if i ^ 1 < size]
    far_route = [(i + 1, i) for i in range(1, size - 1, 2)]
    far_route = far_route + [(i, j) for j, i in far_route]
    return lax.ppermute(near, axis, near_route), lax.ppermute(far, axis, far_route)


def dot(a, b, dims):
    return lax.dot_general(a, b, dims, preferred_element_type=F32)


def lanes_of(i):
    return pl.ds(pl.multiple_of(i * LANES, LANES), LANES)


def spread(line):
    return jnp.broadcast_to(line, (TAPS, TAPS)).T


def copy_all(pairs, sems, i, wait=False):
    for n, (source, target) in enumerate(pairs):
        copy = pltpu.make_async_copy(source, target, sems.at[i, n])
        if wait:
            copy.wait()
        else:
            copy.start()


def half_kernel(
    rows,
    edge,
    ids_hbm,
    w_hbm,
    q_hbm,
    k_hbm,
    v_hbm,
    g_hbm,
    conv_hbm,
    dzr_hbm,
    one_hbm,
    two_hbm,
    ids_ref,
    w_ref,
    bq,
    bk,
    bv,
    bg,
    conv_ref,
    dzr_ref,
    one_ref,
    two_ref,
    idc,
    mj,
    xq,
    xk,
    xv,
    uf,
    dzf,
    small_sems,
    in_sems,
    out_sems,
    packet_sems,
):
    count = q_hbm.shape[2] // LANES
    odd = lax.rem(lax.axis_index("ctx"), 2)
    kv_low, q_low = (TAPS, 0) if edge else (0, TAPS)
    lead = 16

    def small():
        return ((ids_hbm, ids_ref), (w_hbm, w_ref))

    def inputs(i):
        lane = lanes_of(i)
        pairs = ((q_hbm, bq), (k_hbm, bk), (v_hbm, bv), (g_hbm, bg))
        return [(a.at[0, :, lane], b.at[:, lane]) for a, b in pairs]

    def outputs(i):
        pairs = [(conv_ref, conv_hbm), (dzr_ref, dzr_hbm)]
        return [(a.at[i], b.at[i]) for a, b in pairs]

    def packets(i):
        one, two = one_ref.at[i], two_ref.at[i]
        near, far = one_hbm.at[i], two_hbm.at[i]
        return ((one, near), (two, far)), ((two, near), (one, far))

    def send_packets(i):
        if not edge:
            copy_all(packets(i)[0], packet_sems, i)
            return

        @pl.when(odd == 0)
        def even_packets():
            copy_all(packets(i)[0], packet_sems, i)

        @pl.when(odd == 1)
        def odd_packets():
            copy_all(packets(i)[1], packet_sems, i)

    copy_all(small(), small_sems, 0)

    def fetch(i, carry):
        copy_all(inputs(i), in_sems, i)
        return carry

    lax.fori_loop(0, count, fetch, 0)
    copy_all(small(), small_sems, 0, wait=True)
    ids = (ids_ref[...] + 1).astype(F32)
    idc[0:EDGE] = jnp.zeros((EDGE, LANES), F32)
    for b in range(2):
        idc[EDGE + TAPS * b : EDGE + TAPS * (b + 1)] = spread(ids[:, TAPS * b : TAPS * (b + 1)])
    for x in (xq, xk, xv):
        x[0:lead] = jnp.zeros((lead, LANES), F32)

    def masks(i, carry):
        base = pl.multiple_of(16 * i, 16)
        here = idc[pl.ds(base + EDGE, 16), :]
        for j in range(1, SHORT):
            mj[j - 1, pl.ds(base, 16), :] = (here == idc[pl.ds(base + EDGE - j, 16), :]).astype(F32)
        return carry

    lax.fori_loop(0, rows // 16, masks, 0)
    pad = jnp.zeros((EDGE - 2, LANES), F32)
    id_rows = [ids[:, TAPS * b : TAPS * (b + 1)] for b in range(2)]
    id_tile = jnp.concatenate(id_rows + [pad], axis=0)
    part = 32

    def pair(a, b):
        return jnp.concatenate([a, b], axis=0).astype(BF16)

    def one_block(i, carry):
        lane = lanes_of(i)
        copy_all(inputs(i), in_sems, i, wait=True)
        w = [[w_ref[n, j : j + 1, lane] for j in range(SHORT)] for n in range(3)]
        for x, source, low in ((xq, bq, q_low), (xk, bk, kv_low), (xv, bv, kv_low)):
            if low:
                x[0:lead] = source[low - lead : low, lane].astype(F32)
            size = TAPS if low else TAPS + lead
            x[lead : lead + size] = source[low : low + size, lane].astype(F32)

        def filtered(x, taps, low, at, size):
            total = taps[0] * x[pl.ds(at + lead, size), :]
            for j in range(1, SHORT):
                mask = mj[j - 1, pl.ds(at + low, size), :]
                total += taps[j] * (mask * x[pl.ds(at + lead - j, size), :])
            return total

        def convolve(n, inner):
            at = pl.multiple_of(part * n, part)
            key = filtered(xk, w[1], kv_low, at, part)
            value = filtered(xv, w[2], kv_low, at, part)
            query = filtered(xq, w[0], q_low, at, part)
            conv_ref[i, 0, pl.ds(at, part), :] = key
            conv_ref[i, 1, pl.ds(at, part), :] = value
            uf[pl.ds(at, part), :] = key * value
            dz = bg[pl.ds(at + q_low, part), lane].astype(F32) * query
            dzf[pl.ds(at, part), :] = dz
            dzr_ref[i, pl.ds(at, part), :] = dz.astype(BF16)
            return inner

        lax.fori_loop(0, TAPS // part, convolve, 0)
        one_ref[i, 0:LANES, :] = uf[...].T.astype(BF16)
        two_ref[i, 0:LANES, :] = dzf[...].T.astype(BF16)
        if edge:
            beyond = bg[TAPS : TAPS + 16, lane].astype(F32)[:EDGE]
            beyond = beyond * filtered(xq, w[0], q_low, TAPS, EDGE)
            last = slice(lead + TAPS - EDGE, lead + TAPS)
            q_last = bq[rows - 16 : rows, lane].astype(F32)[EDGE:]
            k_first = bk[0:16, lane].astype(F32)[:EDGE]
            v_first = bv[0:16, lane].astype(F32)[:EDGE]
            g_first = bg[0:16, lane].astype(F32)[:EDGE]
            one_ref[i, LANES : LANES + 16, :] = pair(xk[last, :], xv[last, :])
            one_ref[i, LANES + 16 : LANES + 32, :] = pair(q_last, id_tile)
            one_ref[i, LANES + 32 : LANES + 48, :] = jnp.zeros((16, LANES), BF16)
            two_ref[i, LANES : LANES + 16, :] = pair(xq[lead : lead + EDGE, :], g_first)
            two_ref[i, LANES + 16 : LANES + 32, :] = pair(k_first, v_first)
            two_ref[i, LANES + 32 : LANES + 48, :] = pair(beyond, id_tile)
        send_packets(i)
        copy_all(outputs(i), out_sems, i)
        return carry

    lax.fori_loop(0, count, one_block, 0)

    def drain(i, carry):
        copy_all(packets(i)[0], packet_sems, i, wait=True)
        copy_all(outputs(i), out_sems, i, wait=True)
        return carry

    lax.fori_loop(0, count, drain, 0)


def half_part(edge, ids, short_filter, q_in, k_in, v_in, grad_out):
    rows, channels = q_in.shape[1:]
    count = channels // LANES
    vm = lambda *shape: pltpu.VMEM(shape, F32)
    vb = lambda *shape: pltpu.VMEM(shape, BF16)
    packet = (count, HEAD_ROWS if edge else LANES, LANES)
    results = (
        ((count, 2, TAPS, LANES), F32),
        ((count, TAPS, LANES), BF16),
        (packet, BF16),
        (packet, BF16),
    )
    return pl.pallas_call(
        functools.partial(half_kernel, rows, edge),
        in_specs=[HBM] * 6,
        out_specs=[HBM] * 4,
        out_shape=[jax.ShapeDtypeStruct(*r) for r in results],
        scratch_shapes=[
            pltpu.VMEM(ids.shape, jnp.int32),
            vm(*short_filter.shape),
            *[vb(rows, channels)] * 4,
            *[pltpu.VMEM(*r) for r in results],
            vm(rows + EDGE, LANES),
            vm(SHORT - 1, rows, LANES),
            *[vm(TAPS + 32, LANES)] * 3,
            vm(TAPS, LANES),
            vm(TAPS, LANES),
            pltpu.SemaphoreType.DMA((1, 2)),
            pltpu.SemaphoreType.DMA((count, 4)),
            pltpu.SemaphoreType.DMA((count, 2)),
            pltpu.SemaphoreType.DMA((count, 2)),
        ],
        compiler_params=pltpu.CompilerParams(vmem_limit_bytes=VMEM_LIMIT),
        cost_estimate=pl.CostEstimate(
            flops=8_000_000_000, bytes_accessed=16_000_000, transcendentals=0
        ),
        name="edge_half" if edge else "other_half",
    )(ids, short_filter, q_in, k_in, v_in, grad_out)


def mixer_kernel(
    rows,
    long_scale,
    short_scale,
    ids_hbm,
    one_half_hbm,
    other_half_hbm,
    w_hbm,
    near_hbm,
    far_hbm,
    q_hbm,
    k_hbm,
    v_hbm,
    g_hbm,
    sent_near_hbm,
    sent_far_hbm,
    conv_late_hbm,
    dzr_early_hbm,
    conv_early_hbm,
    dzr_late_hbm,
    u_early_hbm,
    dz_late_hbm,
    oq_hbm,
    ok_hbm,
    ov_hbm,
    part_hbm,
    ids_ref,
    one_half,
    other_half,
    w_ref,
    prev_ref,
    next_ref,
    bq,
    bk,
    bv,
    bg,
    tail_ref,
    head_ref,
    conv_late,
    dzr_early,
    conv_early,
    dzr_late,
    u_early,
    dz_late,
    oq_ref,
    ok_ref,
    ov_ref,
    part_ref,
    tiles,
    idr,
    idc,
    mj,
    ml,
    mn,
    mp,
    flip,
    edges,
    ut,
    utr,
    dzt,
    dzr,
    zt,
    dut,
    dq,
    dk,
    dv,
    gl,
    fixes,
    bands,
    others,
    tops,
    products,
    small_sems,
    halo_sems,
    in_sems,
    out_sems,
):
    blocks = rows // TAPS
    frame = rows
    count = q_hbm.shape[2] // LANES
    per = LANES // GROUP
    odd = lax.rem(lax.axis_index("ctx"), 2)

    def small():
        return (
            (ids_hbm, ids_ref),
            (one_half_hbm, one_half),
            (other_half_hbm, other_half),
            (w_hbm, w_ref),
        )

    waves = ((0, 1), (1, 2), (3, count - 3))

    def halos(wave):
        span = pl.ds(*waves[wave])
        far, near = far_hbm.at[span], near_hbm.at[span]
        prev, succ = prev_ref.at[span], next_ref.at[span]
        sent_far, sent_near = sent_far_hbm.at[span], sent_near_hbm.at[span]
        tail, head = tail_ref.at[span], head_ref.at[span]
        return (
            ((far, prev), (near, succ), (sent_near, tail), (sent_far, head)),
            ((near, prev), (far, succ), (sent_far, tail), (sent_near, head)),
        )

    def inputs(wave):
        start, size = waves[wave]
        span = pl.ds(start, size)
        lane = pl.ds(start * LANES, size * LANES)
        pairs = ((q_hbm, bq), (k_hbm, bk), (v_hbm, bv), (g_hbm, bg))
        pairs = [(a.at[0, :, lane], b.at[:, lane]) for a, b in pairs]
        more = (
            (conv_late_hbm, conv_late),
            (dzr_early_hbm, dzr_early),
            (conv_early_hbm, conv_early),
            (dzr_late_hbm, dzr_late),
            (u_early_hbm, u_early),
            (dz_late_hbm, dz_late),
        )
        return [(a.at[span], b.at[span]) for a, b in more] + pairs

    def outputs(i):
        lane = lanes_of(i)
        pairs = ((oq_ref, oq_hbm), (ok_ref, ok_hbm), (ov_ref, ov_hbm))
        return [(a.at[:, lane], b.at[0, :, lane]) for a, b in pairs]

    def start_wave(wave):
        @pl.when(odd == 0)
        def even_halos():
            copy_all(halos(wave)[0], halo_sems, wave)

        @pl.when(odd == 1)
        def odd_halos():
            copy_all(halos(wave)[1], halo_sems, wave)

        copy_all(inputs(wave), in_sems, wave)

    def arrive_halos(wave):
        copy_all(halos(wave)[0], halo_sems, wave, wait=True)

    def arrive(wave):
        copy_all(inputs(wave), in_sems, wave, wait=True)

    copy_all(small(), small_sems, 0)
    start_wave(0)
    copy_all(small(), small_sems, 0, wait=True)
    arrive_halos(0)
    start_wave(1)

    row = lax.broadcasted_iota(jnp.int32, (TAPS, TAPS), 0)
    col = lax.broadcasted_iota(jnp.int32, (TAPS, TAPS), 1)
    own_ids = (ids_ref[...] + 1).astype(F32)
    prev_ids = prev_ref[0, LANES + 16 : LANES + 32, :].astype(F32)
    next_ids = next_ref[0, LANES + 32 : LANES + 48, :].astype(F32)
    for b in range(blocks):
        idr[b : b + 1, :] = prev_ids[EDGE + b : EDGE + b + 1]
        idr[blocks + b : blocks + b + 1, :] = own_ids[:, TAPS * b : TAPS * (b + 1)]
        idr[2 * blocks + b : 2 * blocks + b + 1, :] = next_ids[EDGE + b : EDGE + b + 1]
    for b in range(3 * blocks):
        idc[TAPS * b : TAPS * (b + 1), :] = spread(idr[b : b + 1, :])

    def short_masks(i, carry):
        base = pl.multiple_of(frame + EDGE * i, EDGE)
        here = idc[pl.ds(base, EDGE), :]
        for j in range(1, SHORT):
            mj[j - 1, pl.ds(base, EDGE), :] = (here == idc[pl.ds(base - j, EDGE), :]).astype(F32)
        return carry

    lax.fori_loop(0, (rows + 2 * EDGE) // EDGE, short_masks, 0)

    def same(t_block, s_block, length):
        start = frame + TAPS * t_block
        line = idr[blocks + s_block : blocks + s_block + 1, :]
        return (idc[start : start + length, :] == line).astype(F32)

    lower = (row >= col).astype(F32)
    upper = 1.0 - lower
    flip[...] = (row + col == TAPS - 1).astype(BF16)
    for b in range(blocks):
        ml[b] = (same(b, b, TAPS) * lower).astype(BF16)
    for b in range(blocks + 1):
        ml[blocks + b] = (same(b, b - 1, TAPS) * upper).astype(BF16)
    mn[0] = (same(blocks, blocks, 16) * lower[:16]).astype(BF16)
    mn[1] = (same(blocks, blocks, 16) * (row <= col).astype(F32)[:16]).astype(BF16)
    mn[2] = (same(blocks, blocks + 1, 16) * (row > col).astype(F32)[:16]).astype(BF16)
    for b in range(blocks):
        both = same(b, b, TAPS) * lower + same(b, b - 1, TAPS) * upper
        mp[b] = dot(both.astype(BF16), flip[...], NN)
    negated = jnp.logical_or(row + col == TAPS, row + col == 0).astype(BF16)
    first, second = one_half[...].astype(F32), other_half[...].astype(F32)
    if lax.axis_size("fsdp") == 2:
        mine = lax.axis_index("fsdp") == 0
        first, second = jnp.where(mine, first, second), jnp.where(mine, second, first)
    forward_taps = jnp.concatenate([first, second], axis=1)
    reversed_taps = dot(forward_taps.astype(BF16), negated, NN)
    for i in range(count * per):
        tiles[i, 0:1, :] = reversed_taps[i : i + 1]
        tiles[i, 1:2, :] = forward_taps[i : i + 1]

    lane_group = col // GROUP
    lower_flipped = row + col >= TAPS - 1
    first_lanes = col < EDGE
    blank = jnp.zeros((TAPS - EDGE, LANES), F32)

    def turned(x):
        return jnp.concatenate([x, blank], axis=0).T.astype(BF16)

    def filters_of(i):
        return [[w_ref[n, j : j + 1, lanes_of(i)] for j in range(SHORT)] for n in range(3)]

    def prepare(i):
        w = filters_of(i)
        prev_kv = prev_ref[i, LANES : LANES + 16, :].astype(F32)
        prev_q = prev_ref[i, LANES + 16 : LANES + 32, :].astype(F32)
        next_qg = next_ref[i, LANES : LANES + 16, :].astype(F32)
        next_kv = next_ref[i, LANES + 16 : LANES + 32, :].astype(F32)
        next_dz = next_ref[i, LANES + 32 : LANES + 48, :].astype(F32)
        for n, (source, before, after) in enumerate(
            (
                (bq, prev_q[:EDGE], next_qg[:EDGE]),
                (bk, prev_kv[:EDGE], next_kv[:EDGE]),
                (bv, prev_kv[EDGE:], next_kv[EDGE:]),
            )
        ):
            edges[n, 0, 0:EDGE] = before
            edges[n, 0, EDGE : 2 * EDGE] = source[0:16, lanes_of(i)].astype(F32)[:EDGE]
            edges[n, 1, 0:EDGE] = source[rows - 16 : rows, lanes_of(i)].astype(F32)[EDGE:]
            edges[n, 1, EDGE : 2 * EDGE] = after

        def convolve(n, m):
            low = frame + rows * m
            total = w[n][0] * edges[n, m, EDGE : 2 * EDGE]
            for j in range(1, SHORT):
                mask = mj[j - 1, low : low + EDGE, :]
                total += w[n][j] * (mask * edges[n, m, EDGE - j : 2 * EDGE - j])
            return total

        upstream = (bg[0:16, lanes_of(i)].astype(F32)[:EDGE], next_qg[EDGE:])
        fixed = []
        for m in range(2):
            query, key, value = [convolve(n, m) for n in range(3)]
            fixed.append((key, value, key * value, upstream[m] * query))

        ut[:, 0:TAPS] = prev_ref[i, 0:LANES, :]
        ut[:, TAPS : 2 * TAPS] = jnp.where(first_lanes, turned(fixed[0][2]), u_early[i])
        ut[:, 2 * TAPS : 3 * TAPS] = tail_ref[i, 0:LANES, :]
        ut[:, 3 * TAPS :] = turned(fixed[1][2])
        dzt[:, 0:TAPS] = jnp.where(first_lanes, turned(fixed[0][3]), head_ref[i, 0:LANES, :])
        dzt[:, TAPS : 2 * TAPS] = dz_late[i]
        dzt[:, 2 * TAPS : 3 * TAPS] = jnp.where(
            first_lanes, turned(fixed[1][3]), next_ref[i, 0:LANES, :]
        )
        dzt[:, 3 * TAPS :] = turned(next_dz[:EDGE])
        dzr[0:TAPS] = dzr_early[i]
        dzr[TAPS:] = dzr_late[i]
        rest = dzr_early[i, 0:16, :].astype(F32)[EDGE:]
        dzr[0:16] = jnp.concatenate([fixed[0][3], rest], axis=0).astype(BF16)
        for b in range(blocks + 1):
            here = slice(TAPS * b, TAPS * (b + 1))
            utr[:, here] = dot(ut[:, here], flip[...], NN).astype(BF16)

        for m in range(2):
            for n in range(2):
                fixes[m, n] = fixed[m][n]

    def make_bands(i, m, slot):
        if True:
            g = per * i + m
            base = pltpu.roll(jnp.broadcast_to(tiles[g, 0:1, :], (16, TAPS)), 0, 1, stride=1, stride_axis=0)
            base = base.astype(BF16)
            bands[slot, 0:16] = base
            for r in range(16, TAPS, 16):
                bands[slot, r : r + 16] = pltpu.roll(base, r, 1)
            tops[16 * m : 16 * m + 16] = base
            line = jnp.broadcast_to(tiles[g, 1:2, :], (16, TAPS))
            line = pltpu.roll(line, 0, 1, stride=1, stride_axis=0).astype(BF16)
            others[16 * m : 16 * m + 16] = line

    def sum_taps(i, m):
        skewed = pltpu.roll(products[m], 1, 1, stride=1, stride_axis=0)
        gl[per * i + m] = jnp.sum(skewed.reshape(TAPS // 8, 8, TAPS), axis=0)

    def multiply_taps():
        for b in range(blocks):
            here = slice(TAPS * b, TAPS * (b + 1))
            mine = [jnp.where(lane_group == m, dzr[here, :], jnp.zeros((), BF16)) for m in range(per)]
            pairs = dot(jnp.concatenate(mine, axis=0), utr[:, TAPS * b : TAPS * (b + 2)], NN)
            for m in range(per):
                own = pairs[TAPS * m : TAPS * (m + 1)]
                term = jnp.where(lower_flipped, own[:, TAPS:], own[:, :TAPS]) * mp[b]
                products[m] = term if b == 0 else products[m] + term

    def multiply(m, slot):
        c = slice(GROUP * m, GROUP * (m + 1))
        band = bands[slot]
        near = [band * ml[b] for b in range(blocks)]
        far = [band * ml[blocks + b] for b in range(blocks + 1)]
        weights = jnp.concatenate(
            [jnp.concatenate([far[b], near[b]], axis=1) for b in range(blocks)], axis=0
        )
        both = jnp.concatenate([ut[c, TAPS * b : TAPS * (b + 2)] for b in range(blocks)], axis=0)
        result = dot(both, weights, NT)
        for b in range(blocks):
            here = slice(TAPS * b, TAPS * (b + 1))
            zt[c, here] = result[GROUP * b : GROUP * (b + 1), here]
        weights = jnp.concatenate(
            [jnp.concatenate([near[b], far[b + 1]], axis=0) for b in range(blocks)], axis=1
        )
        both = jnp.concatenate([dzt[c, TAPS * b : TAPS * (b + 2)] for b in range(blocks)], axis=0)
        result = dot(both, weights, NN)
        for b in range(blocks):
            here = slice(TAPS * b, TAPS * (b + 1))
            dut[c, here] = result[GROUP * b : GROUP * (b + 1), here]

    def edge_rows(rows_of, first, second, signal):
        left = [rows_of[16 * m : 16 * m + 16] * first for m in range(per)]
        right = [rows_of[16 * m : 16 * m + 16] * second for m in range(per)]
        left, right = jnp.concatenate(left, axis=0), jnp.concatenate(right, axis=0)
        result = dot(jnp.concatenate([left, right], axis=1), signal, NT)
        total = None
        for m in range(per):
            own = jnp.where(lane_group[:16] == m, result[16 * m : 16 * m + 16], 0.0)
            total = own if total is None else total + own
        return total

    def close(i):
        below = next_ref[i, LANES : LANES + 16, :].astype(F32)[EDGE:]
        window = slice(TAPS * blocks, TAPS * (blocks + 2))
        z2 = edge_rows(tops, ml[2 * blocks, 0:16], mn[0], ut[:, window])
        du2 = edge_rows(others, mn[1], mn[2], dzt[:, window])
        for b in range(blocks + 1):
            length = TAPS if b < blocks else EDGE
            here = slice(TAPS * b, TAPS * b + length)
            z = zt[:, here].T if b < blocks else z2[:EDGE]
            du = dut[:, here].T if b < blocks else du2[:EDGE]
            if b < blocks:
                dq[here, :] = bg[here, lanes_of(i)].astype(F32) * z
                conv = conv_late if b else conv_early
                dk[here, :] = du * conv[i, 1]
                dv[here, :] = du * conv[i, 0]
            else:
                dq[here, :] = below * z
            if b in (0, blocks):
                m = 0 if b == 0 else 1
                key, value = fixes[m, 0], fixes[m, 1]
                there = slice(TAPS * b, TAPS * b + EDGE)
                dk[there, :] = du[:EDGE] * value
                dv[there, :] = du[:EDGE] * key

    steps = per
    groups = count * per
    part = 32

    def finish_steps(i):
        arrays = ((dq, bq, oq_ref), (dk, bk, ok_ref), (dv, bv, ov_ref))
        lane = lanes_of(i)
        for n in range(3 * SHORT):
            tiles[groups + n] = jnp.zeros((8, LANES), F32)

        def one_part(m):
            for n, (grad, source, out) in enumerate(arrays):
                sums = [None] * SHORT
                for at in range(rows // steps // part):
                    low = rows // steps * m + part * at
                    x = source[pl.ds(low, part), lane].astype(F32)
                    total = None
                    for j in range(SHORT):
                        piece = grad[pl.ds(low + j, part), :]
                        if j:
                            piece = piece * mj[j - 1, pl.ds(low + frame + j, part), :]
                        scaled = w_ref[n, j : j + 1, lane] * piece
                        total = scaled if total is None else total + scaled
                        fresh = jnp.sum((x * piece).reshape(part // 8, 8, LANES), axis=0)
                        sums[j] = fresh if at == 0 else sums[j] + fresh
                    out[pl.ds(low, part), lane] = total.astype(BF16)
                for j in range(SHORT):
                    tiles[groups + SHORT * n + j] += sums[j]

        def close():
            for n in range(3 * SHORT):
                line = jnp.sum(tiles[groups + n], axis=0, keepdims=True) * short_scale
                part_ref[n : n + 1, lane] = line
            copy_all(outputs(i), out_sems, i)

        return one_part, close

    part_ref[3 * SHORT : 24, :] = jnp.zeros((24 - 3 * SHORT, part_ref.shape[1]), F32)

    def long_block(i, between):
        make_bands(i, 0, 0)
        multiply_taps()
        for m in range(per):
            if m + 1 < per:
                make_bands(i, m + 1, (m + 1) % 2)
            multiply(m, m % 2)
            sum_taps(i, m)
            between(m)

    arrive(0)
    start_wave(2)
    prepare(0)
    long_block(0, lambda m: None)
    close(0)
    arrive_halos(1)
    arrive(1)
    prepare(1)

    def both(i, carry):
        @pl.when(i == 2)
        def rest_arrives():
            arrive_halos(2)
            arrive(2)

        one_part, close_finish = finish_steps(i - 1)
        long_block(i, one_part)
        close_finish()
        close(i)
        prepare(jnp.minimum(i + 1, count - 1))
        return carry

    lax.fori_loop(1, count, both, 0)
    one_part, close_finish = finish_steps(count - 1)
    for m in range(per):
        one_part(m)
    close_finish()
    for i in range(count):
        lines = [jnp.sum(gl[per * i + n], axis=0, keepdims=True) for n in range(per)]
        here = slice(LANES * i, LANES * (i + 1))
        part_ref[24:32, here] = jnp.concatenate(lines, axis=0) * long_scale

    copy_all([(part_ref, part_hbm)], small_sems, 0)

    def drain(i, carry):
        copy_all(outputs(i), out_sems, i, wait=True)
        return carry

    lax.fori_loop(0, count, drain, 0)
    copy_all([(part_ref, part_hbm)], small_sems, 0, wait=True)


def mixer(operands, rows, channels, scales):
    blocks = rows // TAPS
    count = channels // LANES
    ids, short_filter = operands[0], operands[3]
    vm = lambda *shape: pltpu.VMEM(shape, F32)
    vb = lambda *shape: pltpu.VMEM(shape, BF16)
    out = jax.ShapeDtypeStruct((1, rows, channels), BF16)
    buffered = [vb(rows, channels)] * 4
    return pl.pallas_call(
        functools.partial(mixer_kernel, rows, *scales),
        in_specs=[HBM] * len(operands),
        out_specs=[HBM] * 4,
        out_shape=[out, out, out, jax.ShapeDtypeStruct((32, channels), F32)],
        scratch_shapes=[
            pltpu.VMEM(ids.shape, jnp.int32),
            vb(*operands[1].shape),
            vb(*operands[2].shape),
            vm(*short_filter.shape),
            vb(count, HEAD_ROWS, LANES),
            vb(count, HEAD_ROWS, LANES),
            *buffered,
            vb(count, HEAD_ROWS, LANES),
            vb(count, HEAD_ROWS, LANES),
            vm(count, 2, TAPS, LANES),
            vb(count, TAPS, LANES),
            vm(count, 2, TAPS, LANES),
            vb(count, TAPS, LANES),
            vb(count, LANES, TAPS),
            vb(count, LANES, TAPS),
            *buffered[:3],
            vm(32, channels),
            vm(channels // GROUP + 3 * SHORT, 8, TAPS),
            vm(8, LANES),
            vm(3 * rows, LANES),
            vm(SHORT - 1, 3 * rows, LANES),
            vb(2 * blocks + 1, TAPS, TAPS),
            vb(3, 16, TAPS),
            vm(blocks, TAPS, TAPS),
            vb(TAPS, TAPS),
            vm(3, 2, 2 * EDGE, LANES),
            vb(LANES, rows + 2 * TAPS),
            vb(LANES, rows + TAPS),
            vb(LANES, rows + 2 * TAPS),
            vb(rows, LANES),
            vm(LANES, rows + TAPS),
            vm(LANES, rows + TAPS),
            vm(rows + 16, LANES),
            vm(rows + 16, LANES),
            vm(rows + 16, LANES),
            vm(channels // GROUP, 8, TAPS),
            vm(2, 2, EDGE, LANES),
            vb(2, TAPS, TAPS),
            vb(LANES, TAPS),
            vb(LANES, TAPS),
            vm(LANES // GROUP, TAPS, TAPS),
            pltpu.SemaphoreType.DMA((1, 4)),
            pltpu.SemaphoreType.DMA((3, 4)),
            pltpu.SemaphoreType.DMA((3, 10)),
            pltpu.SemaphoreType.DMA((count, 3)),
        ],
        compiler_params=pltpu.CompilerParams(vmem_limit_bytes=63 << 20),
        name="mixer",
    )(*operands)


AXES = ("fsdp", "ctx")


def exchanged(x, bits):
    size = lax.axis_size(AXES)
    return lax.ppermute(x, AXES, [(i, i ^ bits) for i in range(size)]).astype(F32)


def sum_pair(x):
    return x + exchanged(x, 1)


def sum_rest(x):
    size = lax.axis_size(AXES)
    bit = 2
    while bit < size:
        sent = x.astype(BF16)
        x = sent.astype(F32) + exchanged(sent, bit)
        if 2 * bit < size:
            x = x + (exchanged(sent, 2 * bit) + exchanged(sent, 3 * bit))
        bit *= 4
    return x


def tap_halves(long_filter):
    if lax.axis_size("fsdp") == 2:
        return long_filter, lax.ppermute(long_filter, "fsdp", [(0, 1), (1, 0)])
    filters = lax.all_gather(long_filter, "fsdp", axis=1, tiled=True)
    return filters[:, : TAPS // 2], filters[:, TAPS // 2 :]


def body(q_in, k_in, v_in, grad_out, genome_ids, long_filter, short_filter):
    rows, channels = q_in.shape[1:]
    seq_count = lax.axis_size("fsdp")
    length = rows * lax.axis_size("ctx")
    halves = tap_halves(long_filter)
    groups = long_filter.shape[0]
    arrays = (genome_ids, short_filter, q_in, k_in, v_in, grad_out)
    conv_late, dzr_early, sent_near, sent_far = half_part(True, *arrays)
    near, far = swapped(sent_near, sent_far, "ctx")
    sent_near, sent_far, genome_ids = lax.optimization_barrier((sent_near, sent_far, genome_ids))
    conv_early, dzr_late, u_early, dz_late = half_part(False, genome_ids, *arrays[1:])
    scales = (
        1.0 / math.sqrt(seq_count * length * (channels // groups)),
        1.0 / math.sqrt(seq_count * length),
    )
    operands = (
        genome_ids, *halves, short_filter, near, far, q_in, k_in, v_in, grad_out,
        sent_near, sent_far, conv_late, dzr_early, conv_early, dzr_late, u_early, dz_late,
    )
    out_q, out_k, out_v, sums = mixer(operands, rows, channels, scales)
    power = lax.axis_size(AXES)
    if power & (power - 1):
        sums = lax.psum(sums, AXES)
    else:
        sums = sum_rest(sum_pair(sums))
    grad_short = sums[: 3 * SHORT].reshape(3, SHORT, channels)
    grad_long = sums[24:].reshape(8, channels // LANES, LANES).transpose(1, 0, 2)
    grad_long = grad_long.reshape(groups, TAPS)
    own = TAPS // seq_count
    grad_long = lax.dynamic_slice_in_dim(grad_long, lax.axis_index("fsdp") * own, own, 1)
    return out_q, out_k, out_v, grad_long, grad_short


def solution(mesh):
    return jax.shard_map(
        body,
        mesh=mesh,
        in_specs=(
            P("fsdp", "ctx", "tp"),
            P("fsdp", "ctx", "tp"),
            P("fsdp", "ctx", "tp"),
            P("fsdp", "ctx", "tp"),
            P("fsdp", "ctx"),
            P("tp", "fsdp"),
            P(None, None, "tp"),
        ),
        out_specs=(
            P("fsdp", "ctx", "tp"),
            P("fsdp", "ctx", "tp"),
            P("fsdp", "ctx", "tp"),
            P("tp", "fsdp"),
            P(None, None, "tp"),
        ),
        check_vma=False,
    )
```

```python
import functools
import math

import jax
import jax.numpy as jnp
from jax import lax
from jax.experimental import pallas as pl
from jax.experimental.pallas import tpu as pltpu
from jax.sharding import PartitionSpec as P

TAPS = 128
SHORT = 7
LANES = 128
GROUP = 16
EDGE = 8
VMEM_LIMIT = 65300 << 10
HEAD_ROWS = LANES + 32
F32 = jnp.float32
BF16 = jnp.bfloat16
NT = (((1,), (1,)), ((), ()))
NN = (((1,), (0,)), ((), ()))
VMEM = pl.BlockSpec(memory_space=pltpu.VMEM)
HBM = pl.BlockSpec(memory_space=pltpu.HBM)


def swapped(near, far, axis):
    size = lax.axis_size(axis)
    near_route = [(i, i ^ 1) for i in range(size) if i ^ 1 < size]
    far_route = [(i + 1, i) for i in range(1, size - 1, 2)]
    far_route = far_route + [(i, j) for j, i in far_route]
    return lax.ppermute(near, axis, near_route), lax.ppermute(far, axis, far_route)


def dot(a, b, dims):
    return lax.dot_general(a, b, dims, preferred_element_type=F32)


def lanes_of(i):
    return pl.ds(pl.multiple_of(i * LANES, LANES), LANES)


def spread(line):
    return jnp.broadcast_to(line, (TAPS, TAPS)).T


def copy_all(pairs, sems, i, wait=False):
    for n, (source, target) in enumerate(pairs):
        copy = pltpu.make_async_copy(source, target, sems.at[i, n])
        if wait:
            copy.wait()
        else:
            copy.start()


def half_kernel(
    rows,
    edge,
    ids_hbm,
    w_hbm,
    q_hbm,
    k_hbm,
    v_hbm,
    g_hbm,
    conv_hbm,
    dzr_hbm,
    one_hbm,
    two_hbm,
    ids_ref,
    w_ref,
    bq,
    bk,
    bv,
    bg,
    conv_ref,
    dzr_ref,
    one_ref,
    two_ref,
    idc,
    mj,
    xq,
    xk,
    xv,
    uf,
    dzf,
    small_sems,
    in_sems,
    out_sems,
    packet_sems,
):
    count = q_hbm.shape[2] // LANES
    odd = lax.rem(lax.axis_index("ctx"), 2)
    kv_low, q_low = (TAPS, 0) if edge else (0, TAPS)
    lead = 16

    def small():
        return ((ids_hbm, ids_ref), (w_hbm, w_ref))

    def inputs(i):
        lane = lanes_of(i)
        pairs = ((q_hbm, bq), (k_hbm, bk), (v_hbm, bv), (g_hbm, bg))
        return [(a.at[0, :, lane], b.at[:, lane]) for a, b in pairs]

    def outputs(i):
        pairs = [(conv_ref, conv_hbm), (dzr_ref, dzr_hbm)]
        return [(a.at[i], b.at[i]) for a, b in pairs]

    def packets(i):
        one, two = one_ref.at[i], two_ref.at[i]
        near, far = one_hbm.at[i], two_hbm.at[i]
        return ((one, near), (two, far)), ((two, near), (one, far))

    def send_packets(i):
        if not edge:
            copy_all(packets(i)[0], packet_sems, i)
            return

        @pl.when(odd == 0)
        def even_packets():
            copy_all(packets(i)[0], packet_sems, i)

        @pl.when(odd == 1)
        def odd_packets():
            copy_all(packets(i)[1], packet_sems, i)

    copy_all(small(), small_sems, 0)

    def fetch(i, carry):
        copy_all(inputs(i), in_sems, i)
        return carry

    lax.fori_loop(0, count, fetch, 0)
    copy_all(small(), small_sems, 0, wait=True)
    ids = (ids_ref[...] + 1).astype(F32)
    idc[0:EDGE] = jnp.zeros((EDGE, LANES), F32)
    for b in range(2):
        idc[EDGE + TAPS * b : EDGE + TAPS * (b + 1)] = spread(ids[:, TAPS * b : TAPS * (b + 1)])
    for x in (xq, xk, xv):
        x[:, 0:lead] = jnp.zeros((2, lead, LANES), F32)

    def masks(i, carry):
        base = pl.multiple_of(16 * i, 16)
        here = idc[pl.ds(base + EDGE, 16), :]
        for j in range(1, SHORT):
            mj[j - 1, pl.ds(base, 16), :] = (here == idc[pl.ds(base + EDGE - j, 16), :]).astype(F32)
        return carry

    lax.fori_loop(0, rows // 16, masks, 0)
    pad = jnp.zeros((EDGE - 2, LANES), F32)
    id_rows = [ids[:, TAPS * b : TAPS * (b + 1)] for b in range(2)]
    id_tile = jnp.concatenate(id_rows + [pad], axis=0)
    id_late = jnp.concatenate([pad] + id_rows, axis=0)
    sub = lax.broadcasted_iota(jnp.int32, (EDGE, LANES), 0)
    part = 32

    def pair(a, b):
        return jnp.concatenate([a, b], axis=0).astype(BF16)

    def filtered(x, h, taps, low, at, size):
        total = taps[0] * x[h, pl.ds(at + lead, size), :]
        for j in range(1, SHORT):
            mask = mj[j - 1, pl.ds(at + low, size), :]
            total += taps[j] * (mask * x[h, pl.ds(at + lead - j, size), :])
        return total

    def two_blocks(half, carry):
        pair_of = [2 * half, 2 * half + 1]
        for h, i in enumerate(pair_of):
            lane = lanes_of(i)
            copy_all(inputs(i), in_sems, i, wait=True)
            for x, source, low in ((xq, bq, q_low), (xk, bk, kv_low), (xv, bv, kv_low)):
                if low:
                    x[h, 0:lead] = source[low - lead : low, lane].astype(F32)
                size = TAPS if low else TAPS + lead
                x[h, lead : lead + size] = source[low : low + size, lane].astype(F32)

        def taps_of(n, i):
            return [w_ref[n, j : j + 1, lanes_of(i)] for j in range(SHORT)]

        def convolve(n, inner):
            at = pl.multiple_of(part * n, part)
            for h, i in enumerate(pair_of):
                key = filtered(xk, h, taps_of(1, i), kv_low, at, part)
                value = filtered(xv, h, taps_of(2, i), kv_low, at, part)
                query = filtered(xq, h, taps_of(0, i), q_low, at, part)
                conv_ref[i, 0, pl.ds(at, part), :] = key
                conv_ref[i, 1, pl.ds(at, part), :] = value
                uf[h, pl.ds(at, part), :] = key * value
                dz = bg[pl.ds(at + q_low, part), lanes_of(i)].astype(F32) * query
                dzf[h, pl.ds(at, part), :] = dz
                dzr_ref[i, pl.ds(at, part), :] = dz.astype(BF16)
            return inner

        lax.fori_loop(0, TAPS // part, convolve, 0)
        for h, i in enumerate(pair_of):
            one_ref[i, 0:LANES, :] = uf[h].T.astype(BF16)
            two_ref[i, 0:LANES, :] = dzf[h].T.astype(BF16)
            if edge:
                lane = lanes_of(i)
                beyond = bg[TAPS : TAPS + 16, lane].astype(F32)[:EDGE]
                beyond = beyond * filtered(xq, h, taps_of(0, i), q_low, TAPS, EDGE)
                last = slice(lead + TAPS - EDGE, lead + TAPS)
                q_last = bq[rows - 16 : rows, lane].astype(F32)[EDGE:]
                k_first = bk[0:16, lane].astype(F32)[:EDGE]
                v_first = bv[0:16, lane].astype(F32)[:EDGE]
                g_first = bg[0:16, lane].astype(F32)[:EDGE]
                q_first = xq[h, lead : lead + EDGE, :]
                one_ref[i, LANES : LANES + 16, :] = pair(xk[h, last, :], xv[h, last, :])
                one_ref[i, LANES + 16 : LANES + 32, :] = pair(q_last, id_tile)
                late = sub >= EDGE - 2
                q_first = jnp.where(late, id_late, q_first)
                g_first = jnp.where(late, pltpu.roll(beyond, 6, 0), g_first)
                k_first = jnp.where(late, pltpu.roll(beyond, 4, 0), k_first)
                v_first = jnp.where(late, pltpu.roll(beyond, 2, 0), v_first)
                two_ref[i, LANES : LANES + 16, :] = pair(q_first, g_first)
                two_ref[i, LANES + 16 : LANES + 32, :] = pair(k_first, v_first)
        for i in pair_of:
            send_packets(i)
            copy_all(outputs(i), out_sems, i)
        return carry

    lax.fori_loop(0, count // 2, two_blocks, 0)

    def drain(i, carry):
        copy_all(packets(i)[0], packet_sems, i, wait=True)
        copy_all(outputs(i), out_sems, i, wait=True)
        return carry

    lax.fori_loop(0, count, drain, 0)


def half_part(edge, ids, short_filter, q_in, k_in, v_in, grad_out):
    rows, channels = q_in.shape[1:]
    count = channels // LANES
    vm = lambda *shape: pltpu.VMEM(shape, F32)
    vb = lambda *shape: pltpu.VMEM(shape, BF16)
    packet = (count, HEAD_ROWS if edge else LANES, LANES)
    results = (
        ((count, 2, TAPS, LANES), F32),
        ((count, TAPS, LANES), BF16),
        (packet, BF16),
        (packet, BF16),
    )
    return pl.pallas_call(
        functools.partial(half_kernel, rows, edge),
        in_specs=[HBM] * 6,
        out_specs=[HBM] * 4,
        out_shape=[jax.ShapeDtypeStruct(*r) for r in results],
        scratch_shapes=[
            pltpu.VMEM(ids.shape, jnp.int32),
            vm(*short_filter.shape),
            *[vb(rows, channels)] * 4,
            *[pltpu.VMEM(*r) for r in results],
            vm(rows + EDGE, LANES),
            vm(SHORT - 1, rows, LANES),
            *[vm(2, TAPS + 32, LANES)] * 3,
            vm(2, TAPS, LANES),
            vm(2, TAPS, LANES),
            pltpu.SemaphoreType.DMA((1, 2)),
            pltpu.SemaphoreType.DMA((count, 4)),
            pltpu.SemaphoreType.DMA((count, 2)),
            pltpu.SemaphoreType.DMA((count, 2)),
        ],
        compiler_params=pltpu.CompilerParams(vmem_limit_bytes=VMEM_LIMIT),
        cost_estimate=pl.CostEstimate(
            flops=8_000_000_000, bytes_accessed=16_000_000, transcendentals=0
        ),
        name="edge_half" if edge else "other_half",
    )(ids, short_filter, q_in, k_in, v_in, grad_out)


def mixer_kernel(
    rows,
    long_scale,
    short_scale,
    ids_hbm,
    one_half_hbm,
    other_half_hbm,
    w_hbm,
    near_hbm,
    far_hbm,
    q_hbm,
    k_hbm,
    v_hbm,
    g_hbm,
    sent_near_hbm,
    sent_far_hbm,
    conv_late_hbm,
    dzr_early_hbm,
    conv_early_hbm,
    dzr_late_hbm,
    u_early_hbm,
    dz_late_hbm,
    oq_hbm,
    ok_hbm,
    ov_hbm,
    part_hbm,
    ids_ref,
    one_half,
    other_half,
    w_ref,
    prev_ref,
    next_ref,
    bq,
    bk,
    bv,
    bg,
    tail_ref,
    head_ref,
    conv_late,
    dzr_early,
    conv_early,
    dzr_late,
    u_early,
    dz_late,
    oq_ref,
    ok_ref,
    ov_ref,
    part_ref,
    tiles,
    idr,
    idc,
    mj,
    ml,
    mn,
    mp,
    flip,
    edges,
    ut,
    utr,
    dzt,
    dzr,
    zt,
    dut,
    dq,
    dk,
    dv,
    gl,
    fixes,
    bands,
    others,
    tops,
    products,
    small_sems,
    halo_sems,
    in_sems,
    out_sems,
):
    blocks = rows // TAPS
    frame = rows
    count = q_hbm.shape[2] // LANES
    per = LANES // GROUP
    odd = lax.rem(lax.axis_index("ctx"), 2)

    def small():
        return (
            (ids_hbm, ids_ref),
            (one_half_hbm, one_half),
            (other_half_hbm, other_half),
            (w_hbm, w_ref),
        )

    waves = ((0, 1), (1, 2), (3, count - 3))

    def halos(wave):
        span = pl.ds(*waves[wave])
        far, near = far_hbm.at[span], near_hbm.at[span]
        prev, succ = prev_ref.at[span], next_ref.at[span]
        sent_far, sent_near = sent_far_hbm.at[span], sent_near_hbm.at[span]
        tail, head = tail_ref.at[span], head_ref.at[span]
        return (
            ((far, prev), (near, succ), (sent_near, tail), (sent_far, head)),
            ((near, prev), (far, succ), (sent_far, tail), (sent_near, head)),
        )

    def inputs(wave):
        start, size = waves[wave]
        span = pl.ds(start, size)
        lane = pl.ds(start * LANES, size * LANES)
        pairs = ((q_hbm, bq), (k_hbm, bk), (v_hbm, bv), (g_hbm, bg))
        pairs = [(a.at[0, :, lane], b.at[:, lane]) for a, b in pairs]
        more = (
            (conv_late_hbm, conv_late),
            (dzr_early_hbm, dzr_early),
            (conv_early_hbm, conv_early),
            (dzr_late_hbm, dzr_late),
            (u_early_hbm, u_early),
            (dz_late_hbm, dz_late),
        )
        return [(a.at[span], b.at[span]) for a, b in more] + pairs

    def outputs(i):
        lane = lanes_of(i)
        pairs = ((oq_ref, oq_hbm), (ok_ref, ok_hbm), (ov_ref, ov_hbm))
        return [(a.at[:, lane], b.at[0, :, lane]) for a, b in pairs]

    def start_wave(wave):
        @pl.when(odd == 0)
        def even_halos():
            copy_all(halos(wave)[0], halo_sems, wave)

        @pl.when(odd == 1)
        def odd_halos():
            copy_all(halos(wave)[1], halo_sems, wave)

        copy_all(inputs(wave), in_sems, wave)

    def arrive_halos(wave):
        copy_all(halos(wave)[0], halo_sems, wave, wait=True)

    def arrive(wave):
        copy_all(inputs(wave), in_sems, wave, wait=True)

    copy_all(small(), small_sems, 0)
    start_wave(0)
    copy_all(small(), small_sems, 0, wait=True)
    arrive_halos(0)
    start_wave(1)

    row = lax.broadcasted_iota(jnp.int32, (TAPS, TAPS), 0)
    col = lax.broadcasted_iota(jnp.int32, (TAPS, TAPS), 1)
    own_ids = (ids_ref[...] + 1).astype(F32)
    prev_ids = prev_ref[0, LANES + 16 : LANES + 32, :].astype(F32)
    next_ids = next_ref[0, LANES : LANES + 16, :].astype(F32)
    for b in range(blocks):
        idr[b : b + 1, :] = prev_ids[EDGE + b : EDGE + b + 1]
        idr[blocks + b : blocks + b + 1, :] = own_ids[:, TAPS * b : TAPS * (b + 1)]
        idr[2 * blocks + b : 2 * blocks + b + 1, :] = next_ids[EDGE - blocks + b : EDGE - blocks + b + 1]
    for b in range(3 * blocks):
        idc[TAPS * b : TAPS * (b + 1), :] = spread(idr[b : b + 1, :])

    def short_masks(i, carry):
        base = pl.multiple_of(frame + EDGE * i, EDGE)
        here = idc[pl.ds(base, EDGE), :]
        for j in range(1, SHORT):
            mj[j - 1, pl.ds(base, EDGE), :] = (here == idc[pl.ds(base - j, EDGE), :]).astype(F32)
        return carry

    lax.fori_loop(0, (rows + 2 * EDGE) // EDGE, short_masks, 0)

    def same(t_block, s_block, length):
        start = frame + TAPS * t_block
        line = idr[blocks + s_block : blocks + s_block + 1, :]
        return (idc[start : start + length, :] == line).astype(F32)

    lower = (row >= col).astype(F32)
    upper = 1.0 - lower
    flip[...] = (row + col == TAPS - 1).astype(BF16)
    for b in range(blocks):
        ml[b] = (same(b, b, TAPS) * lower).astype(BF16)
    for b in range(blocks + 1):
        ml[blocks + b] = (same(b, b - 1, TAPS) * upper).astype(BF16)
    mn[0] = (same(blocks, blocks, 16) * lower[:16]).astype(BF16)
    mn[1] = (same(blocks, blocks, 16) * (row <= col).astype(F32)[:16]).astype(BF16)
    mn[2] = (same(blocks, blocks + 1, 16) * (row > col).astype(F32)[:16]).astype(BF16)
    for b in range(blocks):
        both = same(b, b, TAPS) * lower + same(b, b - 1, TAPS) * upper
        mp[b] = dot(both.astype(BF16), flip[...], NN)
    negated = jnp.logical_or(row + col == TAPS, row + col == 0).astype(BF16)
    first, second = one_half[...].astype(F32), other_half[...].astype(F32)
    if lax.axis_size("fsdp") == 2:
        mine = lax.axis_index("fsdp") == 0
        first, second = jnp.where(mine, first, second), jnp.where(mine, second, first)
    forward_taps = jnp.concatenate([first, second], axis=1)
    reversed_taps = dot(forward_taps.astype(BF16), negated, NN)
    for i in range(count * per):
        tiles[i, 0:1, :] = reversed_taps[i : i + 1]
        tiles[i, 1:2, :] = forward_taps[i : i + 1]

    lane_group = col // GROUP
    lower_flipped = row + col >= TAPS - 1
    first_lanes = col < EDGE
    next_lanes = col < SHORT - 1
    sub = lax.broadcasted_iota(jnp.int32, (EDGE, LANES), 0)
    blank = jnp.zeros((TAPS - EDGE, LANES), F32)

    def turned(x):
        return jnp.concatenate([x, blank], axis=0).T.astype(BF16)

    def filters_of(i):
        return [[w_ref[n, j : j + 1, lanes_of(i)] for j in range(SHORT)] for n in range(3)]

    def prepare(i):
        w = filters_of(i)
        prev_kv = prev_ref[i, LANES : LANES + 16, :].astype(F32)
        prev_q = prev_ref[i, LANES + 16 : LANES + 32, :].astype(F32)
        next_qg = next_ref[i, LANES : LANES + 16, :].astype(F32)
        next_kv = next_ref[i, LANES + 16 : LANES + 32, :].astype(F32)
        next_dz = jnp.where(
            sub < 2,
            pltpu.roll(next_qg[EDGE:], 2, 0),
            jnp.where(
                sub < 4,
                pltpu.roll(next_kv[:EDGE], 4, 0),
                jnp.where(sub < 5, pltpu.roll(next_kv[EDGE:], 6, 0), 0.0),
            ),
        )
        for n, (source, before, after) in enumerate(
            (
                (bq, prev_q[:EDGE], next_qg[:EDGE]),
                (bk, prev_kv[:EDGE], next_kv[:EDGE]),
                (bv, prev_kv[EDGE:], next_kv[EDGE:]),
            )
        ):
            edges[n, 0, 0:EDGE] = before
            edges[n, 0, EDGE : 2 * EDGE] = source[0:16, lanes_of(i)].astype(F32)[:EDGE]
            edges[n, 1, 0:EDGE] = source[rows - 16 : rows, lanes_of(i)].astype(F32)[EDGE:]
            edges[n, 1, EDGE : 2 * EDGE] = after

        def convolve(n, m):
            low = frame + rows * m
            total = w[n][0] * edges[n, m, EDGE : 2 * EDGE]
            for j in range(1, SHORT):
                mask = mj[j - 1, low : low + EDGE, :]
                total += w[n][j] * (mask * edges[n, m, EDGE - j : 2 * EDGE - j])
            return total

        upstream = (bg[0:16, lanes_of(i)].astype(F32)[:EDGE], next_qg[EDGE:])
        fixed = []
        for m in range(2):
            query, key, value = [convolve(n, m) for n in range(3)]
            fixed.append((key, value, key * value, upstream[m] * query))

        ut[:, 0:TAPS] = prev_ref[i, 0:LANES, :]
        ut[:, TAPS : 2 * TAPS] = jnp.where(first_lanes, turned(fixed[0][2]), u_early[i])
        ut[:, 2 * TAPS : 3 * TAPS] = tail_ref[i, 0:LANES, :]
        ut[:, 3 * TAPS :] = turned(fixed[1][2])
        dzt[:, 0:TAPS] = jnp.where(first_lanes, turned(fixed[0][3]), head_ref[i, 0:LANES, :])
        dzt[:, TAPS : 2 * TAPS] = dz_late[i]
        dzt[:, 2 * TAPS : 3 * TAPS] = jnp.where(
            next_lanes, turned(fixed[1][3]), next_ref[i, 0:LANES, :]
        )
        dzt[:, 3 * TAPS :] = turned(next_dz[:EDGE])
        dzr[0:TAPS] = dzr_early[i]
        dzr[TAPS:] = dzr_late[i]
        rest = dzr_early[i, 0:16, :].astype(F32)[EDGE:]
        dzr[0:16] = jnp.concatenate([fixed[0][3], rest], axis=0).astype(BF16)
        for b in range(blocks + 1):
            here = slice(TAPS * b, TAPS * (b + 1))
            utr[:, here] = dot(ut[:, here], flip[...], NN).astype(BF16)

        for m in range(2):
            for n in range(2):
                fixes[m, n] = fixed[m][n]

    def make_bands(i, m, slot):
        if True:
            g = per * i + m
            base = pltpu.roll(jnp.broadcast_to(tiles[g, 0:1, :], (16, TAPS)), 0, 1, stride=1, stride_axis=0)
            base = base.astype(BF16)
            bands[slot, 0:16] = base
            for r in range(16, TAPS, 16):
                bands[slot, r : r + 16] = pltpu.roll(base, r, 1)
            tops[16 * m : 16 * m + 16] = base
            line = jnp.broadcast_to(tiles[g, 1:2, :], (16, TAPS))
            line = pltpu.roll(line, 0, 1, stride=1, stride_axis=0).astype(BF16)
            others[16 * m : 16 * m + 16] = line

    def sum_taps(i, m):
        skewed = pltpu.roll(products[m], 1, 1, stride=1, stride_axis=0)
        gl[per * i + m] = jnp.sum(skewed.reshape(TAPS // 8, 8, TAPS), axis=0)

    def multiply_taps():
        for b in range(blocks):
            here = slice(TAPS * b, TAPS * (b + 1))
            mine = [jnp.where(lane_group == m, dzr[here, :], jnp.zeros((), BF16)) for m in range(per)]
            pairs = dot(jnp.concatenate(mine, axis=0), utr[:, TAPS * b : TAPS * (b + 2)], NN)
            for m in range(per):
                own = pairs[TAPS * m : TAPS * (m + 1)]
                term = jnp.where(lower_flipped, own[:, TAPS:], own[:, :TAPS]) * mp[b]
                products[m] = term if b == 0 else products[m] + term

    def multiply(m, slot):
        c = slice(GROUP * m, GROUP * (m + 1))
        band = bands[slot]
        near = [band * ml[b] for b in range(blocks)]
        far = [band * ml[blocks + b] for b in range(blocks + 1)]
        weights = jnp.concatenate(
            [jnp.concatenate([far[b], near[b]], axis=1) for b in range(blocks)], axis=0
        )
        both = jnp.concatenate([ut[c, TAPS * b : TAPS * (b + 2)] for b in range(blocks)], axis=0)
        result = dot(both, weights, NT)
        for b in range(blocks):
            here = slice(TAPS * b, TAPS * (b + 1))
            zt[c, here] = result[GROUP * b : GROUP * (b + 1), here]
        weights = jnp.concatenate(
            [jnp.concatenate([near[b], far[b + 1]], axis=0) for b in range(blocks)], axis=1
        )
        both = jnp.concatenate([dzt[c, TAPS * b : TAPS * (b + 2)] for b in range(blocks)], axis=0)
        result = dot(both, weights, NN)
        for b in range(blocks):
            here = slice(TAPS * b, TAPS * (b + 1))
            dut[c, here] = result[GROUP * b : GROUP * (b + 1), here]

    def edge_rows(rows_of, first, second, signal):
        left = [rows_of[16 * m : 16 * m + 16] * first for m in range(per)]
        right = [rows_of[16 * m : 16 * m + 16] * second for m in range(per)]
        left, right = jnp.concatenate(left, axis=0), jnp.concatenate(right, axis=0)
        result = dot(jnp.concatenate([left, right], axis=1), signal, NT)
        total = None
        for m in range(per):
            own = jnp.where(lane_group[:16] == m, result[16 * m : 16 * m + 16], 0.0)
            total = own if total is None else total + own
        return total

    def close(i):
        below = next_ref[i, LANES : LANES + 16, :].astype(F32)[EDGE:]
        window = slice(TAPS * blocks, TAPS * (blocks + 2))
        z2 = edge_rows(tops, ml[2 * blocks, 0:16], mn[0], ut[:, window])
        du2 = edge_rows(others, mn[1], mn[2], dzt[:, window])
        for b in range(blocks + 1):
            length = TAPS if b < blocks else EDGE
            here = slice(TAPS * b, TAPS * b + length)
            z = zt[:, here].T if b < blocks else z2[:EDGE]
            du = dut[:, here].T if b < blocks else du2[:EDGE]
            if b < blocks:
                dq[here, :] = bg[here, lanes_of(i)].astype(F32) * z
                conv = conv_late if b else conv_early
                dk[here, :] = du * conv[i, 1]
                dv[here, :] = du * conv[i, 0]
            else:
                dq[here, :] = below * z
            if b in (0, blocks):
                m = 0 if b == 0 else 1
                key, value = fixes[m, 0], fixes[m, 1]
                there = slice(TAPS * b, TAPS * b + EDGE)
                dk[there, :] = du[:EDGE] * value
                dv[there, :] = du[:EDGE] * key

    steps = per
    groups = count * per
    part = 32

    def finish_steps(i):
        arrays = ((dq, bq, oq_ref), (dk, bk, ok_ref), (dv, bv, ov_ref))
        lane = lanes_of(i)
        for n in range(3 * SHORT):
            tiles[groups + n] = jnp.zeros((8, LANES), F32)

        def one_part(m):
            for n, (grad, source, out) in enumerate(arrays):
                sums = [None] * SHORT
                for at in range(rows // steps // part):
                    low = rows // steps * m + part * at
                    x = source[pl.ds(low, part), lane].astype(F32)
                    total = None
                    for j in range(SHORT):
                        piece = grad[pl.ds(low + j, part), :]
                        if j:
                            piece = piece * mj[j - 1, pl.ds(low + frame + j, part), :]
                        scaled = w_ref[n, j : j + 1, lane] * piece
                        total = scaled if total is None else total + scaled
                        fresh = jnp.sum((x * piece).reshape(part // 8, 8, LANES), axis=0)
                        sums[j] = fresh if at == 0 else sums[j] + fresh
                    out[pl.ds(low, part), lane] = total.astype(BF16)
                for j in range(SHORT):
                    tiles[groups + SHORT * n + j] += sums[j]

        def close():
            for n in range(3 * SHORT):
                line = jnp.sum(tiles[groups + n], axis=0, keepdims=True) * short_scale
                part_ref[n : n + 1, lane] = line
            copy_all(outputs(i), out_sems, i)

        return one_part, close

    part_ref[3 * SHORT : 24, :] = jnp.zeros((24 - 3 * SHORT, part_ref.shape[1]), F32)

    def long_block(i, between):
        multiply_taps()
        for m in range(per):
            make_bands(i, m, m)
            multiply(m, m)
            sum_taps(i, m)
            between(m)

    arrive(0)
    start_wave(2)
    prepare(0)
    long_block(0, lambda m: None)
    close(0)
    arrive_halos(1)
    arrive(1)
    prepare(1)

    def both(i, carry):
        @pl.when(i == 2)
        def rest_arrives():
            arrive_halos(2)
            arrive(2)

        one_part, close_finish = finish_steps(i - 1)
        long_block(i, one_part)
        close_finish()
        close(i)
        prepare(jnp.minimum(i + 1, count - 1))
        return carry

    lax.fori_loop(1, count, both, 0)
    one_part, close_finish = finish_steps(count - 1)
    for m in range(per):
        one_part(m)
    close_finish()
    for i in range(count):
        lines = [jnp.sum(gl[per * i + n], axis=0, keepdims=True) for n in range(per)]
        here = slice(LANES * i, LANES * (i + 1))
        part_ref[24:32, here] = jnp.concatenate(lines, axis=0) * long_scale

    copy_all([(part_ref, part_hbm)], small_sems, 0)

    def drain(i, carry):
        copy_all(outputs(i), out_sems, i, wait=True)
        return carry

    lax.fori_loop(0, count, drain, 0)
    copy_all([(part_ref, part_hbm)], small_sems, 0, wait=True)


def mixer(operands, rows, channels, scales):
    blocks = rows // TAPS
    count = channels // LANES
    ids, short_filter = operands[0], operands[3]
    vm = lambda *shape: pltpu.VMEM(shape, F32)
    vb = lambda *shape: pltpu.VMEM(shape, BF16)
    out = jax.ShapeDtypeStruct((1, rows, channels), BF16)
    buffered = [vb(rows, channels)] * 4
    return pl.pallas_call(
        functools.partial(mixer_kernel, rows, *scales),
        in_specs=[HBM] * len(operands),
        out_specs=[HBM] * 4,
        out_shape=[out, out, out, jax.ShapeDtypeStruct((32, channels), F32)],
        scratch_shapes=[
            pltpu.VMEM(ids.shape, jnp.int32),
            vb(*operands[1].shape),
            vb(*operands[2].shape),
            vm(*short_filter.shape),
            vb(count, HEAD_ROWS, LANES),
            vb(count, HEAD_ROWS, LANES),
            *buffered,
            vb(count, HEAD_ROWS, LANES),
            vb(count, HEAD_ROWS, LANES),
            vm(count, 2, TAPS, LANES),
            vb(count, TAPS, LANES),
            vm(count, 2, TAPS, LANES),
            vb(count, TAPS, LANES),
            vb(count, LANES, TAPS),
            vb(count, LANES, TAPS),
            *buffered[:3],
            vm(32, channels),
            vm(channels // GROUP + 3 * SHORT, 8, TAPS),
            vm(8, LANES),
            vm(3 * rows, LANES),
            vm(SHORT - 1, 3 * rows, LANES),
            vb(2 * blocks + 1, TAPS, TAPS),
            vb(3, 16, TAPS),
            vm(blocks, TAPS, TAPS),
            vb(TAPS, TAPS),
            vm(3, 2, 2 * EDGE, LANES),
            vb(LANES, rows + 2 * TAPS),
            vb(LANES, rows + TAPS),
            vb(LANES, rows + 2 * TAPS),
            vb(rows, LANES),
            vm(LANES, rows + TAPS),
            vm(LANES, rows + TAPS),
            vm(rows + 16, LANES),
            vm(rows + 16, LANES),
            vm(rows + 16, LANES),
            vm(channels // GROUP, 8, TAPS),
            vm(2, 2, EDGE, LANES),
            vb(LANES // GROUP, TAPS, TAPS),
            vb(LANES, TAPS),
            vb(LANES, TAPS),
            vm(LANES // GROUP, TAPS, TAPS),
            pltpu.SemaphoreType.DMA((1, 4)),
            pltpu.SemaphoreType.DMA((3, 4)),
            pltpu.SemaphoreType.DMA((3, 10)),
            pltpu.SemaphoreType.DMA((count, 3)),
        ],
        compiler_params=pltpu.CompilerParams(vmem_limit_bytes=63 << 20),
        name="mixer",
    )(*operands)


AXES = ("fsdp", "ctx")


def exchanged(x, bits):
    size = lax.axis_size(AXES)
    return lax.ppermute(x, AXES, [(i, i ^ bits) for i in range(size)]).astype(F32)


def sum_pair(x):
    return x + exchanged(x, 1)


def sum_rest(x):
    size = lax.axis_size(AXES)
    bit = 2
    while bit < size:
        sent = x.astype(BF16)
        x = sent.astype(F32) + exchanged(sent, bit)
        if 2 * bit < size:
            x = x + (exchanged(sent, 2 * bit) + exchanged(sent, 3 * bit))
        bit *= 4
    return x


def tap_halves(long_filter):
    if lax.axis_size("fsdp") == 2:
        return long_filter, lax.ppermute(long_filter, "fsdp", [(0, 1), (1, 0)])
    filters = lax.all_gather(long_filter, "fsdp", axis=1, tiled=True)
    return filters[:, : TAPS // 2], filters[:, TAPS // 2 :]


def body(q_in, k_in, v_in, grad_out, genome_ids, long_filter, short_filter):
    rows, channels = q_in.shape[1:]
    seq_count = lax.axis_size("fsdp")
    length = rows * lax.axis_size("ctx")
    halves = tap_halves(long_filter)
    groups = long_filter.shape[0]
    arrays = (genome_ids, short_filter, q_in, k_in, v_in, grad_out)
    conv_late, dzr_early, sent_near, sent_far = half_part(True, *arrays)
    near, far = swapped(sent_near, sent_far, "ctx")
    sent_near, sent_far, genome_ids = lax.optimization_barrier((sent_near, sent_far, genome_ids))
    conv_early, dzr_late, u_early, dz_late = half_part(False, genome_ids, *arrays[1:])
    scales = (
        1.0 / math.sqrt(seq_count * length * (channels // groups)),
        1.0 / math.sqrt(seq_count * length),
    )
    operands = (
        genome_ids, *halves, short_filter, near, far, q_in, k_in, v_in, grad_out,
        sent_near, sent_far, conv_late, dzr_early, conv_early, dzr_late, u_early, dz_late,
    )
    out_q, out_k, out_v, sums = mixer(operands, rows, channels, scales)
    power = lax.axis_size(AXES)
    if power & (power - 1):
        sums = lax.psum(sums, AXES)
    else:
        sums = sum_rest(sum_pair(sums))
    grad_short = sums[: 3 * SHORT].reshape(3, SHORT, channels)
    grad_long = sums[24:].reshape(8, channels // LANES, LANES).transpose(1, 0, 2)
    grad_long = grad_long.reshape(groups, TAPS)
    own = TAPS // seq_count
    grad_long = lax.dynamic_slice_in_dim(grad_long, lax.axis_index("fsdp") * own, own, 1)
    return out_q, out_k, out_v, grad_long, grad_short


def solution(mesh):
    return jax.shard_map(
        body,
        mesh=mesh,
        in_specs=(
            P("fsdp", "ctx", "tp"),
            P("fsdp", "ctx", "tp"),
            P("fsdp", "ctx", "tp"),
            P("fsdp", "ctx", "tp"),
            P("fsdp", "ctx"),
            P("tp", "fsdp"),
            P(None, None, "tp"),
        ),
        out_specs=(
            P("fsdp", "ctx", "tp"),
            P("fsdp", "ctx", "tp"),
            P("fsdp", "ctx", "tp"),
            P("tp", "fsdp"),
            P(None, None, "tp"),
        ),
        check_vma=False,
    )
```

```python
import functools
import math

import jax
import jax.numpy as jnp
from jax import lax
from jax.experimental import pallas as pl
from jax.experimental.pallas import tpu as pltpu
from jax.sharding import PartitionSpec as P

TAPS = 128
SHORT = 7
LANES = 128
GROUP = 16
EDGE = 8
VMEM_LIMIT = 65300 << 10
HEAD_ROWS = LANES + 32
F32 = jnp.float32
BF16 = jnp.bfloat16
NT = (((1,), (1,)), ((), ()))
NN = (((1,), (0,)), ((), ()))
VMEM = pl.BlockSpec(memory_space=pltpu.VMEM)
HBM = pl.BlockSpec(memory_space=pltpu.HBM)


def swapped(near, far, axis):
    size = lax.axis_size(axis)
    near_route = [(i, i ^ 1) for i in range(size) if i ^ 1 < size]
    far_route = [(i + 1, i) for i in range(1, size - 1, 2)]
    far_route = far_route + [(i, j) for j, i in far_route]
    return lax.ppermute(near, axis, near_route), lax.ppermute(far, axis, far_route)


def dot(a, b, dims):
    return lax.dot_general(a, b, dims, preferred_element_type=F32)


def lanes_of(i):
    return pl.ds(pl.multiple_of(i * LANES, LANES), LANES)


def spread(line):
    return jnp.broadcast_to(line, (TAPS, TAPS)).T


def copy_all(pairs, sems, i, wait=False):
    for n, (source, target) in enumerate(pairs):
        copy = pltpu.make_async_copy(source, target, sems.at[i, n])
        if wait:
            copy.wait()
        else:
            copy.start()


def half_kernel(
    rows,
    edge,
    ids_hbm,
    w_hbm,
    q_hbm,
    k_hbm,
    v_hbm,
    g_hbm,
    conv_hbm,
    dzr_hbm,
    one_hbm,
    two_hbm,
    ids_ref,
    w_ref,
    bq,
    bk,
    bv,
    bg,
    conv_ref,
    dzr_ref,
    one_ref,
    two_ref,
    idc,
    mj,
    xq,
    xk,
    xv,
    uf,
    dzf,
    small_sems,
    in_sems,
    out_sems,
    packet_sems,
    border_sems,
):
    count = q_hbm.shape[2] // LANES
    odd = lax.rem(lax.axis_index("ctx"), 2)
    kv_low, q_low = (TAPS, 0) if edge else (0, TAPS)
    lead = 16

    def small():
        return ((ids_hbm, ids_ref), (w_hbm, w_ref))

    def rows_from(low, before):
        start = low - before if low else 0
        return pl.ds(start, rows - start if low else TAPS + lead)

    def inputs(half):
        lane = pl.ds(pl.multiple_of(2 * LANES * half, 2 * LANES), 2 * LANES)
        spans = (
            (q_hbm, bq, rows_from(q_low, lead)),
            (k_hbm, bk, rows_from(kv_low, lead)),
            (v_hbm, bv, rows_from(kv_low, lead)),
            (g_hbm, bg, rows_from(q_low, 0)),
        )
        return [(a.at[0, span, lane], b.at[span, lane]) for a, b, span in spans]

    def borders():
        first, last = pl.ds(0, 16), pl.ds(rows - 16, 16)
        spans = ((k_hbm, bk, first), (v_hbm, bv, first), (q_hbm, bq, last))
        return [(a.at[0, span], b.at[span]) for a, b, span in spans]

    def outputs(half):
        span = pl.ds(2 * half, 2)
        pairs = [(conv_ref, conv_hbm), (dzr_ref, dzr_hbm)]
        return [(a.at[span], b.at[span]) for a, b in pairs]

    def packets(half):
        span = pl.ds(2 * half, 2)
        one, two = one_ref.at[span], two_ref.at[span]
        near, far = one_hbm.at[span], two_hbm.at[span]
        return ((one, near), (two, far)), ((two, near), (one, far))

    def send_packets(i):
        if not edge:
            copy_all(packets(i)[0], packet_sems, i)
            return

        @pl.when(odd == 0)
        def even_packets():
            copy_all(packets(i)[0], packet_sems, i)

        @pl.when(odd == 1)
        def odd_packets():
            copy_all(packets(i)[1], packet_sems, i)

    copy_all(small(), small_sems, 0)

    def fetch(i, carry):
        copy_all(inputs(i), in_sems, i)
        return carry

    lax.fori_loop(0, count // 2, fetch, 0)
    if edge:
        copy_all(borders(), border_sems, 0)
    copy_all(small(), small_sems, 0, wait=True)
    ids = (ids_ref[...] + 1).astype(F32)
    idc[0:EDGE] = jnp.zeros((EDGE, LANES), F32)
    for b in range(2):
        idc[EDGE + TAPS * b : EDGE + TAPS * (b + 1)] = spread(ids[:, TAPS * b : TAPS * (b + 1)])
    for x in (xq, xk, xv):
        x[:, 0:lead] = jnp.zeros((2, lead, LANES), F32)

    def masks(i, carry):
        base = pl.multiple_of(16 * i, 16)
        here = idc[pl.ds(base + EDGE, 16), :]
        for j in range(1, SHORT):
            mj[j - 1, pl.ds(base, 16), :] = (here == idc[pl.ds(base + EDGE - j, 16), :]).astype(F32)
        return carry

    lax.fori_loop(0, rows // 16, masks, 0)
    pad = jnp.zeros((EDGE - 2, LANES), F32)
    id_rows = [ids[:, TAPS * b : TAPS * (b + 1)] for b in range(2)]
    id_tile = jnp.concatenate(id_rows + [pad], axis=0)
    id_late = jnp.concatenate([pad] + id_rows, axis=0)
    sub = lax.broadcasted_iota(jnp.int32, (EDGE, LANES), 0)
    part = 32

    def pair(a, b):
        return jnp.concatenate([a, b], axis=0).astype(BF16)

    def filtered(x, h, taps, low, at, size):
        total = taps[0] * x[h, pl.ds(at + lead, size), :]
        for j in range(1, SHORT):
            mask = mj[j - 1, pl.ds(at + low, size), :]
            total += taps[j] * (mask * x[h, pl.ds(at + lead - j, size), :])
        return total

    def two_blocks(half, carry):
        pair_of = [2 * half, 2 * half + 1]
        copy_all(inputs(half), in_sems, half, wait=True)
        for h, i in enumerate(pair_of):
            lane = lanes_of(i)
            for x, source, low in ((xq, bq, q_low), (xk, bk, kv_low), (xv, bv, kv_low)):
                if low:
                    x[h, 0:lead] = source[low - lead : low, lane].astype(F32)
                size = TAPS if low else TAPS + lead
                x[h, lead : lead + size] = source[low : low + size, lane].astype(F32)

        def taps_of(n, i):
            return [w_ref[n, j : j + 1, lanes_of(i)] for j in range(SHORT)]

        def convolve(n, inner):
            at = pl.multiple_of(part * n, part)
            for h, i in enumerate(pair_of):
                key = filtered(xk, h, taps_of(1, i), kv_low, at, part)
                value = filtered(xv, h, taps_of(2, i), kv_low, at, part)
                query = filtered(xq, h, taps_of(0, i), q_low, at, part)
                conv_ref[i, 0, pl.ds(at, part), :] = key
                conv_ref[i, 1, pl.ds(at, part), :] = value
                uf[h, pl.ds(at, part), :] = key * value
                dz = bg[pl.ds(at + q_low, part), lanes_of(i)].astype(F32) * query
                dzf[h, pl.ds(at, part), :] = dz
                dzr_ref[i, pl.ds(at, part), :] = dz.astype(BF16)
            return inner

        lax.fori_loop(0, TAPS // part, convolve, 0)
        for h, i in enumerate(pair_of):
            one_ref[i, 0:LANES, :] = uf[h].T.astype(BF16)
            two_ref[i, 0:LANES, :] = dzf[h].T.astype(BF16)
            if edge:
                lane = lanes_of(i)
                beyond = bg[TAPS : TAPS + 16, lane].astype(F32)[:EDGE]
                beyond = beyond * filtered(xq, h, taps_of(0, i), q_low, TAPS, EDGE)
                last = slice(lead + TAPS - EDGE, lead + TAPS)
                q_last = bq[rows - 16 : rows, lane].astype(F32)[EDGE:]
                k_first = bk[0:16, lane].astype(F32)[:EDGE]
                v_first = bv[0:16, lane].astype(F32)[:EDGE]
                g_first = bg[0:16, lane].astype(F32)[:EDGE]
                q_first = xq[h, lead : lead + EDGE, :]
                one_ref[i, LANES : LANES + 16, :] = pair(xk[h, last, :], xv[h, last, :])
                one_ref[i, LANES + 16 : LANES + 32, :] = pair(q_last, id_tile)
                late = sub >= EDGE - 2
                q_first = jnp.where(late, id_late, q_first)
                g_first = jnp.where(late, pltpu.roll(beyond, 6, 0), g_first)
                k_first = jnp.where(late, pltpu.roll(beyond, 4, 0), k_first)
                v_first = jnp.where(late, pltpu.roll(beyond, 2, 0), v_first)
                two_ref[i, LANES : LANES + 16, :] = pair(q_first, g_first)
                two_ref[i, LANES + 16 : LANES + 32, :] = pair(k_first, v_first)
        send_packets(half)
        copy_all(outputs(half), out_sems, half)
        return carry

    if edge:
        copy_all(borders(), border_sems, 0, wait=True)
    lax.fori_loop(0, count // 2, two_blocks, 0)

    def drain(i, carry):
        copy_all(packets(i)[0], packet_sems, i, wait=True)
        copy_all(outputs(i), out_sems, i, wait=True)
        return carry

    lax.fori_loop(0, count // 2, drain, 0)


def half_part(edge, ids, short_filter, q_in, k_in, v_in, grad_out):
    rows, channels = q_in.shape[1:]
    count = channels // LANES
    vm = lambda *shape: pltpu.VMEM(shape, F32)
    vb = lambda *shape: pltpu.VMEM(shape, BF16)
    packet = (count, HEAD_ROWS if edge else LANES, LANES)
    results = (
        ((count, 2, TAPS, LANES), F32),
        ((count, TAPS, LANES), BF16),
        (packet, BF16),
        (packet, BF16),
    )
    return pl.pallas_call(
        functools.partial(half_kernel, rows, edge),
        in_specs=[HBM] * 6,
        out_specs=[HBM] * 4,
        out_shape=[jax.ShapeDtypeStruct(*r) for r in results],
        scratch_shapes=[
            pltpu.VMEM(ids.shape, jnp.int32),
            vm(*short_filter.shape),
            *[vb(rows, channels)] * 4,
            *[pltpu.VMEM(*r) for r in results],
            vm(rows + EDGE, LANES),
            vm(SHORT - 1, rows, LANES),
            *[vm(2, TAPS + 32, LANES)] * 3,
            vm(2, TAPS, LANES),
            vm(2, TAPS, LANES),
            pltpu.SemaphoreType.DMA((1, 2)),
            pltpu.SemaphoreType.DMA((count // 2, 4)),
            pltpu.SemaphoreType.DMA((count // 2, 2)),
            pltpu.SemaphoreType.DMA((count // 2, 2)),
            pltpu.SemaphoreType.DMA((1, 3)),
        ],
        compiler_params=pltpu.CompilerParams(vmem_limit_bytes=VMEM_LIMIT),
        cost_estimate=pl.CostEstimate(
            flops=8_000_000_000, bytes_accessed=16_000_000, transcendentals=0
        ),
        name="edge_half" if edge else "other_half",
    )(ids, short_filter, q_in, k_in, v_in, grad_out)


def mixer_kernel(
    rows,
    long_scale,
    short_scale,
    ids_hbm,
    one_half_hbm,
    other_half_hbm,
    w_hbm,
    near_hbm,
    far_hbm,
    q_hbm,
    k_hbm,
    v_hbm,
    g_hbm,
    sent_near_hbm,
    sent_far_hbm,
    conv_late_hbm,
    dzr_early_hbm,
    conv_early_hbm,
    dzr_late_hbm,
    u_early_hbm,
    dz_late_hbm,
    oq_hbm,
    ok_hbm,
    ov_hbm,
    part_hbm,
    ids_ref,
    one_half,
    other_half,
    w_ref,
    prev_ref,
    next_ref,
    bq,
    bk,
    bv,
    bg,
    tail_ref,
    head_ref,
    conv_late,
    dzr_early,
    conv_early,
    dzr_late,
    u_early,
    dz_late,
    oq_ref,
    ok_ref,
    ov_ref,
    part_ref,
    tiles,
    idr,
    idc,
    mj,
    ml,
    mn,
    mp,
    flip,
    edges,
    ut,
    utr,
    dzt,
    dzr,
    zt,
    dut,
    dq,
    dk,
    dv,
    gl,
    fixes,
    bands,
    others,
    tops,
    products,
    small_sems,
    halo_sems,
    in_sems,
    out_sems,
):
    blocks = rows // TAPS
    frame = rows
    count = q_hbm.shape[2] // LANES
    per = LANES // GROUP
    odd = lax.rem(lax.axis_index("ctx"), 2)

    def small():
        return (
            (ids_hbm, ids_ref),
            (one_half_hbm, one_half),
            (other_half_hbm, other_half),
            (w_hbm, w_ref),
        )

    waves = ((0, 1), (1, 2), (3, count - 3))

    def halos(wave):
        span = pl.ds(*waves[wave])
        far, near = far_hbm.at[span], near_hbm.at[span]
        prev, succ = prev_ref.at[span], next_ref.at[span]
        sent_far, sent_near = sent_far_hbm.at[span], sent_near_hbm.at[span]
        tail, head = tail_ref.at[span], head_ref.at[span]
        return (
            ((far, prev), (near, succ), (sent_near, tail), (sent_far, head)),
            ((near, prev), (far, succ), (sent_far, tail), (sent_near, head)),
        )

    def inputs(wave):
        start, size = waves[wave]
        span = pl.ds(start, size)
        lane = pl.ds(start * LANES, size * LANES)
        pairs = ((q_hbm, bq), (k_hbm, bk), (v_hbm, bv), (g_hbm, bg))
        pairs = [(a.at[0, :, lane], b.at[:, lane]) for a, b in pairs]
        more = (
            (conv_late_hbm, conv_late),
            (dzr_early_hbm, dzr_early),
            (conv_early_hbm, conv_early),
            (dzr_late_hbm, dzr_late),
            (u_early_hbm, u_early),
            (dz_late_hbm, dz_late),
        )
        return [(a.at[span], b.at[span]) for a, b in more] + pairs

    def outputs(i):
        lane = lanes_of(i)
        pairs = ((oq_ref, oq_hbm), (ok_ref, ok_hbm), (ov_ref, ov_hbm))
        return [(a.at[:, lane], b.at[0, :, lane]) for a, b in pairs]

    def start_wave(wave):
        @pl.when(odd == 0)
        def even_halos():
            copy_all(halos(wave)[0], halo_sems, wave)

        @pl.when(odd == 1)
        def odd_halos():
            copy_all(halos(wave)[1], halo_sems, wave)

        copy_all(inputs(wave), in_sems, wave)

    def arrive_halos(wave):
        copy_all(halos(wave)[0], halo_sems, wave, wait=True)

    def arrive(wave):
        copy_all(inputs(wave), in_sems, wave, wait=True)

    copy_all(small(), small_sems, 0)
    start_wave(0)
    copy_all(small(), small_sems, 0, wait=True)
    arrive_halos(0)
    start_wave(1)

    row = lax.broadcasted_iota(jnp.int32, (TAPS, TAPS), 0)
    col = lax.broadcasted_iota(jnp.int32, (TAPS, TAPS), 1)
    own_ids = (ids_ref[...] + 1).astype(F32)
    prev_ids = prev_ref[0, LANES + 16 : LANES + 32, :].astype(F32)
    next_ids = next_ref[0, LANES : LANES + 16, :].astype(F32)
    for b in range(blocks):
        idr[b : b + 1, :] = prev_ids[EDGE + b : EDGE + b + 1]
        idr[blocks + b : blocks + b + 1, :] = own_ids[:, TAPS * b : TAPS * (b + 1)]
        idr[2 * blocks + b : 2 * blocks + b + 1, :] = next_ids[EDGE - blocks + b : EDGE - blocks + b + 1]
    for b in range(3 * blocks):
        idc[TAPS * b : TAPS * (b + 1), :] = spread(idr[b : b + 1, :])

    def short_masks(i, carry):
        base = pl.multiple_of(frame + EDGE * i, EDGE)
        here = idc[pl.ds(base, EDGE), :]
        for j in range(1, SHORT):
            mj[j - 1, pl.ds(base, EDGE), :] = (here == idc[pl.ds(base - j, EDGE), :]).astype(F32)
        return carry

    lax.fori_loop(0, (rows + 2 * EDGE) // EDGE, short_masks, 0)

    def same(t_block, s_block, length):
        start = frame + TAPS * t_block
        line = idr[blocks + s_block : blocks + s_block + 1, :]
        return (idc[start : start + length, :] == line).astype(F32)

    lower = (row >= col).astype(F32)
    upper = 1.0 - lower
    flip[...] = (row + col == TAPS - 1).astype(BF16)
    for b in range(blocks):
        ml[b] = (same(b, b, TAPS) * lower).astype(BF16)
    for b in range(blocks + 1):
        ml[blocks + b] = (same(b, b - 1, TAPS) * upper).astype(BF16)
    mn[0] = (same(blocks, blocks, 16) * lower[:16]).astype(BF16)
    mn[1] = (same(blocks, blocks, 16) * (row <= col).astype(F32)[:16]).astype(BF16)
    mn[2] = (same(blocks, blocks + 1, 16) * (row > col).astype(F32)[:16]).astype(BF16)
    for b in range(blocks):
        both = same(b, b, TAPS) * lower + same(b, b - 1, TAPS) * upper
        mp[b] = dot(both.astype(BF16), flip[...], NN)
    negated = jnp.logical_or(row + col == TAPS, row + col == 0).astype(BF16)
    first, second = one_half[...].astype(F32), other_half[...].astype(F32)
    if lax.axis_size("fsdp") == 2:
        mine = lax.axis_index("fsdp") == 0
        first, second = jnp.where(mine, first, second), jnp.where(mine, second, first)
    forward_taps = jnp.concatenate([first, second], axis=1)
    reversed_taps = dot(forward_taps.astype(BF16), negated, NN)
    for i in range(count * per):
        tiles[i, 0:1, :] = reversed_taps[i : i + 1]
        tiles[i, 1:2, :] = forward_taps[i : i + 1]

    lane_group = col // GROUP
    lower_flipped = row + col >= TAPS - 1
    first_lanes = col < EDGE
    next_lanes = col < SHORT - 1
    sub = lax.broadcasted_iota(jnp.int32, (EDGE, LANES), 0)
    blank = jnp.zeros((TAPS - EDGE, LANES), F32)

    def turned(x):
        return jnp.concatenate([x, blank], axis=0).T.astype(BF16)

    def filters_of(i):
        return [[w_ref[n, j : j + 1, lanes_of(i)] for j in range(SHORT)] for n in range(3)]

    def prepare(i):
        w = filters_of(i)
        prev_kv = prev_ref[i, LANES : LANES + 16, :].astype(F32)
        prev_q = prev_ref[i, LANES + 16 : LANES + 32, :].astype(F32)
        next_qg = next_ref[i, LANES : LANES + 16, :].astype(F32)
        next_kv = next_ref[i, LANES + 16 : LANES + 32, :].astype(F32)
        next_dz = jnp.where(
            sub < 2,
            pltpu.roll(next_qg[EDGE:], 2, 0),
            jnp.where(
                sub < 4,
                pltpu.roll(next_kv[:EDGE], 4, 0),
                jnp.where(sub < 5, pltpu.roll(next_kv[EDGE:], 6, 0), 0.0),
            ),
        )
        for n, (source, before, after) in enumerate(
            (
                (bq, prev_q[:EDGE], next_qg[:EDGE]),
                (bk, prev_kv[:EDGE], next_kv[:EDGE]),
                (bv, prev_kv[EDGE:], next_kv[EDGE:]),
            )
        ):
            edges[n, 0, 0:EDGE] = before
            edges[n, 0, EDGE : 2 * EDGE] = source[0:16, lanes_of(i)].astype(F32)[:EDGE]
            edges[n, 1, 0:EDGE] = source[rows - 16 : rows, lanes_of(i)].astype(F32)[EDGE:]
            edges[n, 1, EDGE : 2 * EDGE] = after

        def convolve(n, m):
            low = frame + rows * m
            total = w[n][0] * edges[n, m, EDGE : 2 * EDGE]
            for j in range(1, SHORT):
                mask = mj[j - 1, low : low + EDGE, :]
                total += w[n][j] * (mask * edges[n, m, EDGE - j : 2 * EDGE - j])
            return total

        upstream = (bg[0:16, lanes_of(i)].astype(F32)[:EDGE], next_qg[EDGE:])
        fixed = []
        for m in range(2):
            query, key, value = [convolve(n, m) for n in range(3)]
            fixed.append((key, value, key * value, upstream[m] * query))

        ut[:, 0:TAPS] = prev_ref[i, 0:LANES, :]
        ut[:, TAPS : 2 * TAPS] = jnp.where(first_lanes, turned(fixed[0][2]), u_early[i])
        ut[:, 2 * TAPS : 3 * TAPS] = tail_ref[i, 0:LANES, :]
        ut[:, 3 * TAPS :] = turned(fixed[1][2])
        dzt[:, 0:TAPS] = jnp.where(first_lanes, turned(fixed[0][3]), head_ref[i, 0:LANES, :])
        dzt[:, TAPS : 2 * TAPS] = dz_late[i]
        dzt[:, 2 * TAPS : 3 * TAPS] = jnp.where(
            next_lanes, turned(fixed[1][3]), next_ref[i, 0:LANES, :]
        )
        dzt[:, 3 * TAPS :] = turned(next_dz[:EDGE])
        dzr[0:TAPS] = dzr_early[i]
        dzr[TAPS:] = dzr_late[i]
        rest = dzr_early[i, 0:16, :].astype(F32)[EDGE:]
        dzr[0:16] = jnp.concatenate([fixed[0][3], rest], axis=0).astype(BF16)
        for b in range(blocks + 1):
            here = slice(TAPS * b, TAPS * (b + 1))
            utr[:, here] = dot(ut[:, here], flip[...], NN).astype(BF16)

        for m in range(2):
            for n in range(2):
                fixes[m, n] = fixed[m][n]

    def make_bands(i, m, slot):
        if True:
            g = per * i + m
            base = pltpu.roll(jnp.broadcast_to(tiles[g, 0:1, :], (16, TAPS)), 0, 1, stride=1, stride_axis=0)
            base = base.astype(BF16)
            bands[slot, 0:16] = base
            for r in range(16, TAPS, 16):
                bands[slot, r : r + 16] = pltpu.roll(base, r, 1)
            tops[16 * m : 16 * m + 16] = base
            line = jnp.broadcast_to(tiles[g, 1:2, :], (16, TAPS))
            line = pltpu.roll(line, 0, 1, stride=1, stride_axis=0).astype(BF16)
            others[16 * m : 16 * m + 16] = line

    def sum_taps(i, m):
        skewed = pltpu.roll(products[m], 1, 1, stride=1, stride_axis=0)
        gl[per * i + m] = jnp.sum(skewed.reshape(TAPS // 8, 8, TAPS), axis=0)

    def multiply_taps():
        for b in range(blocks):
            here = slice(TAPS * b, TAPS * (b + 1))
            mine = [jnp.where(lane_group == m, dzr[here, :], jnp.zeros((), BF16)) for m in range(per)]
            pairs = dot(jnp.concatenate(mine, axis=0), utr[:, TAPS * b : TAPS * (b + 2)], NN)
            for m in range(per):
                own = pairs[TAPS * m : TAPS * (m + 1)]
                term = jnp.where(lower_flipped, own[:, TAPS:], own[:, :TAPS]) * mp[b]
                products[m] = term if b == 0 else products[m] + term

    def multiply(m, slot):
        c = slice(GROUP * m, GROUP * (m + 1))
        band = bands[slot]
        near = [band * ml[b] for b in range(blocks)]
        far = [band * ml[blocks + b] for b in range(blocks + 1)]
        weights = jnp.concatenate(
            [jnp.concatenate([far[b], near[b]], axis=1) for b in range(blocks)], axis=0
        )
        both = jnp.concatenate([ut[c, TAPS * b : TAPS * (b + 2)] for b in range(blocks)], axis=0)
        result = dot(both, weights, NT)
        for b in range(blocks):
            here = slice(TAPS * b, TAPS * (b + 1))
            zt[c, here] = result[GROUP * b : GROUP * (b + 1), here]
        weights = jnp.concatenate(
            [jnp.concatenate([near[b], far[b + 1]], axis=0) for b in range(blocks)], axis=1
        )
        both = jnp.concatenate([dzt[c, TAPS * b : TAPS * (b + 2)] for b in range(blocks)], axis=0)
        result = dot(both, weights, NN)
        for b in range(blocks):
            here = slice(TAPS * b, TAPS * (b + 1))
            dut[c, here] = result[GROUP * b : GROUP * (b + 1), here]

    def edge_rows(rows_of, first, second, signal):
        left = [rows_of[16 * m : 16 * m + 16] * first for m in range(per)]
        right = [rows_of[16 * m : 16 * m + 16] * second for m in range(per)]
        left, right = jnp.concatenate(left, axis=0), jnp.concatenate(right, axis=0)
        result = dot(jnp.concatenate([left, right], axis=1), signal, NT)
        total = None
        for m in range(per):
            own = jnp.where(lane_group[:16] == m, result[16 * m : 16 * m + 16], 0.0)
            total = own if total is None else total + own
        return total

    def close(i):
        below = next_ref[i, LANES : LANES + 16, :].astype(F32)[EDGE:]
        window = slice(TAPS * blocks, TAPS * (blocks + 2))
        z2 = edge_rows(tops, ml[2 * blocks, 0:16], mn[0], ut[:, window])
        du2 = edge_rows(others, mn[1], mn[2], dzt[:, window])
        for b in range(blocks + 1):
            length = TAPS if b < blocks else EDGE
            here = slice(TAPS * b, TAPS * b + length)
            z = zt[:, here].T if b < blocks else z2[:EDGE]
            du = dut[:, here].T if b < blocks else du2[:EDGE]
            if b < blocks:
                dq[here, :] = bg[here, lanes_of(i)].astype(F32) * z
                conv = conv_late if b else conv_early
                dk[here, :] = du * conv[i, 1]
                dv[here, :] = du * conv[i, 0]
            else:
                dq[here, :] = below * z
            if b in (0, blocks):
                m = 0 if b == 0 else 1
                key, value = fixes[m, 0], fixes[m, 1]
                there = slice(TAPS * b, TAPS * b + EDGE)
                dk[there, :] = du[:EDGE] * value
                dv[there, :] = du[:EDGE] * key

    steps = per
    groups = count * per
    part = 32

    def finish_steps(i):
        arrays = ((dq, bq, oq_ref), (dk, bk, ok_ref), (dv, bv, ov_ref))
        lane = lanes_of(i)
        for n in range(3 * SHORT):
            tiles[groups + n] = jnp.zeros((8, LANES), F32)

        def one_part(m):
            for n, (grad, source, out) in enumerate(arrays):
                sums = [None] * SHORT
                for at in range(rows // steps // part):
                    low = rows // steps * m + part * at
                    x = source[pl.ds(low, part), lane].astype(F32)
                    total = None
                    for j in range(SHORT):
                        piece = grad[pl.ds(low + j, part), :]
                        if j:
                            piece = piece * mj[j - 1, pl.ds(low + frame + j, part), :]
                        scaled = w_ref[n, j : j + 1, lane] * piece
                        total = scaled if total is None else total + scaled
                        fresh = jnp.sum((x * piece).reshape(part // 8, 8, LANES), axis=0)
                        sums[j] = fresh if at == 0 else sums[j] + fresh
                    out[pl.ds(low, part), lane] = total.astype(BF16)
                for j in range(SHORT):
                    tiles[groups + SHORT * n + j] += sums[j]

        def close():
            for n in range(3 * SHORT):
                line = jnp.sum(tiles[groups + n], axis=0, keepdims=True) * short_scale
                part_ref[n : n + 1, lane] = line
            copy_all(outputs(i), out_sems, i)

        return one_part, close

    part_ref[3 * SHORT : 24, :] = jnp.zeros((24 - 3 * SHORT, part_ref.shape[1]), F32)

    def long_block(i, between):
        multiply_taps()
        for m in range(per):
            make_bands(i, m, m)
            multiply(m, m)
            sum_taps(i, m)
            between(m)

    arrive(0)
    start_wave(2)
    prepare(0)
    long_block(0, lambda m: None)
    close(0)
    arrive_halos(1)
    arrive(1)
    prepare(1)

    def both(i, carry):
        @pl.when(i == 2)
        def rest_arrives():
            arrive_halos(2)
            arrive(2)

        one_part, close_finish = finish_steps(i - 1)
        long_block(i, one_part)
        close_finish()
        close(i)
        prepare(jnp.minimum(i + 1, count - 1))
        return carry

    lax.fori_loop(1, count, both, 0)
    one_part, close_finish = finish_steps(count - 1)
    for m in range(per):
        one_part(m)
    close_finish()
    for i in range(count):
        lines = [jnp.sum(gl[per * i + n], axis=0, keepdims=True) for n in range(per)]
        here = slice(LANES * i, LANES * (i + 1))
        part_ref[24:32, here] = jnp.concatenate(lines, axis=0) * long_scale

    copy_all([(part_ref, part_hbm)], small_sems, 0)

    def drain(i, carry):
        copy_all(outputs(i), out_sems, i, wait=True)
        return carry

    lax.fori_loop(0, count, drain, 0)
    copy_all([(part_ref, part_hbm)], small_sems, 0, wait=True)


def mixer(operands, rows, channels, scales):
    blocks = rows // TAPS
    count = channels // LANES
    ids, short_filter = operands[0], operands[3]
    vm = lambda *shape: pltpu.VMEM(shape, F32)
    vb = lambda *shape: pltpu.VMEM(shape, BF16)
    out = jax.ShapeDtypeStruct((1, rows, channels), BF16)
    buffered = [vb(rows, channels)] * 4
    return pl.pallas_call(
        functools.partial(mixer_kernel, rows, *scales),
        in_specs=[HBM] * len(operands),
        out_specs=[HBM] * 4,
        out_shape=[out, out, out, jax.ShapeDtypeStruct((32, channels), F32)],
        scratch_shapes=[
            pltpu.VMEM(ids.shape, jnp.int32),
            vb(*operands[1].shape),
            vb(*operands[2].shape),
            vm(*short_filter.shape),
            vb(count, HEAD_ROWS, LANES),
            vb(count, HEAD_ROWS, LANES),
            *buffered,
            vb(count, HEAD_ROWS, LANES),
            vb(count, HEAD_ROWS, LANES),
            vm(count, 2, TAPS, LANES),
            vb(count, TAPS, LANES),
            vm(count, 2, TAPS, LANES),
            vb(count, TAPS, LANES),
            vb(count, LANES, TAPS),
            vb(count, LANES, TAPS),
            *buffered[:3],
            vm(32, channels),
            vm(channels // GROUP + 3 * SHORT, 8, TAPS),
            vm(8, LANES),
            vm(3 * rows, LANES),
            vm(SHORT - 1, 3 * rows, LANES),
            vb(2 * blocks + 1, TAPS, TAPS),
            vb(3, 16, TAPS),
            vm(blocks, TAPS, TAPS),
            vb(TAPS, TAPS),
            vm(3, 2, 2 * EDGE, LANES),
            vb(LANES, rows + 2 * TAPS),
            vb(LANES, rows + TAPS),
            vb(LANES, rows + 2 * TAPS),
            vb(rows, LANES),
            vm(LANES, rows + TAPS),
            vm(LANES, rows + TAPS),
            vm(rows + 16, LANES),
            vm(rows + 16, LANES),
            vm(rows + 16, LANES),
            vm(channels // GROUP, 8, TAPS),
            vm(2, 2, EDGE, LANES),
            vb(LANES // GROUP, TAPS, TAPS),
            vb(LANES, TAPS),
            vb(LANES, TAPS),
            vm(LANES // GROUP, TAPS, TAPS),
            pltpu.SemaphoreType.DMA((1, 4)),
            pltpu.SemaphoreType.DMA((3, 4)),
            pltpu.SemaphoreType.DMA((3, 10)),
            pltpu.SemaphoreType.DMA((count, 3)),
        ],
        compiler_params=pltpu.CompilerParams(vmem_limit_bytes=63 << 20),
        name="mixer",
    )(*operands)


AXES = ("fsdp", "ctx")


def exchanged(x, bits):
    size = lax.axis_size(AXES)
    return lax.ppermute(x, AXES, [(i, i ^ bits) for i in range(size)]).astype(F32)


def sum_pair(x):
    return x + exchanged(x, 1)


def sum_rest(x):
    size = lax.axis_size(AXES)
    bit = 2
    while bit < size:
        sent = x.astype(BF16)
        x = sent.astype(F32) + exchanged(sent, bit)
        if 2 * bit < size:
            x = x + (exchanged(sent, 2 * bit) + exchanged(sent, 3 * bit))
        bit *= 4
    return x


def tap_halves(long_filter):
    if lax.axis_size("fsdp") == 2:
        return long_filter, lax.ppermute(long_filter, "fsdp", [(0, 1), (1, 0)])
    filters = lax.all_gather(long_filter, "fsdp", axis=1, tiled=True)
    return filters[:, : TAPS // 2], filters[:, TAPS // 2 :]


def body(q_in, k_in, v_in, grad_out, genome_ids, long_filter, short_filter):
    rows, channels = q_in.shape[1:]
    seq_count = lax.axis_size("fsdp")
    length = rows * lax.axis_size("ctx")
    halves = tap_halves(long_filter)
    groups = long_filter.shape[0]
    arrays = (genome_ids, short_filter, q_in, k_in, v_in, grad_out)
    conv_late, dzr_early, sent_near, sent_far = half_part(True, *arrays)
    near, far = swapped(sent_near, sent_far, "ctx")
    sent_near, sent_far, genome_ids = lax.optimization_barrier((sent_near, sent_far, genome_ids))
    conv_early, dzr_late, u_early, dz_late = half_part(False, genome_ids, *arrays[1:])
    scales = (
        1.0 / math.sqrt(seq_count * length * (channels // groups)),
        1.0 / math.sqrt(seq_count * length),
    )
    operands = (
        genome_ids, *halves, short_filter, near, far, q_in, k_in, v_in, grad_out,
        sent_near, sent_far, conv_late, dzr_early, conv_early, dzr_late, u_early, dz_late,
    )
    out_q, out_k, out_v, sums = mixer(operands, rows, channels, scales)
    power = lax.axis_size(AXES)
    if power & (power - 1):
        sums = lax.psum(sums, AXES)
    else:
        sums = sum_rest(sum_pair(sums))
    grad_short = sums[: 3 * SHORT].reshape(3, SHORT, channels)
    grad_long = sums[24:].reshape(8, channels // LANES, LANES).transpose(1, 0, 2)
    grad_long = grad_long.reshape(groups, TAPS)
    own = TAPS // seq_count
    grad_long = lax.dynamic_slice_in_dim(grad_long, lax.axis_index("fsdp") * own, own, 1)
    return out_q, out_k, out_v, grad_long, grad_short


def solution(mesh):
    return jax.shard_map(
        body,
        mesh=mesh,
        in_specs=(
            P("fsdp", "ctx", "tp"),
            P("fsdp", "ctx", "tp"),
            P("fsdp", "ctx", "tp"),
            P("fsdp", "ctx", "tp"),
            P("fsdp", "ctx"),
            P("tp", "fsdp"),
            P(None, None, "tp"),
        ),
        out_specs=(
            P("fsdp", "ctx", "tp"),
            P("fsdp", "ctx", "tp"),
            P("fsdp", "ctx", "tp"),
            P("tp", "fsdp"),
            P(None, None, "tp"),
        ),
        check_vma=False,
    )
```

```python
import functools
import math

import jax
import jax.numpy as jnp
from jax import lax
from jax.experimental import pallas as pl
from jax.experimental.pallas import tpu as pltpu
from jax.sharding import PartitionSpec as P

TAPS = 128
SHORT = 7
LANES = 128
GROUP = 16
EDGE = 8
VMEM_LIMIT = 65528 << 10
HEAD_ROWS = LANES + 32
F32 = jnp.float32
BF16 = jnp.bfloat16
NT = (((1,), (1,)), ((), ()))
NN = (((1,), (0,)), ((), ()))
VMEM = pl.BlockSpec(memory_space=pltpu.VMEM)
HBM = pl.BlockSpec(memory_space=pltpu.HBM)


def swapped(near, far, axis):
    size = lax.axis_size(axis)
    near_route = [(i, i ^ 1) for i in range(size) if i ^ 1 < size]
    far_route = [(i + 1, i) for i in range(1, size - 1, 2)]
    far_route = far_route + [(i, j) for j, i in far_route]
    return lax.ppermute(near, axis, near_route), lax.ppermute(far, axis, far_route)


def dot(a, b, dims):
    return lax.dot_general(a, b, dims, preferred_element_type=F32)


def lanes_of(i):
    return pl.ds(pl.multiple_of(i * LANES, LANES), LANES)


def spread(line):
    return jnp.broadcast_to(line, (TAPS, TAPS)).T


def copy_all(pairs, sems, i, wait=False):
    for n, (source, target) in enumerate(pairs):
        copy = pltpu.make_async_copy(source, target, sems.at[i, n])
        if wait:
            copy.wait()
        else:
            copy.start()


def half_kernel(
    rows,
    edge,
    ids_hbm,
    w_hbm,
    q_hbm,
    k_hbm,
    v_hbm,
    g_hbm,
    conv_hbm,
    dzr_hbm,
    one_hbm,
    two_hbm,
    ids_ref,
    ids_scalar,
    w_ref,
    bq,
    bk,
    bv,
    bg,
    conv_ref,
    dzr_ref,
    one_ref,
    two_ref,
    idc,
    mj,
    xq,
    xk,
    xv,
    uf,
    dzf,
    small_sems,
    in_sems,
    out_sems,
    packet_sems,
    border_sems,
):
    count = q_hbm.shape[2] // LANES
    odd = lax.rem(lax.axis_index("ctx"), 2)
    kv_low, q_low = (TAPS, 0) if edge else (0, TAPS)
    lead = 16

    def small():
        return ((ids_hbm, ids_ref), (ids_hbm, ids_scalar), (w_hbm, w_ref))

    def rows_from(low, before):
        start = low - before if low else 0
        return pl.ds(start, rows - start if low else TAPS + lead)

    def inputs(half):
        lane = pl.ds(pl.multiple_of(2 * LANES * half, 2 * LANES), 2 * LANES)
        spans = (
            (q_hbm, bq, rows_from(q_low, lead)),
            (k_hbm, bk, rows_from(kv_low, lead)),
            (v_hbm, bv, rows_from(kv_low, lead)),
            (g_hbm, bg, rows_from(q_low, 0)),
        )
        return [(a.at[0, span, lane], b.at[span, lane]) for a, b, span in spans]

    def borders():
        first, last = pl.ds(0, 16), pl.ds(rows - 16, 16)
        spans = ((k_hbm, bk, first), (v_hbm, bv, first), (q_hbm, bq, last))
        return [(a.at[0, span], b.at[span]) for a, b, span in spans]

    def outputs(half):
        span = pl.ds(2 * half, 2)
        pairs = [(conv_ref, conv_hbm), (dzr_ref, dzr_hbm)]
        return [(a.at[span], b.at[span]) for a, b in pairs]

    def packets(half):
        span = pl.ds(2 * half, 2)
        one, two = one_ref.at[span], two_ref.at[span]
        near, far = one_hbm.at[span], two_hbm.at[span]
        return ((one, near), (two, far)), ((two, near), (one, far))

    def send_packets(i):
        if not edge:
            copy_all(packets(i)[0], packet_sems, i)
            return

        @pl.when(odd == 0)
        def even_packets():
            copy_all(packets(i)[0], packet_sems, i)

        @pl.when(odd == 1)
        def odd_packets():
            copy_all(packets(i)[1], packet_sems, i)

    copy_all(small(), small_sems, 0)

    def fetch(i, carry):
        copy_all(inputs(i), in_sems, i)
        return carry

    lax.fori_loop(0, count // 2, fetch, 0)
    if edge:
        copy_all(borders(), border_sems, 0)
    copy_all(small(), small_sems, 0, wait=True)
    ids = (ids_ref[...] + 1).astype(F32)
    idc[0:EDGE] = jnp.zeros((EDGE, LANES), F32)
    for b in range(2):
        idc[EDGE + TAPS * b : EDGE + TAPS * (b + 1)] = spread(ids[:, TAPS * b : TAPS * (b + 1)])
    for x in (xq, xk, xv):
        x[:, 0:lead] = jnp.zeros((2, lead, LANES), F32)

    def masks(i, carry):
        base = pl.multiple_of(16 * i, 16)
        here = idc[pl.ds(base + EDGE, 16), :]
        for j in range(1, SHORT):
            mj[j - 1, pl.ds(base, 16), :] = (here == idc[pl.ds(base + EDGE - j, 16), :]).astype(F32)
        return carry

    lax.fori_loop(0, rows // 16, masks, 0)
    pad = jnp.zeros((EDGE - 2, LANES), F32)
    id_rows = [ids[:, TAPS * b : TAPS * (b + 1)] for b in range(2)]
    id_tile = jnp.concatenate(id_rows + [pad], axis=0)
    id_late = jnp.concatenate([pad] + id_rows, axis=0)
    sub = lax.broadcasted_iota(jnp.int32, (EDGE, LANES), 0)
    part = 32

    def pair(a, b):
        return jnp.concatenate([a, b], axis=0).astype(BF16)

    def filtered(x, h, taps, low, at, size, masked=True):
        total = taps[0] * x[h, pl.ds(at + lead, size), :]
        for j in range(1, SHORT):
            piece = x[h, pl.ds(at + lead - j, size), :]
            if masked:
                piece = mj[j - 1, pl.ds(at + low, size), :] * piece
            total += taps[j] * piece
        return total

    def two_blocks(half, carry):
        pair_of = [2 * half, 2 * half + 1]
        copy_all(inputs(half), in_sems, half, wait=True)
        for h, i in enumerate(pair_of):
            lane = lanes_of(i)
            for x, source, low in ((xq, bq, q_low), (xk, bk, kv_low), (xv, bv, kv_low)):
                if low:
                    x[h, 0:lead] = source[low - lead : low, lane].astype(F32)
                size = TAPS if low else TAPS + lead
                x[h, lead : lead + size] = source[low : low + size, lane].astype(F32)

        def taps_of(n, i):
            return [w_ref[n, j : j + 1, lanes_of(i)] for j in range(SHORT)]

        def convolve_part(at, masked):
            for h, i in enumerate(pair_of):
                key = filtered(xk, h, taps_of(1, i), kv_low, at, part, masked)
                value = filtered(xv, h, taps_of(2, i), kv_low, at, part, masked)
                query = filtered(xq, h, taps_of(0, i), q_low, at, part, masked)
                conv_ref[i, 0, pl.ds(at, part), :] = key
                conv_ref[i, 1, pl.ds(at, part), :] = value
                uf[h, pl.ds(at, part), :] = key * value
                dz = bg[pl.ds(at + q_low, part), lanes_of(i)].astype(F32) * query
                dzf[h, pl.ds(at, part), :] = dz
                dzr_ref[i, pl.ds(at, part), :] = dz.astype(BF16)

        def one_genome(low, at):
            start = jnp.maximum(low + at - (SHORT - 1), 0)
            return ids_scalar[0, start] == ids_scalar[0, low + at + part - 1]

        def convolve(n, inner):
            at = pl.multiple_of(part * n, part)
            plain = jnp.logical_and(one_genome(kv_low, at), one_genome(q_low, at))

            @pl.when(plain)
            def without_masks():
                convolve_part(at, False)

            @pl.when(jnp.logical_not(plain))
            def with_masks():
                convolve_part(at, True)

            return inner

        lax.fori_loop(0, TAPS // part, convolve, 0)
        for h, i in enumerate(pair_of):
            one_ref[i, 0:LANES, :] = uf[h].T.astype(BF16)
            two_ref[i, 0:LANES, :] = dzf[h].T.astype(BF16)
            if edge:
                lane = lanes_of(i)
                beyond = bg[TAPS : TAPS + 16, lane].astype(F32)[:EDGE]
                beyond = beyond * filtered(xq, h, taps_of(0, i), q_low, TAPS, EDGE)
                last = slice(lead + TAPS - EDGE, lead + TAPS)
                q_last = bq[rows - 16 : rows, lane].astype(F32)[EDGE:]
                k_first = bk[0:16, lane].astype(F32)[:EDGE]
                v_first = bv[0:16, lane].astype(F32)[:EDGE]
                g_first = bg[0:16, lane].astype(F32)[:EDGE]
                q_first = xq[h, lead : lead + EDGE, :]
                one_ref[i, LANES : LANES + 16, :] = pair(xk[h, last, :], xv[h, last, :])
                one_ref[i, LANES + 16 : LANES + 32, :] = pair(q_last, id_tile)
                late = sub >= EDGE - 2
                q_first = jnp.where(late, id_late, q_first)
                g_first = jnp.where(late, pltpu.roll(beyond, 6, 0), g_first)
                k_first = jnp.where(late, pltpu.roll(beyond, 4, 0), k_first)
                v_first = jnp.where(late, pltpu.roll(beyond, 2, 0), v_first)
                two_ref[i, LANES : LANES + 16, :] = pair(q_first, g_first)
                two_ref[i, LANES + 16 : LANES + 32, :] = pair(k_first, v_first)
        send_packets(half)
        copy_all(outputs(half), out_sems, half)
        return carry

    if edge:
        copy_all(borders(), border_sems, 0, wait=True)
    lax.fori_loop(0, count // 2, two_blocks, 0)

    def drain(i, carry):
        copy_all(packets(i)[0], packet_sems, i, wait=True)
        copy_all(outputs(i), out_sems, i, wait=True)
        return carry

    lax.fori_loop(0, count // 2, drain, 0)


def half_part(edge, ids, short_filter, q_in, k_in, v_in, grad_out):
    rows, channels = q_in.shape[1:]
    count = channels // LANES
    vm = lambda *shape: pltpu.VMEM(shape, F32)
    vb = lambda *shape: pltpu.VMEM(shape, BF16)
    packet = (count, HEAD_ROWS if edge else LANES, LANES)
    results = (
        ((count, 2, TAPS, LANES), F32),
        ((count, TAPS, LANES), BF16),
        (packet, BF16),
        (packet, BF16),
    )
    return pl.pallas_call(
        functools.partial(half_kernel, rows, edge),
        in_specs=[HBM] * 6,
        out_specs=[HBM] * 4,
        out_shape=[jax.ShapeDtypeStruct(*r) for r in results],
        scratch_shapes=[
            pltpu.VMEM(ids.shape, jnp.int32),
            pltpu.SMEM(ids.shape, jnp.int32),
            vm(*short_filter.shape),
            *[vb(rows, channels)] * 4,
            *[pltpu.VMEM(*r) for r in results],
            vm(rows + EDGE, LANES),
            vm(SHORT - 1, rows, LANES),
            *[vm(2, TAPS + 32, LANES)] * 3,
            vm(2, TAPS, LANES),
            vm(2, TAPS, LANES),
            pltpu.SemaphoreType.DMA((1, 3)),
            pltpu.SemaphoreType.DMA((count // 2, 4)),
            pltpu.SemaphoreType.DMA((count // 2, 2)),
            pltpu.SemaphoreType.DMA((count // 2, 2)),
            pltpu.SemaphoreType.DMA((1, 3)),
        ],
        compiler_params=pltpu.CompilerParams(vmem_limit_bytes=VMEM_LIMIT),
        cost_estimate=pl.CostEstimate(
            flops=8_000_000_000, bytes_accessed=16_000_000, transcendentals=0
        ),
        name="edge_half" if edge else "other_half",
    )(ids, short_filter, q_in, k_in, v_in, grad_out)


def mixer_kernel(
    rows,
    long_scale,
    short_scale,
    ids_hbm,
    one_half_hbm,
    other_half_hbm,
    w_hbm,
    near_hbm,
    far_hbm,
    q_hbm,
    k_hbm,
    v_hbm,
    g_hbm,
    sent_near_hbm,
    sent_far_hbm,
    conv_late_hbm,
    dzr_early_hbm,
    conv_early_hbm,
    dzr_late_hbm,
    u_early_hbm,
    dz_late_hbm,
    oq_hbm,
    ok_hbm,
    ov_hbm,
    part_hbm,
    ids_ref,
    one_half,
    other_half,
    w_ref,
    prev_ref,
    next_ref,
    bq,
    bk,
    bv,
    bg,
    tail_ref,
    head_ref,
    conv_late,
    dzr_early,
    conv_early,
    dzr_late,
    u_early,
    dz_late,
    oq_ref,
    ok_ref,
    ov_ref,
    part_ref,
    tiles,
    idr,
    idc,
    mj,
    ml,
    mn,
    mp,
    flip,
    edges,
    ut,
    utr,
    dzt,
    dzr,
    zt,
    dut,
    dq,
    dk,
    dv,
    gl,
    fixes,
    bands,
    others,
    tops,
    products,
    small_sems,
    halo_sems,
    in_sems,
    out_sems,
):
    blocks = rows // TAPS
    frame = rows
    count = q_hbm.shape[2] // LANES
    per = LANES // GROUP
    odd = lax.rem(lax.axis_index("ctx"), 2)

    def small():
        return (
            (ids_hbm, ids_ref),
            (one_half_hbm, one_half),
            (other_half_hbm, other_half),
            (w_hbm, w_ref),
        )

    waves = ((0, 1), (1, 2), (3, count - 3))

    def halos(wave):
        span = pl.ds(*waves[wave])
        far, near = far_hbm.at[span], near_hbm.at[span]
        prev, succ = prev_ref.at[span], next_ref.at[span]
        sent_far, sent_near = sent_far_hbm.at[span], sent_near_hbm.at[span]
        tail, head = tail_ref.at[span], head_ref.at[span]
        return (
            ((far, prev), (near, succ), (sent_near, tail), (sent_far, head)),
            ((near, prev), (far, succ), (sent_far, tail), (sent_near, head)),
        )

    def inputs(wave):
        start, size = waves[wave]
        span = pl.ds(start, size)
        lane = pl.ds(start * LANES, size * LANES)
        pairs = ((q_hbm, bq), (k_hbm, bk), (v_hbm, bv), (g_hbm, bg))
        pairs = [(a.at[0, :, lane], b.at[:, lane]) for a, b in pairs]
        more = (
            (conv_late_hbm, conv_late),
            (dzr_early_hbm, dzr_early),
            (conv_early_hbm, conv_early),
            (dzr_late_hbm, dzr_late),
            (u_early_hbm, u_early),
            (dz_late_hbm, dz_late),
        )
        return [(a.at[span], b.at[span]) for a, b in more] + pairs

    def outputs(i):
        lane = lanes_of(i)
        pairs = ((oq_ref, oq_hbm), (ok_ref, ok_hbm), (ov_ref, ov_hbm))
        return [(a.at[:, lane], b.at[0, :, lane]) for a, b in pairs]

    def start_wave(wave):
        @pl.when(odd == 0)
        def even_halos():
            copy_all(halos(wave)[0], halo_sems, wave)

        @pl.when(odd == 1)
        def odd_halos():
            copy_all(halos(wave)[1], halo_sems, wave)

        copy_all(inputs(wave), in_sems, wave)

    def arrive_halos(wave):
        copy_all(halos(wave)[0], halo_sems, wave, wait=True)

    def arrive(wave):
        copy_all(inputs(wave), in_sems, wave, wait=True)

    copy_all(small(), small_sems, 0)
    start_wave(0)
    copy_all(small(), small_sems, 0, wait=True)
    arrive_halos(0)
    start_wave(1)

    row = lax.broadcasted_iota(jnp.int32, (TAPS, TAPS), 0)
    col = lax.broadcasted_iota(jnp.int32, (TAPS, TAPS), 1)
    own_ids = (ids_ref[...] + 1).astype(F32)
    prev_ids = prev_ref[0, LANES + 16 : LANES + 32, :].astype(F32)
    next_ids = next_ref[0, LANES : LANES + 16, :].astype(F32)
    for b in range(blocks):
        idr[b : b + 1, :] = prev_ids[EDGE + b : EDGE + b + 1]
        idr[blocks + b : blocks + b + 1, :] = own_ids[:, TAPS * b : TAPS * (b + 1)]
        idr[2 * blocks + b : 2 * blocks + b + 1, :] = next_ids[EDGE - blocks + b : EDGE - blocks + b + 1]
    for b in range(3 * blocks):
        idc[TAPS * b : TAPS * (b + 1), :] = spread(idr[b : b + 1, :])

    def short_masks(i, carry):
        base = pl.multiple_of(frame + EDGE * i, EDGE)
        here = idc[pl.ds(base, EDGE), :]
        for j in range(1, SHORT):
            mj[j - 1, pl.ds(base, EDGE), :] = (here == idc[pl.ds(base - j, EDGE), :]).astype(F32)
        return carry

    lax.fori_loop(0, (rows + 2 * EDGE) // EDGE, short_masks, 0)

    def same(t_block, s_block, length):
        start = frame + TAPS * t_block
        line = idr[blocks + s_block : blocks + s_block + 1, :]
        return (idc[start : start + length, :] == line).astype(F32)

    lower = (row >= col).astype(F32)
    upper = 1.0 - lower
    flip[...] = (row + col == TAPS - 1).astype(BF16)
    for b in range(blocks):
        ml[b] = (same(b, b, TAPS) * lower).astype(BF16)
    for b in range(blocks + 1):
        ml[blocks + b] = (same(b, b - 1, TAPS) * upper).astype(BF16)
    mn[0] = (same(blocks, blocks, 16) * lower[:16]).astype(BF16)
    mn[1] = (same(blocks, blocks, 16) * (row <= col).astype(F32)[:16]).astype(BF16)
    mn[2] = (same(blocks, blocks + 1, 16) * (row > col).astype(F32)[:16]).astype(BF16)
    for b in range(blocks):
        both = same(b, b, TAPS) * lower + same(b, b - 1, TAPS) * upper
        mp[b] = dot(both.astype(BF16), flip[...], NN)
    negated = jnp.logical_or(row + col == TAPS, row + col == 0).astype(BF16)
    first, second = one_half[...].astype(F32), other_half[...].astype(F32)
    if lax.axis_size("fsdp") == 2:
        mine = lax.axis_index("fsdp") == 0
        first, second = jnp.where(mine, first, second), jnp.where(mine, second, first)
    forward_taps = jnp.concatenate([first, second], axis=1)
    reversed_taps = dot(forward_taps.astype(BF16), negated, NN)
    for i in range(count * per):
        tiles[i, 0:1, :] = reversed_taps[i : i + 1]
        tiles[i, 1:2, :] = forward_taps[i : i + 1]

    lane_group = col // GROUP
    lower_flipped = row + col >= TAPS - 1
    first_lanes = col < EDGE
    next_lanes = col < SHORT - 1
    sub = lax.broadcasted_iota(jnp.int32, (EDGE, LANES), 0)
    blank = jnp.zeros((TAPS - EDGE, LANES), F32)

    def turned(x):
        return jnp.concatenate([x, blank], axis=0).T.astype(BF16)

    def filters_of(i):
        return [[w_ref[n, j : j + 1, lanes_of(i)] for j in range(SHORT)] for n in range(3)]

    def prepare(i):
        w = filters_of(i)
        prev_kv = prev_ref[i, LANES : LANES + 16, :].astype(F32)
        prev_q = prev_ref[i, LANES + 16 : LANES + 32, :].astype(F32)
        next_qg = next_ref[i, LANES : LANES + 16, :].astype(F32)
        next_kv = next_ref[i, LANES + 16 : LANES + 32, :].astype(F32)
        next_dz = jnp.where(
            sub < 2,
            pltpu.roll(next_qg[EDGE:], 2, 0),
            jnp.where(
                sub < 4,
                pltpu.roll(next_kv[:EDGE], 4, 0),
                jnp.where(sub < 5, pltpu.roll(next_kv[EDGE:], 6, 0), 0.0),
            ),
        )
        for n, (source, before, after) in enumerate(
            (
                (bq, prev_q[:EDGE], next_qg[:EDGE]),
                (bk, prev_kv[:EDGE], next_kv[:EDGE]),
                (bv, prev_kv[EDGE:], next_kv[EDGE:]),
            )
        ):
            edges[n, 0, 0:EDGE] = before
            edges[n, 0, EDGE : 2 * EDGE] = source[0:16, lanes_of(i)].astype(F32)[:EDGE]
            edges[n, 1, 0:EDGE] = source[rows - 16 : rows, lanes_of(i)].astype(F32)[EDGE:]
            edges[n, 1, EDGE : 2 * EDGE] = after

        def convolve(n, m):
            low = frame + rows * m
            total = w[n][0] * edges[n, m, EDGE : 2 * EDGE]
            for j in range(1, SHORT):
                mask = mj[j - 1, low : low + EDGE, :]
                total += w[n][j] * (mask * edges[n, m, EDGE - j : 2 * EDGE - j])
            return total

        upstream = (bg[0:16, lanes_of(i)].astype(F32)[:EDGE], next_qg[EDGE:])
        fixed = []
        for m in range(2):
            query, key, value = [convolve(n, m) for n in range(3)]
            fixed.append((key, value, key * value, upstream[m] * query))

        ut[:, 0:TAPS] = prev_ref[i, 0:LANES, :]
        ut[:, TAPS : 2 * TAPS] = jnp.where(first_lanes, turned(fixed[0][2]), u_early[i])
        ut[:, 2 * TAPS : 3 * TAPS] = tail_ref[i, 0:LANES, :]
        ut[:, 3 * TAPS :] = turned(fixed[1][2])
        dzt[:, 0:TAPS] = jnp.where(first_lanes, turned(fixed[0][3]), head_ref[i, 0:LANES, :])
        dzt[:, TAPS : 2 * TAPS] = dz_late[i]
        dzt[:, 2 * TAPS : 3 * TAPS] = jnp.where(
            next_lanes, turned(fixed[1][3]), next_ref[i, 0:LANES, :]
        )
        dzt[:, 3 * TAPS :] = turned(next_dz[:EDGE])
        dzr[0:TAPS] = dzr_early[i]
        dzr[TAPS:] = dzr_late[i]
        rest = dzr_early[i, 0:16, :].astype(F32)[EDGE:]
        dzr[0:16] = jnp.concatenate([fixed[0][3], rest], axis=0).astype(BF16)
        for b in range(blocks + 1):
            here = slice(TAPS * b, TAPS * (b + 1))
            utr[:, here] = dot(ut[:, here], flip[...], NN).astype(BF16)

        for m in range(2):
            for n in range(2):
                fixes[m, n] = fixed[m][n]

    def make_bands(i, m, slot):
        if True:
            g = per * i + m
            base = pltpu.roll(jnp.broadcast_to(tiles[g, 0:1, :], (16, TAPS)), 0, 1, stride=1, stride_axis=0)
            base = base.astype(BF16)
            bands[slot, 0:16] = base
            for r in range(16, TAPS, 16):
                bands[slot, r : r + 16] = pltpu.roll(base, r, 1)
            tops[16 * m : 16 * m + 16] = base
            line = jnp.broadcast_to(tiles[g, 1:2, :], (16, TAPS))
            line = pltpu.roll(line, 0, 1, stride=1, stride_axis=0).astype(BF16)
            others[16 * m : 16 * m + 16] = line

    def sum_taps(i, m):
        skewed = pltpu.roll(products[m], 1, 1, stride=1, stride_axis=0)
        gl[per * i + m] = jnp.sum(skewed.reshape(TAPS // 8, 8, TAPS), axis=0)

    def multiply_taps():
        for b in range(blocks):
            here = slice(TAPS * b, TAPS * (b + 1))
            mine = [jnp.where(lane_group == m, dzr[here, :], jnp.zeros((), BF16)) for m in range(per)]
            pairs = dot(jnp.concatenate(mine, axis=0), utr[:, TAPS * b : TAPS * (b + 2)], NN)
            for m in range(per):
                own = pairs[TAPS * m : TAPS * (m + 1)]
                term = jnp.where(lower_flipped, own[:, TAPS:], own[:, :TAPS]) * mp[b]
                products[m] = term if b == 0 else products[m] + term

    def multiply(m, slot):
        c = slice(GROUP * m, GROUP * (m + 1))
        band = bands[slot]
        near = [band * ml[b] for b in range(blocks)]
        far = [band * ml[blocks + b] for b in range(blocks + 1)]
        weights = jnp.concatenate(
            [jnp.concatenate([far[b], near[b]], axis=1) for b in range(blocks)], axis=0
        )
        both = jnp.concatenate([ut[c, TAPS * b : TAPS * (b + 2)] for b in range(blocks)], axis=0)
        result = dot(both, weights, NT)
        for b in range(blocks):
            here = slice(TAPS * b, TAPS * (b + 1))
            zt[c, here] = result[GROUP * b : GROUP * (b + 1), here]
        weights = jnp.concatenate(
            [jnp.concatenate([near[b], far[b + 1]], axis=0) for b in range(blocks)], axis=1
        )
        both = jnp.concatenate([dzt[c, TAPS * b : TAPS * (b + 2)] for b in range(blocks)], axis=0)
        result = dot(both, weights, NN)
        for b in range(blocks):
            here = slice(TAPS * b, TAPS * (b + 1))
            dut[c, here] = result[GROUP * b : GROUP * (b + 1), here]

    def edge_rows(rows_of, first, second, signal):
        left = [rows_of[16 * m : 16 * m + 16] * first for m in range(per)]
        right = [rows_of[16 * m : 16 * m + 16] * second for m in range(per)]
        left, right = jnp.concatenate(left, axis=0), jnp.concatenate(right, axis=0)
        result = dot(jnp.concatenate([left, right], axis=1), signal, NT)
        total = None
        for m in range(per):
            own = jnp.where(lane_group[:16] == m, result[16 * m : 16 * m + 16], 0.0)
            total = own if total is None else total + own
        return total

    def close(i):
        below = next_ref[i, LANES : LANES + 16, :].astype(F32)[EDGE:]
        window = slice(TAPS * blocks, TAPS * (blocks + 2))
        z2 = edge_rows(tops, ml[2 * blocks, 0:16], mn[0], ut[:, window])
        du2 = edge_rows(others, mn[1], mn[2], dzt[:, window])
        for b in range(blocks + 1):
            length = TAPS if b < blocks else EDGE
            here = slice(TAPS * b, TAPS * b + length)
            z = zt[:, here].T if b < blocks else z2[:EDGE]
            du = dut[:, here].T if b < blocks else du2[:EDGE]
            if b < blocks:
                dq[here, :] = bg[here, lanes_of(i)].astype(F32) * z
                conv = conv_late if b else conv_early
                dk[here, :] = du * conv[i, 1]
                dv[here, :] = du * conv[i, 0]
            else:
                dq[here, :] = below * z
            if b in (0, blocks):
                m = 0 if b == 0 else 1
                key, value = fixes[m, 0], fixes[m, 1]
                there = slice(TAPS * b, TAPS * b + EDGE)
                dk[there, :] = du[:EDGE] * value
                dv[there, :] = du[:EDGE] * key

    steps = per
    groups = count * per
    part = 32

    def finish_steps(i):
        arrays = ((dq, bq, oq_ref), (dk, bk, ok_ref), (dv, bv, ov_ref))
        lane = lanes_of(i)
        for n in range(3 * SHORT):
            tiles[groups + n] = jnp.zeros((8, LANES), F32)

        def one_part(m):
            for n, (grad, source, out) in enumerate(arrays):
                sums = [None] * SHORT
                for at in range(rows // steps // part):
                    low = rows // steps * m + part * at
                    x = source[pl.ds(low, part), lane].astype(F32)
                    total = None
                    for j in range(SHORT):
                        piece = grad[pl.ds(low + j, part), :]
                        if j:
                            piece = piece * mj[j - 1, pl.ds(low + frame + j, part), :]
                        scaled = w_ref[n, j : j + 1, lane] * piece
                        total = scaled if total is None else total + scaled
                        fresh = jnp.sum((x * piece).reshape(part // 8, 8, LANES), axis=0)
                        sums[j] = fresh if at == 0 else sums[j] + fresh
                    out[pl.ds(low, part), lane] = total.astype(BF16)
                for j in range(SHORT):
                    tiles[groups + SHORT * n + j] += sums[j]

        def close():
            for n in range(3 * SHORT):
                line = jnp.sum(tiles[groups + n], axis=0, keepdims=True) * short_scale
                part_ref[n : n + 1, lane] = line
            copy_all(outputs(i), out_sems, i)

        return one_part, close

    part_ref[3 * SHORT : 24, :] = jnp.zeros((24 - 3 * SHORT, part_ref.shape[1]), F32)

    def long_block(i, between):
        multiply_taps()
        for m in range(per):
            make_bands(i, m, m)
            multiply(m, m)
            sum_taps(i, m)
            between(m)

    arrive(0)
    start_wave(2)
    prepare(0)
    long_block(0, lambda m: None)
    close(0)
    arrive_halos(1)
    arrive(1)
    prepare(1)

    def both(i, carry):
        @pl.when(i == 2)
        def rest_arrives():
            arrive_halos(2)
            arrive(2)

        one_part, close_finish = finish_steps(i - 1)
        long_block(i, one_part)
        close_finish()
        close(i)
        prepare(jnp.minimum(i + 1, count - 1))
        return carry

    lax.fori_loop(1, count, both, 0)
    one_part, close_finish = finish_steps(count - 1)
    for m in range(per):
        one_part(m)
    close_finish()
    for i in range(count):
        lines = [jnp.sum(gl[per * i + n], axis=0, keepdims=True) for n in range(per)]
        here = slice(LANES * i, LANES * (i + 1))
        part_ref[24:32, here] = jnp.concatenate(lines, axis=0) * long_scale

    copy_all([(part_ref, part_hbm)], small_sems, 0)

    def drain(i, carry):
        copy_all(outputs(i), out_sems, i, wait=True)
        return carry

    lax.fori_loop(0, count, drain, 0)
    copy_all([(part_ref, part_hbm)], small_sems, 0, wait=True)


def mixer(operands, rows, channels, scales):
    blocks = rows // TAPS
    count = channels // LANES
    ids, short_filter = operands[0], operands[3]
    vm = lambda *shape: pltpu.VMEM(shape, F32)
    vb = lambda *shape: pltpu.VMEM(shape, BF16)
    out = jax.ShapeDtypeStruct((1, rows, channels), BF16)
    buffered = [vb(rows, channels)] * 4
    return pl.pallas_call(
        functools.partial(mixer_kernel, rows, *scales),
        in_specs=[HBM] * len(operands),
        out_specs=[HBM] * 4,
        out_shape=[out, out, out, jax.ShapeDtypeStruct((32, channels), F32)],
        scratch_shapes=[
            pltpu.VMEM(ids.shape, jnp.int32),
            vb(*operands[1].shape),
            vb(*operands[2].shape),
            vm(*short_filter.shape),
            vb(count, HEAD_ROWS, LANES),
            vb(count, HEAD_ROWS, LANES),
            *buffered,
            vb(count, HEAD_ROWS, LANES),
            vb(count, HEAD_ROWS, LANES),
            vm(count, 2, TAPS, LANES),
            vb(count, TAPS, LANES),
            vm(count, 2, TAPS, LANES),
            vb(count, TAPS, LANES),
            vb(count, LANES, TAPS),
            vb(count, LANES, TAPS),
            *buffered[:3],
            vm(32, channels),
            vm(channels // GROUP + 3 * SHORT, 8, TAPS),
            vm(8, LANES),
            vm(3 * rows, LANES),
            vm(SHORT - 1, 3 * rows, LANES),
            vb(2 * blocks + 1, TAPS, TAPS),
            vb(3, 16, TAPS),
            vm(blocks, TAPS, TAPS),
            vb(TAPS, TAPS),
            vm(3, 2, 2 * EDGE, LANES),
            vb(LANES, rows + 2 * TAPS),
            vb(LANES, rows + TAPS),
            vb(LANES, rows + 2 * TAPS),
            vb(rows, LANES),
            vm(LANES, rows + TAPS),
            vm(LANES, rows + TAPS),
            vm(rows + 16, LANES),
            vm(rows + 16, LANES),
            vm(rows + 16, LANES),
            vm(channels // GROUP, 8, TAPS),
            vm(2, 2, EDGE, LANES),
            vb(LANES // GROUP, TAPS, TAPS),
            vb(LANES, TAPS),
            vb(LANES, TAPS),
            vm(LANES // GROUP, TAPS, TAPS),
            pltpu.SemaphoreType.DMA((1, 4)),
            pltpu.SemaphoreType.DMA((3, 4)),
            pltpu.SemaphoreType.DMA((3, 10)),
            pltpu.SemaphoreType.DMA((count, 3)),
        ],
        compiler_params=pltpu.CompilerParams(vmem_limit_bytes=63 << 20),
        name="mixer",
    )(*operands)


AXES = ("fsdp", "ctx")


def exchanged(x, bits):
    size = lax.axis_size(AXES)
    return lax.ppermute(x, AXES, [(i, i ^ bits) for i in range(size)]).astype(F32)


def sum_pair(x):
    return x + exchanged(x, 1)


def sum_rest(x):
    size = lax.axis_size(AXES)
    bit = 2
    while bit < size:
        sent = x.astype(BF16)
        x = sent.astype(F32) + exchanged(sent, bit)
        if 2 * bit < size:
            x = x + (exchanged(sent, 2 * bit) + exchanged(sent, 3 * bit))
        bit *= 4
    return x


def tap_halves(long_filter):
    if lax.axis_size("fsdp") == 2:
        return long_filter, lax.ppermute(long_filter, "fsdp", [(0, 1), (1, 0)])
    filters = lax.all_gather(long_filter, "fsdp", axis=1, tiled=True)
    return filters[:, : TAPS // 2], filters[:, TAPS // 2 :]


def body(q_in, k_in, v_in, grad_out, genome_ids, long_filter, short_filter):
    rows, channels = q_in.shape[1:]
    seq_count = lax.axis_size("fsdp")
    length = rows * lax.axis_size("ctx")
    halves = tap_halves(long_filter)
    groups = long_filter.shape[0]
    arrays = (genome_ids, short_filter, q_in, k_in, v_in, grad_out)
    conv_late, dzr_early, sent_near, sent_far = half_part(True, *arrays)
    near, far = swapped(sent_near, sent_far, "ctx")
    sent_near, sent_far, genome_ids = lax.optimization_barrier((sent_near, sent_far, genome_ids))
    conv_early, dzr_late, u_early, dz_late = half_part(False, genome_ids, *arrays[1:])
    scales = (
        1.0 / math.sqrt(seq_count * length * (channels // groups)),
        1.0 / math.sqrt(seq_count * length),
    )
    operands = (
        genome_ids, *halves, short_filter, near, far, q_in, k_in, v_in, grad_out,
        sent_near, sent_far, conv_late, dzr_early, conv_early, dzr_late, u_early, dz_late,
    )
    out_q, out_k, out_v, sums = mixer(operands, rows, channels, scales)
    power = lax.axis_size(AXES)
    if power & (power - 1):
        sums = lax.psum(sums, AXES)
    else:
        sums = sum_rest(sum_pair(sums))
    grad_short = sums[: 3 * SHORT].reshape(3, SHORT, channels)
    grad_long = sums[24:].reshape(8, channels // LANES, LANES).transpose(1, 0, 2)
    grad_long = grad_long.reshape(groups, TAPS)
    own = TAPS // seq_count
    grad_long = lax.dynamic_slice_in_dim(grad_long, lax.axis_index("fsdp") * own, own, 1)
    return out_q, out_k, out_v, grad_long, grad_short


def solution(mesh):
    return jax.shard_map(
        body,
        mesh=mesh,
        in_specs=(
            P("fsdp", "ctx", "tp"),
            P("fsdp", "ctx", "tp"),
            P("fsdp", "ctx", "tp"),
            P("fsdp", "ctx", "tp"),
            P("fsdp", "ctx"),
            P("tp", "fsdp"),
            P(None, None, "tp"),
        ),
        out_specs=(
            P("fsdp", "ctx", "tp"),
            P("fsdp", "ctx", "tp"),
            P("fsdp", "ctx", "tp"),
            P("tp", "fsdp"),
            P(None, None, "tp"),
        ),
        check_vma=False,
    )
```
